32 devices in a mesh: rows: 16 (over z, y, core), ang: 2 (over x).
Axes of the slice: x: 2, y: 2, z: 4, core: 2. Of those that a mesh axis runs over, the one named last changes fastest.
Arguments:
- measured: bfloat16 [2, 2048, 2, 2048], P('ang', 'rows'), may hold values from -6 to 6
- slices: bfloat16 [2, 2048, 2, 2048], P(None, 'rows', None, 'ang'), may hold values from -5 to 5
- kernel_taps: bfloat16 [2, 65], replicated, may hold values from -1.25 to 1.25
- angle_freq: float32 [128, 2], replicated, may hold values from -40 to 40
- chosen: int32 [2], P('ang'), may hold values from 0 to 127
Outputs:
- grad_near: float32 [2048, 2, 2048], P('rows', None, 'ang')
- grad_far: float32 [2048, 2, 2048], P('rows', None, 'ang')
The draws below stay inside these ranges and needn't reach their ends.
Inputs may be any that keep to these rules, and one draw needn't show every extreme that they name: `chosen`: indices into the angle table; an index may repeat.
All inputs are finite; a program needn't handle non-finite values.
Results may differ from the reference program's by a relative error of at most 0.014.
Values may be sent and summed in bfloat16 or wider, within the bound.
No kernel may reach another device: no remote copies, remote signals or barrier semaphores. Data moves between devices by JAX's collectives and lax.ppermute only.
A program may use at most 64 MiB of HBM per device.

```python
import math
import jax
import jax.numpy as jnp

N = 2048
TAPS = 65
ANGLES_ALL = 128
ANGLES = 2


def levels(key, shape, split, least, top_value):
    def one(axis_at, blocks):
        draws = jax.random.uniform(jax.random.fold_in(jax.random.fold_in(key, 6), axis_at), (blocks,), jnp.float32, least / len(split), top_value / len(split))
        return jnp.repeat(jnp.exp(draws), shape[axis_at] // blocks).reshape((-1,) + (1,) * (len(shape) - axis_at - 1))

    gain = one(*split[0])
    for cut in split[1:]:
        gain = gain * one(*cut)
    return gain


def centred(own_key, shape, spread, bound, shards=(), kind=jnp.bfloat16):
    level = levels(own_key, shape, shards, -0.22, 0.18) if shards else 1.0
    drawn = jax.random.normal(own_key, shape, jnp.float32) * spread * level
    return jnp.minimum(jnp.maximum(drawn, -bound), bound).astype(kind)


def setup_inputs(seed: int = 0) -> dict:
    key_of = jax.random.split(jax.random.key(seed), 6)
    return {
        "measured": centred(key_of[0], (ANGLES, N, 2, N), 1.0, 6.0, ((0, 2), (1, 16))),
        "slices": centred(key_of[1], (2, N, 2, N), 0.7, 5.0, ((1, 16), (3, 2))),
        "kernel_taps": centred(key_of[2], (2, TAPS), ((2.0 * TAPS) ** -0.5), 1.25),
        "angle_freq": jnp.clip(jax.random.uniform(key_of[3], (ANGLES_ALL, 2), jnp.float32, -40.0, 40.0), -40.0, 40.0),
        "chosen": jax.random.randint(key_of[4], (ANGLES,), 0, ANGLES_ALL).astype(jnp.int32),
    }


def toeplitz(row_taps, out_width):
    tap_count = row_taps.shape[0]
    window = out_width + tap_count - 1
    padded = jnp.concatenate([row_taps, jnp.zeros((out_width,), row_taps.dtype)])
    tiled = jnp.tile(padded, out_width)[: out_width * window]
    return tiled.reshape(out_width, window).T


def kernel_pair(kernel_taps, out_width):
    return jnp.concatenate([toeplitz(kernel_taps[0], out_width), toeplitz(kernel_taps[1], out_width)], axis=1)


def adjoint_taps(kernel_taps):
    return jnp.stack([kernel_taps[0][::-1], -kernel_taps[1][::-1]])


def correlate_columns(field, kernel):
    window, doubled = kernel.shape
    tile_len = doubled // 2
    half_taps = (window - tile_len) // 2
    leading, comps, length = field.shape
    blocks = length // tile_len
    padded = jnp.pad(field, ((0, 0), (0, 0), (half_taps, tile_len - half_taps)))
    main_part = padded[:, :, :length].reshape(leading, comps, blocks, tile_len)
    tail_part = padded[:, :, tile_len:tile_len + length].reshape(leading, comps, blocks, tile_len)[..., : 2 * half_taps]
    windows = jnp.concatenate([main_part, tail_part], axis=3)
    product = jnp.einsum("rpnw,wk->rpnk", windows.astype(jnp.float32), kernel.astype(jnp.float32))
    real_part = product[:, 0, :, :tile_len] - product[:, 1, :, tile_len:]
    imag_part = product[:, 0, :, tile_len:] + product[:, 1, :, :tile_len]
    return jnp.stack([real_part, imag_part], axis=1).reshape(leading, comps, length).astype(jnp.bfloat16)


def correlate_rows(field, kernel):
    window, doubled = kernel.shape
    tile_len = doubled // 2
    half_taps = (window - tile_len) // 2
    leading, comps, length = field.shape
    blocks = leading // tile_len
    padded = jnp.pad(field, ((half_taps, tile_len - half_taps), (0, 0), (0, 0)))
    main_part = padded[:leading].reshape(blocks, tile_len, comps, length)
    tail_part = padded[tile_len:tile_len + leading].reshape(blocks, tile_len, comps, length)[:, : 2 * half_taps]
    windows = jnp.concatenate([main_part, tail_part], axis=1)
    product = jnp.einsum("nwpc,wk->nkpc", windows.astype(jnp.float32), kernel.astype(jnp.float32))
    real_part = product[:, :tile_len, 0] - product[:, tile_len:, 1]
    imag_part = product[:, tile_len:, 0] + product[:, :tile_len, 1]
    return jnp.stack([real_part, imag_part], axis=2).reshape(leading, comps, length).astype(jnp.bfloat16)


def complex_times(left, right):
    left = left.astype(jnp.float32)
    right = right.astype(jnp.float32)
    real_part = left[:, 0] * right[:, 0] - left[:, 1] * right[:, 1]
    imag_part = left[:, 0] * right[:, 1] + left[:, 1] * right[:, 0]
    return jnp.stack([real_part, imag_part], axis=1)


def conjugate_times(left, right):
    left = left.astype(jnp.float32)
    right = right.astype(jnp.float32)
    real_part = left[:, 0] * right[:, 0] + left[:, 1] * right[:, 1]
    imag_part = left[:, 0] * right[:, 1] - left[:, 1] * right[:, 0]
    return jnp.stack([real_part, imag_part], axis=1)


def incident(freq, row_pos, col_pos, length):
    scale = 2.0 * math.pi / length
    phase = scale * (freq[0] * row_pos[:, None] + freq[1] * col_pos[None, :])
    return jnp.stack([jnp.cos(phase), jnp.sin(phase)], axis=1)


def reference(measured, slices, kernel_taps, angle_freq, chosen):
    forward_kernel = kernel_pair(kernel_taps, 128)
    adjoint_kernel = kernel_pair(adjoint_taps(kernel_taps), 128)
    positions = jnp.arange(N).astype(jnp.float32)
    grad_near = jnp.zeros((N, 2, N), jnp.float32)
    grad_far = jnp.zeros((N, 2, N), jnp.float32)
    for member in range(ANGLES):
        freq = angle_freq[chosen[member]]
        entering = incident(freq, positions, positions, N)
        entry0 = complex_times(slices[0], entering).astype(jnp.bfloat16)
        inner = correlate_rows(correlate_columns(entry0, forward_kernel), forward_kernel)
        entry1 = complex_times(slices[1], inner).astype(jnp.bfloat16)
        exit_field = correlate_rows(correlate_columns(entry1, forward_kernel), forward_kernel)
        residue = (exit_field.astype(jnp.float32) - measured[member].astype(jnp.float32)).astype(jnp.bfloat16)
        back_far = correlate_columns(correlate_rows(residue, adjoint_kernel), adjoint_kernel)
        grad_far = grad_far + conjugate_times(inner, back_far)
        carried = conjugate_times(slices[1], back_far).astype(jnp.bfloat16)
        back_near = correlate_columns(correlate_rows(carried, adjoint_kernel), adjoint_kernel)
        grad_near = grad_near + conjugate_times(entering, back_near)
    return grad_near, grad_far
```

```python
import functools
import math

import jax
import jax.numpy as jnp
from jax import lax
from jax.experimental import pallas as pl
from jax.experimental.pallas import tpu as pltpu
from jax.sharding import PartitionSpec as P

LANES = 128
BF16 = jnp.bfloat16
F32 = jnp.float32


def dot(left, right):
    return jnp.dot(left, right, preferred_element_type=F32)


def iota(shape, dim):
    return lax.broadcasted_iota(jnp.int32, shape, dim)


def lane_chunks(width, step=2 * LANES):
    return [(at, min(step, width - at)) for at in range(0, width, step)]


def edges_kernel(half, slices, angle_freq, chosen, outer, inner, across, corner):
    rows, cols = slices.shape[1], slices.shape[3]
    parity = lax.axis_index("rows") % 2
    side = lax.axis_index("ang")
    near_rows, far_rows = 2 * half, half
    for out, late in ((outer, parity), (inner, 1 - parity)):
        near = slices[0, pl.ds(late * (rows - near_rows), near_rows)]
        far = slices[1, pl.ds(late * (rows - far_rows), far_rows)]
        out[: 2 * near_rows] = near.reshape(2 * near_rows, cols)
        out[2 * near_rows :] = far.reshape(2 * far_rows, cols)
    corner[...] = jnp.where(side == 0, outer[:, cols - LANES :], outer[:, :LANES])
    for slab in range(2):
        left = slices[slab, :, :, :LANES].reshape(2 * rows, LANES)
        right = slices[slab, :, :, cols - LANES :].reshape(2 * rows, LANES)
        across[slab * 2 * rows : (slab + 1) * 2 * rows] = jnp.where(side == 0, right, left)
    row = iota((16, LANES), 0)
    block = jnp.zeros((16, LANES), F32)
    for part in range(2):
        rest = jnp.full((16, LANES), angle_freq[chosen[0], part], F32)
        for piece in range(3):
            rounded = rest.astype(BF16).astype(F32)
            block = jnp.where(row == 3 * part + piece, rounded, block)
            rest = rest - rounded
    across[4 * rows :] = block.astype(BF16)


def measured_kernel(measured, own, other):
    rows, cols = measured.shape[1], measured.shape[3] // 2
    side = lax.axis_index("ang")
    first = measured[0, :, :, :cols].reshape(2 * rows, cols)
    second = measured[0, :, :, cols:].reshape(2 * rows, cols)
    before = measured[0, :, :, cols - LANES : cols].reshape(2 * rows, LANES)
    after = measured[0, :, :, cols : cols + LANES].reshape(2 * rows, LANES)
    own[:, :cols] = jnp.where(side == 0, first, second)
    own[:, cols:] = jnp.where(side == 0, after, before)
    other[:, :cols] = jnp.where(side == 0, second, first)
    other[:, cols:] = jnp.where(side == 0, before, after)


def skewed(base, count, stride):
    width = base.shape[1]
    return pltpu.roll(jnp.broadcast_to(base, (count, width)), 0, 1, stride=stride, stride_axis=0)


def matrices_kernel(
    rows, cols, length, taps, angle_freq, chosen, across,
    row_near, row_fwd, row_adj, row_near_adj, col_taps, split_far, split_meas, waves,
):
    count = taps.shape[1]
    half = (count - 1) // 2
    wide = rows + 4 * half
    mid = rows + 2 * half
    side = lax.axis_index("ang")
    table = jnp.concatenate(
        [jnp.concatenate([taps[...], jnp.zeros((2, LANES - count), BF16)], axis=1),
         jnp.zeros((14, LANES), BF16)], axis=0,
    )

    def spread(width, place):
        tap = iota((LANES, width), 0)
        lane = iota((LANES, width), 1)
        hit = jnp.logical_and(lane == place(tap), tap < count)
        return dot(table, jnp.where(hit, 1.0, 0.0).astype(BF16))

    sent = across[4 * rows :].astype(F32)
    freqs = []
    for part in range(2):
        own = jnp.full((1, 1), angle_freq[chosen[0], part], F32)
        got = sent[3 * part : 3 * part + 1] + sent[3 * part + 1 : 3 * part + 2]
        got = got + sent[3 * part + 2 : 3 * part + 3]
        freqs.append((own, got[:, :1]))
    scale = 2.0 * math.pi / length

    lane = iota((1, cols + LANES), 1)
    col = jnp.where(side == 0, lane, jnp.where(lane < cols, lane + cols, lane - LANES)).astype(F32)
    for member in range(2):
        phase = scale * (freqs[1][member] * col)
        waves[2 * member : 2 * member + 1] = jnp.cos(phase)
        waves[2 * member + 1 : 2 * member + 2] = jnp.sin(phase)

    even = spread(2 * wide, lambda tap: 2 * tap)
    odd = spread(2 * wide, lambda tap: 2 * tap + 1)
    real = skewed(even[0:1] - odd[1:2], mid, 2)
    imag = skewed(even[1:2] + odd[0:1], mid, 2)
    start = lax.axis_index("rows") * rows - 2 * half
    row = (start + iota((1, 2 * wide), 1) // 2).astype(F32)
    for member in range(2):
        phase = scale * (freqs[0][member] * row)
        cos, sin = jnp.cos(phase), jnp.sin(phase)
        full = jnp.concatenate([real * cos - imag * sin, imag * cos + real * sin], axis=0)
        at = member * 2 * mid
        row_near[at : at + 2 * mid] = full.astype(BF16)
        row_near_adj[:, at : at + 2 * mid] = full.T.astype(BF16)

    low = spread(2 * mid, lambda tap: tap)
    high = spread(2 * mid, lambda tap: mid + tap)
    full = jnp.concatenate(
        [skewed(low[0:1] - high[1:2], rows, 1), skewed(low[1:2] + high[0:1], rows, 1)], axis=0
    )
    row_fwd[...] = full.astype(BF16)
    row_adj[...] = full.T.astype(BF16)

    window = 2 * LANES
    source = iota((window, LANES), 0)
    target = iota((window, LANES), 1)
    same_side = (source < LANES) == (target < LANES - half)
    left_only = source < window - half
    right_only = source >= LANES - half
    everything = source >= 0
    at = 0
    for adjoint in (False, True):
        for offset, masks in ((0, (everything, same_side)), (2 * half, (everything, left_only, right_only))):
            if adjoint:
                base = spread(window, lambda tap: (window - offset - (count - 1) + tap) % window)
            else:
                base = spread(window, lambda tap: (window - offset - tap) % window)
            re = skewed(base[0:1], window, 1)[:, :LANES]
            im = skewed(base[1:2], window, 1)[:, :LANES]
            im = -im if adjoint else im
            for mask in masks:
                mre = jnp.where(mask, re, 0.0).astype(BF16)
                mim = jnp.where(mask, im, 0.0).astype(BF16)
                col_taps[at, :window, :LANES] = mre
                col_taps[at, :window, LANES:] = mim
                col_taps[at, window:, :LANES] = -mim
                col_taps[at, window:, LANES:] = mre
                at += 1

    for out in (split_far, split_meas):
        size = out.shape[0]
        to, frm = iota((size, size), 0), iota((size, size), 1)
        out[...] = jnp.where(frm == 2 * (to % (size // 2)) + to // (size // 2), 1.0, 0.0).astype(BF16)


def main_kernel(
    half,
    slices, outer, inner, across, corner, across_inner, meas_own, meas_other,
    row_near, row_fwd, row_adj, row_near_adj, col_taps, split_far, split_meas, waves,
    near_own, far_own, outer_sums, inner_sums,
    near_slab, far_raw, far_slab, entry, field, after, carry, shifted, narrow, meas, into, far_sum,
):
    rows, cols = slices.shape[1], slices.shape[3]
    tiles = cols // LANES + 1
    width = tiles * LANES
    wide, mid = rows + 4 * half, rows + 2 * half
    parity = lax.axis_index("rows") % 2
    side = lax.axis_index("ang")
    chunks = lane_chunks(width)
    cut = tiles - 1 - side
    cut_next = lax.rem(cut + 1, tiles)

    def tile(j):
        return pl.ds(pl.multiple_of(j * LANES, LANES), LANES)

    def pair(j):
        return pl.ds(pl.multiple_of(j * LANES, LANES), 2 * LANES)

    def ahead(j, base):
        return base + jnp.where(j == cut, 1, 0)

    def back(j, base):
        return base + jnp.where(j == cut, 1, jnp.where(j == cut_next, 2, 0))

    for slab, ref, margin in ((0, near_slab, 4 * half), (1, far_raw, 2 * half)):
        ref[margin : margin + 2 * rows, :cols] = slices[slab].reshape(2 * rows, cols)
        ref[margin : margin + 2 * rows, cols:width] = across[slab * 2 * rows : (slab + 1) * 2 * rows]
        begin = 0 if slab == 0 else 4 * half
        for late, body, tail in ((parity, outer, corner), (1 - parity, inner, None)):
            at = pl.ds(pl.multiple_of(late * (2 * rows + margin), 16), margin)
            ref[at, :cols] = body[begin : begin + margin]
            if tail is not None:
                ref[at, cols:width] = tail[begin : begin + margin]
            else:
                frm = slab * 2 * rows + (1 - late) * (2 * rows - margin)
                ref[at, cols:width] = across_inner[pl.ds(pl.multiple_of(frm, 16), margin)]
    far_raw[:, width:] = far_raw[:, :LANES]

    def planar(j, carry_):
        both = dot(split_far[...], far_raw[:, pair(j)])
        far_slab[:, tile(j)] = both[:, half : half + LANES]
        return carry_

    lax.fori_loop(0, tiles, planar, 0)

    for at, size in chunks:
        result = dot(row_near[...], near_slab[:, at : at + size])
        for member in range(2):
            top = member * 2 * mid
            re, im = result[top : top + mid], result[top + mid : top + 2 * mid]
            vr = waves[2 * member : 2 * member + 1, at : at + size]
            vi = waves[2 * member + 1 : 2 * member + 2, at : at + size]
            entry[member, :mid, at : at + size] = (re * vr - im * vi).astype(BF16)
            entry[member, mid:, at : at + size] = (re * vi + im * vr).astype(BF16)
    for member in range(2):
        entry[member, :, width:] = entry[member, :, :LANES]

    def angle(member, measured):
        def first(j, carry_):
            x = jnp.concatenate([entry[member, :mid, pair(j)], entry[member, mid:, pair(j)]], axis=1)
            y = dot(x, col_taps[ahead(j, 0)]).astype(BF16)
            re, im = y[:, :LANES], y[:, LANES:]
            field[:mid, tile(j)] = re
            field[mid:, tile(j)] = im
            re, im = re.astype(F32), im.astype(F32)
            sr, si = far_slab[:mid, tile(j)], far_slab[mid:, tile(j)]
            after[:mid, tile(j)] = (sr * re - si * im).astype(BF16)
            after[mid:, tile(j)] = (sr * im + si * re).astype(BF16)
            return carry_

        lax.fori_loop(0, tiles, first, 0)
        for at, size in chunks:
            narrow[:, LANES + at : LANES + at + size] = dot(row_fwd[...], after[:, at : at + size]).astype(BF16)
            meas[:, at : at + size] = dot(split_meas[...], measured[:, at : at + size])
        narrow[:, :LANES] = narrow[:, width : width + LANES]

        def second(j, carry_):
            x = jnp.concatenate([narrow[:rows, pair(j)], narrow[rows:, pair(j)]], axis=1)
            y = dot(x, col_taps[back(j, 2)]).astype(BF16).astype(F32)
            shifted[:rows, tile(j)] = (y[:, :LANES] - meas[:rows, tile(j)]).astype(BF16)
            shifted[rows:, tile(j)] = (y[:, LANES:] - meas[rows:, tile(j)]).astype(BF16)
            return carry_

        lax.fori_loop(0, tiles, second, 0)
        shifted[:, width:] = shifted[:, :LANES]

        def third(j, carry_):
            x = jnp.concatenate([shifted[:rows, pair(j)], shifted[rows:, pair(j)]], axis=1)
            y = dot(x, col_taps[ahead(j, 5)]).astype(BF16)
            narrow[:rows, tile(j)] = y[:, :LANES]
            narrow[rows:, tile(j)] = y[:, LANES:]
            return carry_

        lax.fori_loop(0, tiles, third, 0)
        for at, size in chunks:
            y = dot(row_adj[...], narrow[:, at : at + size])
            br, bi = y[:mid], y[mid:]
            ir, ii = field[:mid, at : at + size].astype(F32), field[mid:, at : at + size].astype(F32)
            sr, si = far_slab[:mid, at : at + size], far_slab[mid:, at : at + size]
            here = slice(LANES + at, LANES + at + size)
            carry[:mid, here] = (sr * br + si * bi).astype(BF16)
            carry[mid:, here] = (sr * bi - si * br).astype(BF16)
            fr, fi = ir * br + ii * bi, ir * bi - ii * br
            if member == 0:
                far_sum[:mid, here] = fr
                far_sum[mid:, here] = fi
            else:
                far_sum[:mid, here] += fr
                far_sum[mid:, here] += fi
        carry[:, :LANES] = carry[:, width : width + LANES]

        def fourth(j, carry_):
            x = jnp.concatenate([carry[:mid, pair(j)], carry[mid:, pair(j)]], axis=1)
            y = dot(x, col_taps[back(j, 7)])
            re, im = y[:, :LANES], y[:, LANES:]
            vr = waves[2 * member : 2 * member + 1, tile(j)]
            vi = waves[2 * member + 1 : 2 * member + 2, tile(j)]
            top = member * 2 * mid
            into[top : top + mid, tile(j)] = (re * vr + im * vi).astype(BF16)
            into[top + mid : top + 2 * mid, tile(j)] = (im * vr - re * vi).astype(BF16)
            return carry_

        lax.fori_loop(0, tiles - 1, fourth, 0)

    angle(0, meas_own)
    angle(1, meas_other)

    near_margin = 4 * half
    for at, size in lane_chunks(cols):
        here = slice(at, at + size)
        y = dot(row_near_adj[...], into[:, here])
        near_own[:, here] = y[near_margin : near_margin + 2 * rows]
        low = y[:near_margin].astype(BF16)
        high = y[near_margin + 2 * rows :].astype(BF16)
        outer_sums[:near_margin, here] = jnp.where(parity == 0, low, high)
        inner_sums[:near_margin, here] = jnp.where(parity == 0, high, low)
    far_sum[:, :LANES] = far_sum[:, width : width + LANES]

    def far_out(j, carry_):
        y = far_sum[:, pair(j)][:, LANES - half : 2 * LANES - half]
        for comp in range(2):
            part = y[comp * mid : (comp + 1) * mid]
            far_own[comp, :, tile(j)] = part[half : half + rows]
            low, high = part[:half].astype(BF16), part[half + rows :].astype(BF16)
            top = near_margin + comp * half
            outer_sums[top : top + half, tile(j)] = jnp.where(parity == 0, low, high)
            inner_sums[top : top + half, tile(j)] = jnp.where(parity == 0, high, low)
        return carry_

    lax.fori_loop(0, tiles - 1, far_out, 0)


def finish_kernel(half, near_own, far_own, outer, inner, near, far, total):
    rows, cols = near.shape[0], near.shape[2]
    parity = lax.axis_index("rows") % 2
    size = 4 * half
    total[...] = near_own[...]
    for late, got in ((parity, outer), (1 - parity, inner)):
        at = pl.ds(pl.multiple_of(late * (2 * rows - size), 16), size)
        total[at] += got[:size].astype(F32)
    near[...] = total[...].reshape(rows, 2, cols)
    for comp in range(2):
        total[:rows] = far_own[comp]
        for late, got in ((parity, outer), (1 - parity, inner)):
            at = pl.ds(pl.multiple_of(late * (rows - half), 16), half)
            total[at] += got[size + comp * half : size + (comp + 1) * half].astype(F32)
        far[:, comp, :] = total[:rows]


def call(kernel, outs, operands, scalars=(), scratch=(), cost=0):
    specs = [
        pl.BlockSpec(memory_space=pltpu.SMEM if i in scalars else pltpu.VMEM) for i in range(len(operands))
    ]
    return pl.pallas_call(
        kernel,
        out_shape=[jax.ShapeDtypeStruct(shape, dtype) for shape, dtype in outs],
        in_specs=specs,
        out_specs=[pl.BlockSpec(memory_space=pltpu.VMEM)] * len(outs),
        scratch_shapes=[pltpu.VMEM(shape, dtype) for shape, dtype in scratch],
        compiler_params=pltpu.CompilerParams(vmem_limit_bytes=40 * 2**20),
        cost_estimate=pl.CostEstimate(flops=cost, bytes_accessed=0, transcendentals=0),
    )(*operands)


def columns_local(measured, slices, kernel_taps, angle_freq, chosen):
    rows, cols = slices.shape[1], slices.shape[3]
    length = measured.shape[3]
    half = (kernel_taps.shape[1] - 1) // 2
    wide, mid, width = rows + 4 * half, rows + 2 * half, cols + LANES
    count = lax.axis_size("rows")
    sides = lax.axis_size("ang")
    outer_pairs = [(i, j) for i in range(count) if 0 <= (j := i - 1 + 2 * (i % 2)) < count]
    inner_pairs = [(i, i + 1 - 2 * (i % 2)) for i in range(count)]
    side_pairs = [(i, 1 - i) for i in range(sides)]
    corner_pairs = [
        (i * sides + s, j * sides + 1 - s) for i, j in outer_pairs for s in range(sides)
    ]
    edge = 6 * half
    outer, inner, across, corner = call(
        functools.partial(edges_kernel, half),
        [((edge, cols), BF16), ((edge, cols), BF16), ((4 * rows + 16, LANES), BF16), ((edge, LANES), BF16)],
        (slices, angle_freq, chosen), scalars=(1, 2),
    )
    outer_got = lax.ppermute(outer, "rows", outer_pairs)
    across_got = lax.ppermute(across, "ang", side_pairs)
    corner_got = lax.ppermute(corner, ("rows", "ang"), corner_pairs)
    inner_got = lax.ppermute(inner, "rows", inner_pairs)
    meas_own, meas_out = call(
        measured_kernel, [((2 * rows, width), BF16)] * 2, (measured,),
    )
    meas_got = lax.ppermute(meas_out, "ang", side_pairs)
    across_inner = lax.ppermute(across_got, "rows", inner_pairs)
    mats = call(
        functools.partial(matrices_kernel, rows, cols, length),
        [
            ((4 * mid, 2 * wide), BF16), ((2 * rows, 2 * mid), BF16), ((2 * mid, 2 * rows), BF16),
            ((2 * wide, 4 * mid), BF16), ((10, 4 * LANES, 2 * LANES), BF16),
            ((2 * mid, 2 * mid), BF16), ((2 * rows, 2 * rows), BF16), ((8, width), F32),
        ],
        (kernel_taps, angle_freq, chosen, across_got), scalars=(1, 2),
    )
    near_own, far_own, outer_sums, inner_sums = call(
        functools.partial(main_kernel, half),
        [((2 * rows, cols), F32), ((2, rows, cols), F32), ((edge, cols), BF16), ((edge, cols), BF16)],
        (slices, outer_got, inner_got, across_got, corner_got, across_inner, meas_own, meas_got, *mats),
        scratch=[
            ((2 * wide, width), BF16), ((2 * mid, width + LANES), BF16), ((2 * mid, width), F32),
            ((2, 2 * mid, width + LANES), BF16), ((2 * mid, width), BF16), ((2 * mid, width), BF16),
            ((2 * mid, width + LANES), BF16), ((2 * rows, width + LANES), BF16),
            ((2 * rows, width + LANES), BF16), ((2 * rows, width), F32), ((4 * mid, cols), BF16),
            ((2 * mid, width + LANES), F32),
        ],
        cost=8 * 10**9,
    )
    outer_back = lax.ppermute(outer_sums, "rows", outer_pairs)
    inner_back = lax.ppermute(inner_sums, "rows", inner_pairs)
    near, far = call(
        functools.partial(finish_kernel, half),
        [((rows, 2, cols), F32)] * 2,
        (near_own, far_own, outer_back, inner_back),
        scratch=[((2 * rows, cols), F32)],
    )
    return near, far


def with_halo(block, sides, width):
    for axis, dim in sides:
        count = lax.axis_size(axis)
        forward = [(i, i + 1) for i in range(count - 1)]
        backward = [(target, source) for source, target in forward]
        low = lax.ppermute(
            lax.slice_in_dim(block, block.shape[dim] - width, None, axis=dim), axis, forward
        )
        high = lax.ppermute(lax.slice_in_dim(block, 0, width, axis=dim), axis, backward)
        block = jnp.concatenate([low, block, high], axis=dim)
    return block


def toeplitz(row_taps, out_width):
    tap_count = row_taps.shape[0]
    window = out_width + tap_count - 1
    padded = jnp.concatenate([row_taps, jnp.zeros((out_width,), row_taps.dtype)])
    tiled = jnp.tile(padded, out_width)[: out_width * window]
    return tiled.reshape(out_width, window).T


def kernel_pair(kernel_taps, out_width):
    return jnp.concatenate(
        [toeplitz(kernel_taps[0], out_width), toeplitz(kernel_taps[1], out_width)], axis=1
    )


def adjoint_taps(kernel_taps):
    return jnp.stack([kernel_taps[0][::-1], -kernel_taps[1][::-1]])


def correlate_columns(field, kernel):
    window, doubled = kernel.shape
    tile_len = doubled // 2
    half_taps = (window - tile_len) // 2
    leading, comps, length = field.shape
    blocks = length // tile_len
    padded = jnp.pad(field, ((0, 0), (0, 0), (half_taps, tile_len - half_taps)))
    main_part = padded[:, :, :length].reshape(leading, comps, blocks, tile_len)
    tail_part = padded[:, :, tile_len : tile_len + length].reshape(
        leading, comps, blocks, tile_len
    )[..., : 2 * half_taps]
    windows = jnp.concatenate([main_part, tail_part], axis=3)
    product = jnp.einsum("rpnw,wk->rpnk", windows, kernel, preferred_element_type=jnp.float32)
    real_part = product[:, 0, :, :tile_len] - product[:, 1, :, tile_len:]
    imag_part = product[:, 0, :, tile_len:] + product[:, 1, :, :tile_len]
    return (
        jnp.stack([real_part, imag_part], axis=1)
        .reshape(leading, comps, length)
        .astype(jnp.bfloat16)
    )


def band_rows(padded, band):
    out_rows = band.shape[1] // 2
    product = jnp.einsum("jpc,jk->kpc", padded, band, preferred_element_type=jnp.float32)
    real_part = product[:out_rows, 0] - product[out_rows:, 1]
    imag_part = product[out_rows:, 0] + product[:out_rows, 1]
    return jnp.stack([real_part, imag_part], axis=1).astype(jnp.bfloat16)


def complex_times(left, right):
    left = left.astype(jnp.float32)
    right = right.astype(jnp.float32)
    real_part = left[:, 0] * right[:, 0] - left[:, 1] * right[:, 1]
    imag_part = left[:, 0] * right[:, 1] + left[:, 1] * right[:, 0]
    return jnp.stack([real_part, imag_part], axis=1)


def conjugate_times(left, right):
    left = left.astype(jnp.float32)
    right = right.astype(jnp.float32)
    real_part = left[:, 0] * right[:, 0] + left[:, 1] * right[:, 1]
    imag_part = left[:, 0] * right[:, 1] - left[:, 1] * right[:, 0]
    return jnp.stack([real_part, imag_part], axis=1)


def incident(freq, row_pos, col_pos, length):
    scale = 2.0 * math.pi / length
    phase = scale * (freq[0] * row_pos[:, None] + freq[1] * col_pos[None, :])
    return jnp.stack([jnp.cos(phase), jnp.sin(phase)], axis=1)


def local(measured, slices, kernel_taps, angle_freq, chosen):
    rows_dev = measured.shape[1]
    length = measured.shape[3]
    half_taps = (kernel_taps.shape[1] - 1) // 2
    backward_taps = adjoint_taps(kernel_taps)
    forward_kernel = kernel_pair(kernel_taps, 128)
    adjoint_kernel = kernel_pair(backward_taps, 128)
    forward_band = kernel_pair(kernel_taps, rows_dev)
    adjoint_band = kernel_pair(backward_taps, rows_dev)
    gathered = lax.all_gather(slices, "ang", axis=3, tiled=True)
    near_slab = gathered[0]
    far_slab = gathered[1]
    start = lax.axis_index("rows") * rows_dev
    row_pos = (start + jnp.arange(rows_dev, dtype=jnp.int32)).astype(jnp.float32)
    col_pos = jnp.arange(length).astype(jnp.float32)
    onehot = (chosen[:, None] == jnp.arange(angle_freq.shape[0], dtype=jnp.int32)[None, :]).astype(
        jnp.float32
    )
    freqs = jnp.dot(onehot, angle_freq, precision=lax.Precision.HIGHEST)

    def along_rows(field, band):
        padded = with_halo(field, (("rows", 0),), half_taps)
        result = band_rows(padded, band)
        return result

    member = 0
    entering = incident(freqs[member], row_pos, col_pos, length)
    entry0 = complex_times(near_slab, entering).astype(jnp.bfloat16)
    inner = along_rows(correlate_columns(entry0, forward_kernel), forward_band)
    entry1 = complex_times(far_slab, inner).astype(jnp.bfloat16)
    exit_field = along_rows(correlate_columns(entry1, forward_kernel), forward_band)
    residue = (exit_field.astype(jnp.float32) - measured[member].astype(jnp.float32)).astype(
        jnp.bfloat16
    )
    back_far = correlate_columns(along_rows(residue, adjoint_band), adjoint_kernel)
    grad_far = conjugate_times(inner, back_far)
    carried_list = [conjugate_times(far_slab, back_far).astype(jnp.bfloat16)]
    member = 0
    entering = incident(freqs[member], row_pos, col_pos, length)
    back_near = correlate_columns(along_rows(carried_list[member], adjoint_band), adjoint_kernel)
    grad_near = conjugate_times(entering, back_near)
    near_total, far_total = (
        lax.psum_scatter(
            grad_near.astype(jnp.bfloat16), "ang", scatter_dimension=2, tiled=True
        ).astype(jnp.float32),
        lax.psum_scatter(
            grad_far.astype(jnp.bfloat16), "ang", scatter_dimension=2, tiled=True
        ).astype(jnp.float32),
    )
    return (near_total, far_total)


def pick(measured, slices, kernel_taps, angle_freq, chosen):
    rows, cols = slices.shape[1], slices.shape[3]
    taps = kernel_taps.shape[1]
    fits = (
        lax.axis_size("ang") == 2
        and lax.axis_size("rows") % 2 == 0
        and 2 * (taps - 1) == LANES
        and rows >= taps - 1
        and rows % LANES == 0
        and cols % (2 * LANES) == 0
    )
    run = columns_local if fits else local
    return run(measured, slices, kernel_taps, angle_freq, chosen)


def solution(mesh):
    return jax.shard_map(
        pick,
        mesh=mesh,
        in_specs=(P("ang", "rows", None, None), P(None, "rows", None, "ang"), P(), P(), P("ang")),
        out_specs=(P("rows", None, "ang"), P("rows", None, "ang")),
        check_vma=False,
    )
```

```python
import functools
import math

import jax
import jax.numpy as jnp
from jax import lax
from jax.experimental import pallas as pl
from jax.experimental.pallas import tpu as pltpu
from jax.sharding import PartitionSpec as P

LANES = 128
BF16 = jnp.bfloat16
OWN_FLOPS = 4 * 10**9
F32 = jnp.float32


def dot(left, right):
    return jnp.dot(left, right, preferred_element_type=F32)


def iota(shape, dim):
    return lax.broadcasted_iota(jnp.int32, shape, dim)


def lane_chunks(width, step=2 * LANES):
    return [(at, min(step, width - at)) for at in range(0, width, step)]


def outer_kernel(half, slices, outer, sems):
    rows = slices.shape[1]
    parity = lax.axis_index("rows") % 2
    copies = []
    for slab, at, size in ((0, 0, 2 * half), (1, 2 * half, half)):
        first = pl.ds(parity * (rows - size), size)
        copies.append(pltpu.make_async_copy(slices.at[slab, first], outer.at[pl.ds(at, size)], sems.at[slab]))
    for copy in copies:
        copy.start()
    for copy in copies:
        copy.wait()


def strip_kernel(half, across, strip):
    rows = (across.shape[0] - 16) // 4
    parity = lax.axis_index("rows") % 2
    begin = 0
    for slab, size in ((0, 4 * half), (1, 2 * half)):
        frm = slab * 2 * rows + parity * (2 * rows - size)
        strip[begin : begin + size] = across[pl.ds(pl.multiple_of(frm, 16), size)]
        begin += size


def edges_kernel(half, slices, angle_freq, chosen, sent, inner, across):
    rows, cols = slices.shape[1], slices.shape[3]
    parity = lax.axis_index("rows") % 2
    side = lax.axis_index("ang")
    near = slices[0, pl.ds((1 - parity) * (rows - 2 * half), 2 * half)]
    far = slices[1, pl.ds((1 - parity) * (rows - half), half)]
    inner[: 4 * half] = near.reshape(4 * half, cols)
    inner[4 * half :] = far.reshape(2 * half, cols)
    for slab in range(2):
        left = slices[slab, :, :, :LANES].reshape(2 * rows, LANES)
        right = slices[slab, :, :, cols - LANES :].reshape(2 * rows, LANES)
        across[slab * 2 * rows : (slab + 1) * 2 * rows] = jnp.where(side == 0, right, left)
    row = iota((16, LANES), 0)
    block = jnp.zeros((16, LANES), F32)
    for part, freq in enumerate(frequencies(angle_freq, chosen)):
        rest = jnp.broadcast_to(freq, (16, LANES))
        for piece in range(3):
            rounded = rest.astype(BF16).astype(F32)
            block = jnp.where(row == 3 * part + piece, rounded, block)
            rest = rest - rounded
    across[4 * rows :] = block.astype(BF16)


def frequencies(angle_freq, chosen):
    entry = jnp.where(iota(angle_freq.shape, 1) == chosen[0], angle_freq[...], 0.0)
    pair = jnp.sum(entry, axis=1, keepdims=True)
    return pair[0:1], pair[1:2]


def measured_kernel(measured, inner, own, other):
    rows, cols = measured.shape[1], measured.shape[3] // 2
    side = lax.axis_index("ang")
    first = measured[0, :, :, :cols].reshape(2 * rows, cols)
    second = measured[0, :, :, cols:].reshape(2 * rows, cols)
    before = measured[0, :, :, cols - LANES : cols].reshape(2 * rows, LANES)
    after = measured[0, :, :, cols : cols + LANES].reshape(2 * rows, LANES)
    own[:, :cols] = jnp.where(side == 0, first, second)
    own[:, cols:] = jnp.where(side == 0, after, before)
    other[:, :cols] = jnp.where(side == 0, second, first)
    other[:, cols:] = jnp.where(side == 0, before, after)


def skewed(base, count, stride):
    width = base.shape[1]
    return pltpu.roll(jnp.broadcast_to(base, (count, width)), 0, 1, stride=stride, stride_axis=0)


def matrices_kernel(
    rows, cols, length, taps, angle_freq, chosen, across,
    row_near, row_fwd, row_adj, row_near_adj, col_taps, split_far, split_meas, waves,
):
    count = taps.shape[1]
    half = (count - 1) // 2
    wide = rows + 4 * half
    mid = rows + 2 * half
    side = lax.axis_index("ang")
    table = jnp.concatenate(
        [jnp.concatenate([taps[...], jnp.zeros((2, LANES - count), BF16)], axis=1),
         jnp.zeros((14, LANES), BF16)], axis=0,
    )

    def spread(width, place):
        tap = iota((LANES, width), 0)
        lane = iota((LANES, width), 1)
        hit = jnp.logical_and(lane == place(tap), tap < count)
        return dot(table, jnp.where(hit, 1.0, 0.0).astype(BF16))

    sent = across[4 * rows :].astype(F32)
    freqs = []
    for part, own in enumerate(frequencies(angle_freq, chosen)):
        got = sent[3 * part : 3 * part + 1] + sent[3 * part + 1 : 3 * part + 2]
        got = got + sent[3 * part + 2 : 3 * part + 3]
        freqs.append((own, got[:, :1]))
    scale = 2.0 * math.pi / length

    lane = iota((1, cols + LANES), 1)
    col = jnp.where(side == 0, lane, jnp.where(lane < cols, lane + cols, lane - LANES)).astype(F32)
    for member in range(2):
        phase = scale * (freqs[1][member] * col)
        waves[2 * member : 2 * member + 1] = jnp.cos(phase)
        waves[2 * member + 1 : 2 * member + 2] = jnp.sin(phase)

    even = spread(2 * wide, lambda tap: 2 * tap)
    odd = spread(2 * wide, lambda tap: 2 * tap + 1)
    real = skewed(even[0:1] - odd[1:2], mid, 2)
    imag = skewed(even[1:2] + odd[0:1], mid, 2)
    start = lax.axis_index("rows") * rows - 2 * half
    row = (start + iota((1, 2 * wide), 1) // 2).astype(F32)
    for member in range(2):
        phase = scale * (freqs[0][member] * row)
        cos, sin = jnp.cos(phase), jnp.sin(phase)
        full = jnp.concatenate([real * cos - imag * sin, imag * cos + real * sin], axis=0)
        at = member * 2 * mid
        row_near[at : at + 2 * mid] = full.astype(BF16)
        row_near_adj[:, at : at + 2 * mid] = full.T.astype(BF16)

    low = spread(2 * mid, lambda tap: tap)
    high = spread(2 * mid, lambda tap: mid + tap)
    full = jnp.concatenate(
        [skewed(low[0:1] - high[1:2], rows, 1), skewed(low[1:2] + high[0:1], rows, 1)], axis=0
    )
    row_fwd[...] = full.astype(BF16)
    row_adj[...] = full.T.astype(BF16)

    window = 2 * LANES
    source = iota((window, LANES), 0)
    target = iota((window, LANES), 1)
    same_side = (source < LANES) == (target < LANES - half)
    left_only = source < window - half
    right_only = source >= LANES - half
    everything = source >= 0
    at = 0
    for adjoint in (False, True):
        for offset, masks in ((0, (everything, same_side)), (2 * half, (everything, left_only, right_only))):
            if adjoint:
                base = spread(window, lambda tap: (window - offset - (count - 1) + tap) % window)
            else:
                base = spread(window, lambda tap: (window - offset - tap) % window)
            re = skewed(base[0:1], window, 1)[:, :LANES]
            im = skewed(base[1:2], window, 1)[:, :LANES]
            im = -im if adjoint else im
            for mask in masks:
                mre = jnp.where(mask, re, 0.0).astype(BF16)
                mim = jnp.where(mask, im, 0.0).astype(BF16)
                col_taps[at, :window, :LANES] = mre
                col_taps[at, :window, LANES:] = mim
                col_taps[at, window:, :LANES] = -mim
                col_taps[at, window:, LANES:] = mre
                at += 1

    for out in (split_far, split_meas):
        size = out.shape[0]
        to, frm = iota((size, size), 0), iota((size, size), 1)
        out[...] = jnp.where(frm == 2 * (to % (size // 2)) + to // (size // 2), 1.0, 0.0).astype(BF16)


class Tiles:
    def __init__(self, cols):
        self.count = cols // LANES + 1
        self.width = self.count * LANES
        self.cut = self.count - 1 - lax.axis_index("ang")
        self.after = lax.rem(self.cut + 1, self.count)

    def ahead(self, j, base):
        return base + jnp.where(j == self.cut, 1, 0) if j >= self.count - 2 else base

    def back(self, j, base):
        if 0 < j < self.count - 2:
            return base
        return base + jnp.where(j == self.cut, 1, jnp.where(j == self.after, 2, 0))


def tile(j):
    return slice(j * LANES, (j + 1) * LANES)


def pair(j):
    return slice(j * LANES, (j + 2) * LANES)


def both_parts(ref, j):
    size = ref.shape[0] // 2
    return jnp.concatenate([ref[:size, pair(j)], ref[size:, pair(j)]], axis=1)


def forward_angle(tiles, entry, far_slab, row_fwd, col_taps, field, after, narrow, leaving):
    mid = field.shape[0] // 2
    rows = leaving.shape[0] // 2
    for j in range(tiles.count):
        y = dot(both_parts(entry, j), col_taps[tiles.ahead(j, 0)]).astype(BF16)
        re, im = y[:, :LANES], y[:, LANES:]
        field[:mid, tile(j)] = re
        field[mid:, tile(j)] = im
        re, im = re.astype(F32), im.astype(F32)
        sr, si = far_slab[:mid, tile(j)], far_slab[mid:, tile(j)]
        after[:mid, tile(j)] = (sr * re - si * im).astype(BF16)
        after[mid:, tile(j)] = (sr * im + si * re).astype(BF16)
    for at, size in lane_chunks(tiles.width):
        narrow[:, LANES + at : LANES + at + size] = dot(row_fwd[...], after[:, at : at + size]).astype(BF16)
    narrow[:, :LANES] = narrow[:, tiles.width :]
    for j in range(tiles.count):
        y = dot(both_parts(narrow, j), col_taps[tiles.back(j, 2)]).astype(BF16)
        leaving[:rows, tile(j)] = y[:, :LANES]
        leaving[rows:, tile(j)] = y[:, LANES:]


def backward_angle(
    tiles, member, leaving, measured, field, far_slab, split_meas, row_adj, col_taps, waves, residue, narrow, carry,
    far_sum, into,
):
    mid = field.shape[0] // 2
    rows = leaving.shape[0] // 2
    for at, size in lane_chunks(tiles.width):
        here = slice(at, at + size)
        meas = dot(split_meas[...], measured[:, here])
        residue[:, here] = (leaving[:, here].astype(F32) - meas).astype(BF16)
    residue[:, tiles.width :] = residue[:, :LANES]
    for j in range(tiles.count):
        y = dot(both_parts(residue, j), col_taps[tiles.ahead(j, 5)]).astype(BF16)
        narrow[:rows, tile(j)] = y[:, :LANES]
        narrow[rows:, tile(j)] = y[:, LANES:]
    for at, size in lane_chunks(tiles.width):
        y = dot(row_adj[...], narrow[:, at : at + size])
        br, bi = y[:mid], y[mid:]
        ir, ii = field[:mid, at : at + size].astype(F32), field[mid:, at : at + size].astype(F32)
        sr, si = far_slab[:mid, at : at + size], far_slab[mid:, at : at + size]
        here = slice(LANES + at, LANES + at + size)
        carry[:mid, here] = (sr * br + si * bi).astype(BF16)
        carry[mid:, here] = (sr * bi - si * br).astype(BF16)
        far_sum(at, here, ir * br + ii * bi, ir * bi - ii * br)
    carry[:, :LANES] = carry[:, tiles.width :]
    for j in range(tiles.count - 1):
        y = dot(both_parts(carry, j), col_taps[tiles.back(j, 7)])
        re, im = y[:, :LANES], y[:, LANES:]
        vr, vi = waves[2 * member : 2 * member + 1, tile(j)], waves[2 * member + 1 : 2 * member + 2, tile(j)]
        into[:mid, tile(j)] = (re * vr + im * vi).astype(BF16)
        into[mid:, tile(j)] = (im * vr - re * vi).astype(BF16)


def own_kernel(
    half,
    slices, outer, inner, across, corner, across_inner, meas_own,
    row_near, row_fwd, row_adj, col_taps, split_far, split_meas, waves,
    far_slab, field_other, leaving_other, far_sum, into_own,
    near_slab, far_raw, entry, field, after, narrow, leaving, residue, carry,
):
    rows, cols = slices.shape[1], slices.shape[3]
    tiles = Tiles(cols)
    width = tiles.width
    mid = rows + 2 * half
    parity = lax.axis_index("rows") % 2

    for slab, ref, margin in ((0, near_slab, 4 * half), (1, far_raw, 2 * half)):
        ref[margin : margin + 2 * rows, :cols] = slices[slab].reshape(2 * rows, cols)
        ref[margin : margin + 2 * rows, cols:width] = across[slab * 2 * rows : (slab + 1) * 2 * rows]
        begin = 0 if slab == 0 else 4 * half
        outer_at = pl.ds(pl.multiple_of(parity * (2 * rows + margin), 16), margin)
        inner_at = pl.ds(pl.multiple_of((1 - parity) * (2 * rows + margin), 16), margin)
        ref[outer_at, :cols] = outer[begin // 2 : (begin + margin) // 2].reshape(margin, cols)
        ref[outer_at, cols:width] = corner[begin : begin + margin]
        ref[inner_at, :cols] = inner[begin : begin + margin]
        frm = slab * 2 * rows + parity * (2 * rows - margin)
        ref[inner_at, cols:width] = across_inner[pl.ds(pl.multiple_of(frm, 16), margin)]
    far_raw[:, width:] = far_raw[:, :LANES]

    for j in range(tiles.count):
        far_slab[:, tile(j)] = dot(split_far[...], far_raw[:, pair(j)])[:, half : half + LANES]

    for at, size in lane_chunks(width):
        here = slice(at, at + size)
        result = dot(row_near[...], near_slab[:, here])
        for member in range(2):
            top = member * 2 * mid
            re, im = result[top : top + mid], result[top + mid : top + 2 * mid]
            vr, vi = waves[2 * member : 2 * member + 1, here], waves[2 * member + 1 : 2 * member + 2, here]
            entry[member, :mid, here] = (re * vr - im * vi).astype(BF16)
            entry[member, mid:, here] = (re * vi + im * vr).astype(BF16)
    for member in range(2):
        entry[member, :, width:] = entry[member, :, :LANES]

    def store(at, here, re, im):
        far_sum[:mid, here] = re
        far_sum[mid:, here] = im

    forward_angle(tiles, entry.at[0], far_slab, row_fwd, col_taps, field, after, narrow, leaving)
    backward_angle(
        tiles, 0, leaving, meas_own, field, far_slab, split_meas, row_adj, col_taps, waves, residue, narrow, carry,
        store, into_own,
    )
    forward_angle(
        tiles, entry.at[1], far_slab, row_fwd, col_taps, field_other, after, narrow, leaving_other
    )


def other_kernel(
    half,
    far_slab, field, leaving, far_own, into_own, measured,
    row_adj, row_near_adj, col_taps, split_meas, waves,
    into, far_sum, outer_sums, inner_sums,
    residue, narrow, carry,
):
    cols = into_own.shape[1]
    tiles = Tiles(cols)
    mid = field.shape[0] // 2
    rows = mid - 2 * half
    parity = lax.axis_index("rows") % 2

    def add(at, here, re, im):
        far_sum[:mid, here] = far_own[:mid, here] + re
        far_sum[mid:, here] = far_own[mid:, here] + im

    into[: 2 * mid] = into_own[...]
    backward_angle(
        tiles, 1, leaving, measured, field, far_slab, split_meas, row_adj, col_taps, waves, residue, narrow, carry,
        add, into.at[2 * mid :],
    )
    far_sum[:, :LANES] = far_sum[:, tiles.width :]

    margin = 4 * half
    for at, size in lane_chunks(cols):
        here = slice(at, at + size)
        low = dot(row_near_adj[:margin], into[:, here]).astype(BF16)
        high = dot(row_near_adj[margin + 2 * rows :], into[:, here]).astype(BF16)
        outer_sums[:margin, here] = jnp.where(parity == 0, low, high)
        inner_sums[:margin, here] = jnp.where(parity == 0, high, low)
    for j in range(tiles.count - 1):
        for comp in range(2):
            top = comp * mid
            low = far_sum[top : top + half, pair(j)][:, LANES - half : 2 * LANES - half].astype(BF16)
            high = far_sum[top + half + rows : top + mid, pair(j)][:, LANES - half : 2 * LANES - half].astype(BF16)
            there = slice(margin + comp * half, margin + (comp + 1) * half)
            outer_sums[there, tile(j)] = jnp.where(parity == 0, low, high)
            inner_sums[there, tile(j)] = jnp.where(parity == 0, high, low)


def sums_kernel(
    half, into, far_sum, row_near_adj, inner, near, far, near_edge, far_edge, near_total, far_total, sems
):
    cols = into.shape[1]
    mid = far_sum.shape[0] // 2
    rows = mid - 2 * half
    parity = lax.axis_index("rows") % 2
    margin = 4 * half
    for j in range(cols // LANES):
        for comp in range(2):
            top = comp * mid + half
            far_total[:, comp, tile(j)] = far_sum[top : top + rows, pair(j)][:, LANES - half : 2 * LANES - half]
    at = pl.ds((1 - parity) * (rows - half), half)
    for comp in range(2):
        far_total[at, comp, :] += inner[margin + comp * half : margin + (comp + 1) * half].astype(F32)
    far_edge[...] = far_total[pl.ds(parity * (rows - half), half)]
    rest = pl.ds((1 - parity) * half, rows - half)
    far_copy = pltpu.make_async_copy(far_total.at[rest], far.at[rest], sems.at[0])
    far_copy.start()
    for at, size in lane_chunks(cols):
        here = slice(at, at + size)
        y = dot(row_near_adj[margin : margin + 2 * rows], into[:, here])
        near_total[:, :, here] = y.reshape(rows, 2, size)
    at = pl.ds((1 - parity) * (rows - 2 * half), 2 * half)
    near_total[at] += inner[:margin].astype(F32).reshape(2 * half, 2, cols)
    near_edge[...] = near_total[pl.ds(parity * (rows - 2 * half), 2 * half)]
    rest = pl.ds((1 - parity) * 2 * half, rows - 2 * half)
    near_copy = pltpu.make_async_copy(near_total.at[rest], near.at[rest], sems.at[1])
    near_copy.start()
    far_copy.wait()
    near_copy.wait()


def finish_kernel(half, near_in, far_in, near_edge, far_edge, outer, near, far, near_total, far_total, sems):
    rows, cols = near.shape[0], near.shape[2]
    parity = lax.axis_index("rows") % 2
    margin = 4 * half
    near_total[...] = near_edge[...] + outer[:margin].astype(F32).reshape(2 * half, 2, cols)
    at = pl.ds(parity * (rows - 2 * half), 2 * half)
    near_copy = pltpu.make_async_copy(near_total, near.at[at], sems.at[0])
    near_copy.start()
    for comp in range(2):
        got = outer[margin + comp * half : margin + (comp + 1) * half].astype(F32)
        far_total[:, comp, :] = far_edge[:, comp, :] + got
    at = pl.ds(parity * (rows - half), half)
    far_copy = pltpu.make_async_copy(far_total, far.at[at], sems.at[1])
    far_copy.start()
    near_copy.wait()
    far_copy.wait()


def call(kernel, outs, operands, scalars=(), outside=(), outs_outside=(), scratch=(), aliases=None, flops=0):
    def place(i):
        return pltpu.SMEM if i in scalars else pl.ANY if i in outside else pltpu.VMEM

    return pl.pallas_call(
        kernel,
        out_shape=[jax.ShapeDtypeStruct(shape, dtype) for shape, dtype in outs],
        in_specs=[pl.BlockSpec(memory_space=place(i)) for i in range(len(operands))],
        out_specs=[
            pl.BlockSpec(memory_space=pl.ANY if i in outs_outside else pltpu.VMEM) for i in range(len(outs))
        ],
        scratch_shapes=[one if not isinstance(one, tuple) else pltpu.VMEM(*one) for one in scratch],
        input_output_aliases=aliases or {},
        compiler_params=pltpu.CompilerParams(vmem_limit_bytes=40 * 2**20),
        cost_estimate=pl.CostEstimate(flops=flops, bytes_accessed=0, transcendentals=0),
    )(*operands)


def columns_local(measured, slices, kernel_taps, angle_freq, chosen):
    rows, cols = slices.shape[1], slices.shape[3]
    length = measured.shape[3]
    half = (kernel_taps.shape[1] - 1) // 2
    wide, mid, width = rows + 4 * half, rows + 2 * half, cols + LANES
    count = lax.axis_size("rows")
    outer_pairs = [(i, j) for i in range(count) if 0 <= (j := i - 1 + 2 * (i % 2)) < count]
    inner_pairs = [(i, i + 1 - 2 * (i % 2)) for i in range(count)]
    side_pairs = [(i, 1 - i) for i in range(lax.axis_size("ang"))]
    edge = 6 * half
    (outer,) = call(
        functools.partial(outer_kernel, half), [((3 * half, 2, cols), BF16)], (slices,), outside=(0,),
        outs_outside=(0,), scratch=[pltpu.SemaphoreType.DMA((2,))],
    )
    outer_got = lax.ppermute(outer, "rows", outer_pairs)
    angle_freq = angle_freq.T
    inner, across = call(
        functools.partial(edges_kernel, half),
        [((edge, cols), BF16), ((4 * rows + 16, LANES), BF16)],
        (slices, angle_freq, chosen, outer), scalars=(2,), outside=(3,),
    )
    across_got = lax.ppermute(across, "ang", side_pairs)
    inner_got = lax.ppermute(inner, "rows", inner_pairs)
    meas_own, meas_out = call(
        measured_kernel, [((2 * rows, width), BF16)] * 2, (measured, inner), outside=(1,),
    )
    meas_got = lax.ppermute(meas_out, "ang", side_pairs)
    across_inner = lax.ppermute(across_got, "rows", inner_pairs)
    (strip,) = call(functools.partial(strip_kernel, half), [((edge, LANES), BF16)], (across_got,))
    corner_got = lax.ppermute(strip, "rows", outer_pairs)
    row_near, row_fwd, row_adj, row_near_adj, col_taps, split_far, split_meas, waves = call(
        functools.partial(matrices_kernel, rows, cols, length),
        [
            ((4 * mid, 2 * wide), BF16), ((2 * rows, 2 * mid), BF16), ((2 * mid, 2 * rows), BF16),
            ((2 * wide, 4 * mid), BF16), ((10, 4 * LANES, 2 * LANES), BF16),
            ((2 * mid, 2 * mid), BF16), ((2 * rows, 2 * rows), BF16), ((8, width), F32),
        ],
        (kernel_taps, angle_freq, chosen, across_got), scalars=(2,),
    )
    far_slab, field_other, leaving_other, far_sum, into_own = call(
        functools.partial(own_kernel, half),
        [
            ((2 * mid, width), F32), ((2 * mid, width), BF16), ((2 * rows, width), BF16),
            ((2 * mid, width + LANES), F32), ((2 * mid, cols), BF16),
        ],
        (
            slices, outer_got, inner_got, across_got, corner_got, across_inner, meas_own,
            row_near, row_fwd, row_adj, col_taps, split_far, split_meas, waves,
        ),
        scratch=[
            ((2 * wide, width), BF16), ((2 * mid, width + LANES), BF16), ((2, 2 * mid, width + LANES), BF16),
            ((2 * mid, width), BF16), ((2 * mid, width), BF16), ((2 * rows, width + LANES), BF16),
            ((2 * rows, width), BF16), ((2 * rows, width + LANES), BF16), ((2 * mid, width + LANES), BF16),
        ],
        flops=OWN_FLOPS,
    )
    into, far_sum, outer_sums, inner_sums = call(
        functools.partial(other_kernel, half),
        [
            ((4 * mid, cols), BF16), ((2 * mid, width + LANES), F32), ((edge, cols), BF16), ((edge, cols), BF16),
        ],
        (
            far_slab, field_other, leaving_other, far_sum, into_own, meas_got,
            row_adj, row_near_adj, col_taps, split_meas, waves,
        ),
        scratch=[
            ((2 * rows, width + LANES), BF16), ((2 * rows, width + LANES), BF16), ((2 * mid, width + LANES), BF16),
        ],
    )
    outer_back = lax.ppermute(outer_sums, "rows", outer_pairs)
    inner_back = lax.ppermute(inner_sums, "rows", inner_pairs)
    near, far, near_edge, far_edge = call(
        functools.partial(sums_kernel, half),
        [
            ((rows, 2, cols), F32), ((rows, 2, cols), F32), ((2 * half, 2, cols), F32), ((half, 2, cols), F32),
        ],
        (into, far_sum, row_near_adj, inner_back), outs_outside=(0, 1),
        scratch=[((rows, 2, cols), F32), ((rows, 2, cols), F32), pltpu.SemaphoreType.DMA((2,))],
    )
    near, far = call(
        functools.partial(finish_kernel, half),
        [((rows, 2, cols), F32)] * 2,
        (near, far, near_edge, far_edge, outer_back), outside=(0, 1), outs_outside=(0, 1), aliases={0: 0, 1: 1},
        scratch=[((2 * half, 2, cols), F32), ((half, 2, cols), F32), pltpu.SemaphoreType.DMA((2,))],
    )
    return near, far


def with_halo(block, sides, width):
    for axis, dim in sides:
        count = lax.axis_size(axis)
        forward = [(i, i + 1) for i in range(count - 1)]
        backward = [(target, source) for source, target in forward]
        low = lax.ppermute(
            lax.slice_in_dim(block, block.shape[dim] - width, None, axis=dim), axis, forward
        )
        high = lax.ppermute(lax.slice_in_dim(block, 0, width, axis=dim), axis, backward)
        block = jnp.concatenate([low, block, high], axis=dim)
    return block


def toeplitz(row_taps, out_width):
    tap_count = row_taps.shape[0]
    window = out_width + tap_count - 1
    padded = jnp.concatenate([row_taps, jnp.zeros((out_width,), row_taps.dtype)])
    tiled = jnp.tile(padded, out_width)[: out_width * window]
    return tiled.reshape(out_width, window).T


def kernel_pair(kernel_taps, out_width):
    return jnp.concatenate(
        [toeplitz(kernel_taps[0], out_width), toeplitz(kernel_taps[1], out_width)], axis=1
    )


def adjoint_taps(kernel_taps):
    return jnp.stack([kernel_taps[0][::-1], -kernel_taps[1][::-1]])


def correlate_columns(field, kernel):
    window, doubled = kernel.shape
    tile_len = doubled // 2
    half_taps = (window - tile_len) // 2
    leading, comps, length = field.shape
    blocks = length // tile_len
    padded = jnp.pad(field, ((0, 0), (0, 0), (half_taps, tile_len - half_taps)))
    main_part = padded[:, :, :length].reshape(leading, comps, blocks, tile_len)
    tail_part = padded[:, :, tile_len : tile_len + length].reshape(
        leading, comps, blocks, tile_len
    )[..., : 2 * half_taps]
    windows = jnp.concatenate([main_part, tail_part], axis=3)
    product = jnp.einsum("rpnw,wk->rpnk", windows, kernel, preferred_element_type=jnp.float32)
    real_part = product[:, 0, :, :tile_len] - product[:, 1, :, tile_len:]
    imag_part = product[:, 0, :, tile_len:] + product[:, 1, :, :tile_len]
    return (
        jnp.stack([real_part, imag_part], axis=1)
        .reshape(leading, comps, length)
        .astype(jnp.bfloat16)
    )


def band_rows(padded, band):
    out_rows = band.shape[1] // 2
    product = jnp.einsum("jpc,jk->kpc", padded, band, preferred_element_type=jnp.float32)
    real_part = product[:out_rows, 0] - product[out_rows:, 1]
    imag_part = product[out_rows:, 0] + product[:out_rows, 1]
    return jnp.stack([real_part, imag_part], axis=1).astype(jnp.bfloat16)


def complex_times(left, right):
    left = left.astype(jnp.float32)
    right = right.astype(jnp.float32)
    real_part = left[:, 0] * right[:, 0] - left[:, 1] * right[:, 1]
    imag_part = left[:, 0] * right[:, 1] + left[:, 1] * right[:, 0]
    return jnp.stack([real_part, imag_part], axis=1)


def conjugate_times(left, right):
    left = left.astype(jnp.float32)
    right = right.astype(jnp.float32)
    real_part = left[:, 0] * right[:, 0] + left[:, 1] * right[:, 1]
    imag_part = left[:, 0] * right[:, 1] - left[:, 1] * right[:, 0]
    return jnp.stack([real_part, imag_part], axis=1)


def incident(freq, row_pos, col_pos, length):
    scale = 2.0 * math.pi / length
    phase = scale * (freq[0] * row_pos[:, None] + freq[1] * col_pos[None, :])
    return jnp.stack([jnp.cos(phase), jnp.sin(phase)], axis=1)


def local(measured, slices, kernel_taps, angle_freq, chosen):
    rows_dev = measured.shape[1]
    length = measured.shape[3]
    half_taps = (kernel_taps.shape[1] - 1) // 2
    backward_taps = adjoint_taps(kernel_taps)
    forward_kernel = kernel_pair(kernel_taps, 128)
    adjoint_kernel = kernel_pair(backward_taps, 128)
    forward_band = kernel_pair(kernel_taps, rows_dev)
    adjoint_band = kernel_pair(backward_taps, rows_dev)
    gathered = lax.all_gather(slices, "ang", axis=3, tiled=True)
    near_slab = gathered[0]
    far_slab = gathered[1]
    start = lax.axis_index("rows") * rows_dev
    row_pos = (start + jnp.arange(rows_dev, dtype=jnp.int32)).astype(jnp.float32)
    col_pos = jnp.arange(length).astype(jnp.float32)
    onehot = (chosen[:, None] == jnp.arange(angle_freq.shape[0], dtype=jnp.int32)[None, :]).astype(
        jnp.float32
    )
    freqs = jnp.dot(onehot, angle_freq, precision=lax.Precision.HIGHEST)

    def along_rows(field, band):
        padded = with_halo(field, (("rows", 0),), half_taps)
        result = band_rows(padded, band)
        return result

    member = 0
    entering = incident(freqs[member], row_pos, col_pos, length)
    entry0 = complex_times(near_slab, entering).astype(jnp.bfloat16)
    inner = along_rows(correlate_columns(entry0, forward_kernel), forward_band)
    entry1 = complex_times(far_slab, inner).astype(jnp.bfloat16)
    exit_field = along_rows(correlate_columns(entry1, forward_kernel), forward_band)
    residue = (exit_field.astype(jnp.float32) - measured[member].astype(jnp.float32)).astype(
        jnp.bfloat16
    )
    back_far = correlate_columns(along_rows(residue, adjoint_band), adjoint_kernel)
    grad_far = conjugate_times(inner, back_far)
    carried_list = [conjugate_times(far_slab, back_far).astype(jnp.bfloat16)]
    member = 0
    entering = incident(freqs[member], row_pos, col_pos, length)
    back_near = correlate_columns(along_rows(carried_list[member], adjoint_band), adjoint_kernel)
    grad_near = conjugate_times(entering, back_near)
    near_total, far_total = (
        lax.psum_scatter(
            grad_near.astype(jnp.bfloat16), "ang", scatter_dimension=2, tiled=True
        ).astype(jnp.float32),
        lax.psum_scatter(
            grad_far.astype(jnp.bfloat16), "ang", scatter_dimension=2, tiled=True
        ).astype(jnp.float32),
    )
    return (near_total, far_total)


def pick(measured, slices, kernel_taps, angle_freq, chosen):
    rows, cols = slices.shape[1], slices.shape[3]
    taps = kernel_taps.shape[1]
    fits = (
        lax.axis_size("ang") == 2
        and lax.axis_size("rows") % 2 == 0
        and 2 * (taps - 1) == LANES
        and rows >= taps - 1
        and rows % LANES == 0
        and cols % (2 * LANES) == 0
    )
    run = columns_local if fits else local
    return run(measured, slices, kernel_taps, angle_freq, chosen)


def solution(mesh):
    return jax.shard_map(
        pick,
        mesh=mesh,
        in_specs=(P("ang", "rows", None, None), P(None, "rows", None, "ang"), P(), P(), P("ang")),
        out_specs=(P("rows", None, "ang"), P("rows", None, "ang")),
        check_vma=False,
    )
```

```python
import functools
import math

import jax
import jax.numpy as jnp
from jax import lax
from jax.experimental import pallas as pl
from jax.experimental.pallas import tpu as pltpu
from jax.sharding import PartitionSpec as P

LANES = 128
BF16 = jnp.bfloat16
STRIP_FLOPS = 1 * 10**9
INNER_FLOPS = 0
MATS_FLOPS = 0
OWN_FLOPS = 1 * 10**9
F32 = jnp.float32


def dot(left, right):
    return jnp.dot(left, right, preferred_element_type=F32)


def iota(shape, dim):
    return lax.broadcasted_iota(jnp.int32, shape, dim)


def lane_chunks(width, step=2 * LANES):
    return [(at, min(step, width - at)) for at in range(0, width, step)]


def edges_kernel(half, slices, angle_freq, chosen, outer, inner, across, strips, table, sems):
    rows, cols = slices.shape[1], slices.shape[3]
    parity = lax.axis_index("rows") % 2
    side = lax.axis_index("ang")
    lane = pl.multiple_of((1 - side) * (cols - LANES), LANES)
    copies = [(angle_freq, table), (slices.at[:, :, :, pl.ds(lane, LANES)], strips)]
    for late, out in ((parity, outer), (1 - parity, inner)):
        for slab, at, size in ((0, 0, 2 * half), (1, 2 * half, half)):
            copies.append((slices.at[slab, pl.ds(late * (rows - size), size)], out.at[pl.ds(at, size)]))
    copies = [pltpu.make_async_copy(frm, to, sems.at[i]) for i, (frm, to) in enumerate(copies)]
    for copy in copies:
        copy.start()
    for copy in copies[:2]:
        copy.wait()
    for slab in range(2):
        across[slab * 2 * rows : (slab + 1) * 2 * rows] = strips[slab].reshape(2 * rows, LANES)
    row = iota((16, LANES), 0)
    block = jnp.zeros((16, LANES), F32)
    entry = jnp.where(iota(table.shape, 1) == chosen[0], table[...], 0.0)
    freqs = jnp.sum(entry, axis=1, keepdims=True)
    for part in range(2):
        rest = jnp.broadcast_to(freqs[part : part + 1], (16, LANES))
        for piece in range(3):
            rounded = rest.astype(BF16).astype(F32)
            block = jnp.where(row == 3 * part + piece, rounded, block)
            rest = rest - rounded
    across[4 * rows :] = block.astype(BF16)
    for copy in copies[2:]:
        copy.wait()


def sent_frequencies(across):
    sent = across[across.shape[0] - 16 :].astype(F32)
    return [(sent[i : i + 1] + sent[i + 1 : i + 2] + sent[i + 2 : i + 3])[:, :1] for i in (0, 3)]


def strip_kernel(half, across, row_half, strip, inner_strip):
    rows = (across.shape[0] - 16) // 4
    parity = lax.axis_index("rows") % 2
    for late, out in ((parity, strip), (1 - parity, inner_strip)):
        begin = 0
        for slab, size in ((0, 4 * half), (1, 2 * half)):
            frm = slab * 2 * rows + late * (2 * rows - size)
            out[begin : begin + size] = across[pl.ds(pl.multiple_of(frm, 16), size)]
            begin += size


def measured_kernel(measured, sent, outer, inner, sems):
    size, cols = outer.shape[0], measured.shape[3] // 2
    parity = lax.axis_index("rows") % 2
    side = lax.axis_index("ang")
    copies = []
    for late, out in ((parity, outer), (1 - parity, inner)):
        for frm, at, lanes in (((1 - side) * cols, 0, cols), (cols - (1 - side) * LANES, cols, LANES)):
            here = pl.ds(pl.multiple_of(frm, LANES), lanes)
            there = measured.at[0, pl.ds(late * size, size), :, here]
            copies.append(pltpu.make_async_copy(there, out.at[:, :, at : at + lanes], sems.at[len(copies)]))
    for copy in copies:
        copy.start()
    for copy in copies:
        copy.wait()


def own_window(measured, late, at, size):
    half_rows, cols = measured.shape[1] // 2, measured.shape[3] // 2
    rows = pl.ds(late * half_rows, half_rows)
    first, second = (at, cols + at) if at < cols else (cols, cols - LANES)
    left = measured[0, rows, :, first : first + size].reshape(2 * half_rows, size)
    right = measured[0, rows, :, second : second + size].reshape(2 * half_rows, size)
    return jnp.where(lax.axis_index("ang") == 0, left, right)


def got_window(window, at, size):
    return window[:, :, at : at + size].reshape(2 * window.shape[0], size)


def skewed(base, count, stride):
    width = base.shape[1]
    return pltpu.roll(jnp.broadcast_to(base, (count, width)), 0, 1, stride=stride, stride_axis=0)


def matrices_kernel(rows, taps, row_real, row_imag, row_half, row_half_adj, row_adj, col_taps, split_far, split_meas):
    count = taps.shape[1]
    half = (count - 1) // 2
    wide = rows + 4 * half
    mid = rows + 2 * half
    table = jnp.concatenate(
        [jnp.concatenate([taps[...], jnp.zeros((2, LANES - count), BF16)], axis=1),
         jnp.zeros((14, LANES), BF16)], axis=0,
    )

    def spread(width, place):
        tap = iota((LANES, width), 0)
        lane = iota((LANES, width), 1)
        hit = jnp.logical_and(lane == place(tap), tap < count)
        return dot(table, jnp.where(hit, 1.0, 0.0).astype(BF16))

    even = spread(2 * wide, lambda tap: 2 * tap)
    odd = spread(2 * wide, lambda tap: 2 * tap + 1)
    row_real[...] = skewed(even[0:1] - odd[1:2], mid, 2)
    row_imag[...] = skewed(even[1:2] + odd[0:1], mid, 2)

    low = spread(2 * mid, lambda tap: tap)
    high = spread(2 * mid, lambda tap: mid + tap)
    full = jnp.concatenate(
        [skewed(low[0:1] - high[1:2], rows, 1), skewed(low[1:2] + high[0:1], rows, 1)], axis=0
    )
    row_adj[...] = full.T.astype(BF16)
    low = spread(2 * rows, lambda tap: tap)
    high = spread(2 * rows, lambda tap: rows + tap)
    full = jnp.concatenate(
        [skewed(low[0:1] - high[1:2], rows // 2, 1), skewed(low[1:2] + high[0:1], rows // 2, 1)], axis=0
    )
    row_half[...] = full.astype(BF16)
    row_half_adj[...] = full.T.astype(BF16)

    window = 2 * LANES
    source = iota((window, LANES), 0)
    target = iota((window, LANES), 1)
    same_side = (source < LANES) == (target < LANES - half)
    left_only = source < window - half
    right_only = source >= LANES - half
    everything = source >= 0
    at = 0
    for adjoint in (False, True):
        for offset, masks in ((0, (everything, same_side)), (2 * half, (everything, left_only, right_only))):
            if adjoint:
                base = spread(window, lambda tap: (window - offset - (count - 1) + tap) % window)
            else:
                base = spread(window, lambda tap: (window - offset - tap) % window)
            re = skewed(base[0:1], window, 1)[:, :LANES]
            im = skewed(base[1:2], window, 1)[:, :LANES]
            im = -im if adjoint else im
            for mask in masks:
                mre = jnp.where(mask, re, 0.0).astype(BF16)
                mim = jnp.where(mask, im, 0.0).astype(BF16)
                col_taps[at, :window, :LANES] = mre
                col_taps[at, :window, LANES:] = mim
                col_taps[at, window:, :LANES] = -mim
                col_taps[at, window:, LANES:] = mre
                at += 1

    for out in (split_far, split_meas):
        size = out.shape[0]
        to, frm = iota((size, size), 0), iota((size, size), 1)
        out[...] = jnp.where(frm == 2 * (to % (size // 2)) + to // (size // 2), 1.0, 0.0).astype(BF16)


def phases_kernel(half, length, row_real, row_imag, across, across_got, row_near, row_near_adj, row_edge, waves):
    mid, wide = row_real.shape[0], row_real.shape[1] // 2
    rows, cols = mid - 2 * half, waves.shape[1] - LANES
    side = lax.axis_index("ang")
    freqs = list(zip(sent_frequencies(across), sent_frequencies(across_got)))
    scale = 2.0 * math.pi / length
    lane = iota((1, cols + LANES), 1)
    col = jnp.where(side == 0, lane, jnp.where(lane < cols, lane + cols, lane - LANES)).astype(F32)
    start = lax.axis_index("rows") * rows - 2 * half
    row = (start + iota((1, 2 * wide), 1) // 2).astype(F32)
    for member in range(2):
        phase = scale * (freqs[1][member] * col)
        waves[2 * member : 2 * member + 1] = jnp.cos(phase)
        waves[2 * member + 1 : 2 * member + 2] = jnp.sin(phase)
        phase = scale * (freqs[0][member] * row)
        cos, sin = jnp.cos(phase), jnp.sin(phase)
        re = row_real[...] * cos - row_imag[...] * sin
        im = row_imag[...] * cos + row_real[...] * sin
        full = jnp.concatenate([re, im], axis=0)
        at = member * 2 * mid
        row_near[at : at + 2 * mid] = full.astype(BF16)
        row_near_adj[:, at : at + 2 * mid] = full.T.astype(BF16)
        for part in range(2):
            low, high = 4 * half, 2 * wide - 4 * half
            near = full[part * mid : part * mid + 2 * half, :low]
            far = full[part * mid + mid - 2 * half : (part + 1) * mid, high:]
            edge = jnp.where(lax.axis_index("rows") % 2 == 0, near, far)
            row_edge[(2 * member + part) * 2 * half : (2 * member + part + 1) * 2 * half] = edge.astype(BF16)


class Tiles:
    def __init__(self, cols):
        self.count = cols // LANES + 1
        self.width = self.count * LANES
        self.cut = self.count - 1 - lax.axis_index("ang")
        self.after = lax.rem(self.cut + 1, self.count)

    def ahead(self, j, base):
        return base + jnp.where(j == self.cut, 1, 0) if j >= self.count - 2 else base

    def back(self, j, base):
        if 0 < j < self.count - 2:
            return base
        return base + jnp.where(j == self.cut, 1, jnp.where(j == self.after, 2, 0))


def tile(j):
    return slice(j * LANES, (j + 1) * LANES)


def pair(j):
    return slice(j * LANES, (j + 2) * LANES)


class Rows:
    def __init__(self, first, count, parts):
        self.first, self.count, self.parts = first, count, parts

    def at(self, part, top=0):
        first = top + part * self.parts + self.first
        return pl.ds(first if isinstance(first, int) else pl.multiple_of(first, 16), self.count)

    def read(self, ref, lanes, top=0):
        return jnp.concatenate([ref[self.at(0, top), lanes], ref[self.at(1, top), lanes]], axis=0)

    def pairs(self, ref, j, top=0):
        return jnp.concatenate([ref[self.at(0, top), pair(j)], ref[self.at(1, top), pair(j)]], axis=1)

    def write(self, ref, lanes, both, top=0):
        ref[self.at(0, top), lanes] = both[: self.count]
        ref[self.at(1, top), lanes] = both[self.count :]


def column_step(tiles, index, col_taps, load, store, count, limit=512):
    groups, room = [], 0
    for j in range(count):
        which = index(j)
        plain = isinstance(which, int)
        if plain and groups and isinstance(groups[-1][0], int) and room > 0:
            groups[-1][1].append(j)
        else:
            groups.append((which, [j]))
            room = limit
        room -= load(j).shape[0] if plain else limit
    for which, members in groups:
        parts = [load(j) for j in members]
        size = parts[0].shape[0]
        y = dot(jnp.concatenate(parts, axis=0), col_taps[which])
        for at, j in enumerate(members):
            store(j, y[at * size : (at + 1) * size])


def forward_rows(
    tiles, part, leave, near_slab, far_slab, row_near, row_half, col_taps, waves, entry, field, after, narrow, leaving,
):
    mid, width = part.parts, tiles.width
    size = part.count
    for at, lanes in lane_chunks(width):
        here = slice(at, at + lanes)
        left = jnp.concatenate(
            [row_near[part.at(comp, member * 2 * mid), :] for member in range(2) for comp in range(2)], axis=0
        )
        result = dot(left, near_slab[:, here])
        for member in range(2):
            re = result[2 * member * size : (2 * member + 1) * size]
            im = result[(2 * member + 1) * size : (2 * member + 2) * size]
            vr, vi = waves[2 * member : 2 * member + 1, here], waves[2 * member + 1 : 2 * member + 2, here]
            entry[member, :size, here] = (re * vr - im * vi).astype(BF16)
            entry[member, size:, here] = (re * vi + im * vr).astype(BF16)
    entry[:, :, width:] = entry[:, :, :LANES]

    def load(j):
        return jnp.concatenate(
            [
                jnp.concatenate([entry[member, :size, pair(j)], entry[member, size:, pair(j)]], axis=1)
                for member in range(2)
            ],
            axis=0,
        )

    def store(j, y):
        y = y.astype(BF16)
        far = part.read(far_slab, tile(j))
        sr, si = far[:size], far[size:]
        for member in range(2):
            re, im = y[member * size : (member + 1) * size, :LANES], y[member * size : (member + 1) * size, LANES:]
            part.write(field.at[member], tile(j), jnp.concatenate([re, im], axis=0))
            re, im = re.astype(F32), im.astype(F32)
            both = jnp.concatenate([sr * re - si * im, sr * im + si * re], axis=0)
            part.write(after.at[member], tile(j), both.astype(BF16))

    column_step(tiles, lambda j: tiles.ahead(j, 0), col_taps, load, store, tiles.count)

    source = Rows(leave.first, 2 * leave.count, mid)
    for at, lanes in lane_chunks(width):
        here = slice(at, at + lanes)
        for member in range(2):
            y = dot(row_half[...], source.read(after.at[member], here)).astype(BF16)
            narrow[member, :, LANES + at : LANES + at + lanes] = y
    narrow[:, :, :LANES] = narrow[:, :, width:]
    size2 = leave.count

    def load2(j):
        return jnp.concatenate(
            [
                jnp.concatenate([narrow[member, :size2, pair(j)], narrow[member, size2:, pair(j)]], axis=1)
                for member in range(2)
            ],
            axis=0,
        )

    def store2(j, y):
        y = y.astype(BF16)
        for member in range(2):
            here = slice(member * size2, (member + 1) * size2)
            leaving[member, :size2, tile(j)] = y[here, :LANES]
            leaving[member, size2:, tile(j)] = y[here, LANES:]

    column_step(tiles, lambda j: tiles.back(j, 2), col_taps, load2, store2, tiles.count)


def residue_rows(tiles, members, windows, leave, split_meas, col_taps, leaving, residue, back):
    size = leave.count
    for member, window in zip(members, windows):
        for at, lanes in lane_chunks(tiles.width):
            here = slice(at, at + lanes)
            meas = dot(split_meas[...], window(at, lanes))
            residue[member, :, here] = (leaving[member, :, here].astype(F32) - meas).astype(BF16)
        residue[member, :, tiles.width :] = residue[member, :, :LANES]

    def load(j):
        return jnp.concatenate(
            [
                jnp.concatenate([residue[member, :size, pair(j)], residue[member, size:, pair(j)]], axis=1)
                for member in members
            ],
            axis=0,
        )

    def store(j, y):
        y = y.astype(BF16)
        for k, member in enumerate(members):
            here = slice(k * size, (k + 1) * size)
            leave.write(back.at[member], tile(j), jnp.concatenate([y[here, :LANES], y[here, LANES:]], axis=0))

    column_step(tiles, lambda j: tiles.ahead(j, 5), col_taps, load, store, tiles.count)


def backward_rows(tiles, members, part, left, right, field, far_slab, col_taps, waves, carry, far_sum, into):
    size, mid = part.count, part.parts
    for at, lanes in lane_chunks(tiles.width):
        here = slice(at, at + lanes)
        there = slice(LANES + at, LANES + at + lanes)
        far = part.read(far_slab, here)
        sr, si = far[:size], far[size:]
        total = None
        for member in members:
            y = dot(left, right(member, here))
            br, bi = y[:size], y[size:]
            inner = part.read(field.at[member], here).astype(F32)
            ir, ii = inner[:size], inner[size:]
            carry[member, :size, there] = (sr * br + si * bi).astype(BF16)
            carry[member, size:, there] = (sr * bi - si * br).astype(BF16)
            term = jnp.concatenate([ir * br + ii * bi, ir * bi - ii * br], axis=0)
            total = term if total is None else total + term
        part.write(far_sum, there, total)
    for member in members:
        carry[member, :, :LANES] = carry[member, :, tiles.width :]

    def load(j):
        return jnp.concatenate(
            [
                jnp.concatenate([carry[member, :size, pair(j)], carry[member, size:, pair(j)]], axis=1)
                for member in members
            ],
            axis=0,
        )

    def store(j, y):
        for k, member in enumerate(members):
            re, im = y[k * size : (k + 1) * size, :LANES], y[k * size : (k + 1) * size, LANES:]
            vr, vi = waves[2 * member : 2 * member + 1, tile(j)], waves[2 * member + 1 : 2 * member + 2, tile(j)]
            both = jnp.concatenate([re * vr + im * vi, im * vr - re * vi], axis=0)
            part.write(into, tile(j), both.astype(BF16), member * 2 * mid)

    column_step(tiles, lambda j: tiles.back(j, 7), col_taps, load, store, tiles.count - 1)


def split_rows(tiles, part, split_far, far_raw, far_slab, half):
    left = jnp.concatenate([split_far[part.at(0), :], split_far[part.at(1), :]], axis=0)
    for j in range(tiles.count):
        part.write(far_slab, tile(j), dot(left, far_raw[:, pair(j)])[:, half : half + LANES])


def far_margin(tiles, half, part, far_sum, sums):
    for j in range(tiles.count - 1):
        y = part.read(far_sum, pair(j))[:, LANES - half : 2 * LANES - half]
        sums[:, tile(j)] = y.astype(BF16)


def outer_kernel(
    half,
    slices, outer, inner, across, corner, across_inner, measured, measured_got,
    row_near, row_half, row_half_adj, row_edge, col_taps, split_far, split_meas, waves,
    near_slab, far_raw, far_slab, field, after, back, far_sum, into, sums,
    entry, narrow, leaving, residue, carry,
):
    rows, cols = slices.shape[1], slices.shape[3]
    tiles = Tiles(cols)
    width = tiles.width
    mid = rows + 2 * half
    parity = lax.axis_index("rows") % 2

    for slab, ref, margin in ((0, near_slab, 4 * half), (1, far_raw, 2 * half)):
        ref[margin : margin + 2 * rows, :cols] = slices[slab].reshape(2 * rows, cols)
        ref[margin : margin + 2 * rows, cols:width] = across[slab * 2 * rows : (slab + 1) * 2 * rows]
        begin = 0 if slab == 0 else 4 * half
        outer_at = pl.ds(pl.multiple_of(parity * (2 * rows + margin), 16), margin)
        inner_at = pl.ds(pl.multiple_of((1 - parity) * (2 * rows + margin), 16), margin)
        ref[outer_at, :cols] = outer[begin // 2 : (begin + margin) // 2].reshape(margin, cols)
        ref[outer_at, cols:width] = corner[begin : begin + margin]
        ref[inner_at, :cols] = inner[begin // 2 : (begin + margin) // 2].reshape(margin, cols)
        ref[inner_at, cols:width] = across_inner[begin : begin + margin]
    far_raw[:, width:] = far_raw[:, :LANES]

    part = Rows(parity * (rows // 2), rows, mid)
    source = Rows(parity * (rows // 2), rows // 2, mid)
    leave = Rows(parity * (rows // 2), rows // 2, rows)
    edge = Rows(parity * rows, 2 * half, mid)
    pick = Rows(parity * 2 * half, 2 * half, rows)
    split_rows(tiles, part, split_far, far_raw, far_slab, half)
    forward_rows(
        tiles, part, source, near_slab, far_slab, row_near, row_half, col_taps, waves, entry, field, after, narrow,
        leaving,
    )
    windows = (functools.partial(own_window, measured, parity), functools.partial(got_window, measured_got))
    residue_rows(tiles, (0, 1), windows, leave, split_meas, col_taps, leaving, residue, back)
    backward_rows(
        tiles, (0, 1), edge, pick.read(row_half_adj, slice(None)), lambda one, here: leave.read(back.at[one], here),
        field, far_slab, col_taps, waves, carry, far_sum, into,
    )
    far_sum[:, :LANES] = far_sum[:, width:]
    left = row_edge[...].T
    for at, size in lane_chunks(cols):
        here = slice(at, at + size)
        right = jnp.concatenate([edge.read(into, here, member * 2 * mid) for member in range(2)], axis=0)
        sums[: 4 * half, here] = dot(left, right).astype(BF16)
    far_margin(tiles, half, Rows(parity * (rows + half), half, mid), far_sum, sums.at[4 * half :])


def inner_kernel(
    half,
    near_slab, far_raw, measured, measured_got, far_slab_in, field_in, after_in, back_in, far_in, into_in,
    row_near, row_half, row_adj, row_near_adj, col_taps, split_far, split_meas, waves,
    far_slab, field, after, back, far_sum, into, sums, far_sums,
    entry, narrow, leaving, residue, carry,
):
    cols = into.shape[1]
    tiles = Tiles(cols)
    mid = far_sum.shape[0] // 2
    rows = mid - 2 * half
    other = 1 - lax.axis_index("rows") % 2
    part = Rows(other * rows, 2 * half, mid)
    source = Rows(other * (rows // 2), rows // 2, mid)
    leave = Rows(other * (rows // 2), rows // 2, rows)
    split_rows(tiles, part, split_far, far_raw, far_slab, half)
    forward_rows(
        tiles, part, source, near_slab, far_slab, row_near, row_half, col_taps, waves, entry, field, after, narrow,
        leaving,
    )
    windows = (functools.partial(own_window, measured, other), functools.partial(got_window, measured_got))
    residue_rows(tiles, (0, 1), windows, leave, split_meas, col_taps, leaving, residue, back)
    rest = Rows(other * 2 * half, rows, mid)
    left = jnp.concatenate([row_adj[rest.at(0), :], row_adj[rest.at(1), :]], axis=0)
    backward_rows(
        tiles, (0, 1), rest, left, lambda one, here: back[one, :, here], field, far_slab, col_taps, waves, carry,
        far_sum, into,
    )
    far_sum[:, :LANES] = far_sum[:, tiles.width :]
    at = pl.ds(pl.multiple_of(other * 2 * (rows + 2 * half), 16), 4 * half)
    for first, size in lane_chunks(cols):
        here = slice(first, first + size)
        sums[:, here] = dot(row_near_adj[at, :], into[:, here]).astype(BF16)
    far_margin(tiles, half, Rows(other * (rows + half), half, mid), far_sum, far_sums)


def sums_kernel(
    half, into, far_sum, row_near_adj, inner, inner_far, near, far, near_edge, far_edge, near_total, far_total, sems
):
    cols = into.shape[1]
    mid = far_sum.shape[0] // 2
    rows = mid - 2 * half
    parity = lax.axis_index("rows") % 2
    margin = 4 * half
    for j in range(cols // LANES):
        for comp in range(2):
            top = comp * mid + half
            far_total[:, comp, tile(j)] = far_sum[top : top + rows, pair(j)][:, LANES - half : 2 * LANES - half]
    at = pl.ds((1 - parity) * (rows - half), half)
    for comp in range(2):
        far_total[at, comp, :] += inner_far[comp * half : (comp + 1) * half].astype(F32)
    far_edge[...] = far_total[pl.ds(parity * (rows - half), half)]
    rest = pl.ds((1 - parity) * half, rows - half)
    far_copy = pltpu.make_async_copy(far_total.at[rest], far.at[rest], sems.at[0])
    far_copy.start()
    for at, size in lane_chunks(cols):
        here = slice(at, at + size)
        y = dot(row_near_adj[margin : margin + 2 * rows], into[:, here])
        near_total[:, :, here] = y.reshape(rows, 2, size)
    at = pl.ds((1 - parity) * (rows - 2 * half), 2 * half)
    near_total[at] += inner[...].astype(F32).reshape(2 * half, 2, cols)
    near_edge[...] = near_total[pl.ds(parity * (rows - 2 * half), 2 * half)]
    rest = pl.ds((1 - parity) * 2 * half, rows - 2 * half)
    near_copy = pltpu.make_async_copy(near_total.at[rest], near.at[rest], sems.at[1])
    near_copy.start()
    far_copy.wait()
    near_copy.wait()


def finish_kernel(half, near_in, far_in, near_edge, far_edge, outer, near, far, near_total, far_total, sems):
    rows, cols = near.shape[0], near.shape[2]
    parity = lax.axis_index("rows") % 2
    margin = 4 * half
    near_total[...] = near_edge[...] + outer[:margin].astype(F32).reshape(2 * half, 2, cols)
    at = pl.ds(parity * (rows - 2 * half), 2 * half)
    near_copy = pltpu.make_async_copy(near_total, near.at[at], sems.at[0])
    near_copy.start()
    for comp in range(2):
        got = outer[margin + comp * half : margin + (comp + 1) * half].astype(F32)
        far_total[:, comp, :] = far_edge[:, comp, :] + got
    at = pl.ds(parity * (rows - half), half)
    far_copy = pltpu.make_async_copy(far_total, far.at[at], sems.at[1])
    far_copy.start()
    near_copy.wait()
    far_copy.wait()


def call(kernel, outs, operands, hbm=(), scalars=(), outside=(), outs_outside=(), scratch=(), aliases=None, flops=0):
    def place(i):
        if i in scalars:
            return pltpu.SMEM
        return pltpu.HBM if i in hbm else pl.ANY if i in outside else pltpu.VMEM

    return pl.pallas_call(
        kernel,
        out_shape=[jax.ShapeDtypeStruct(shape, dtype) for shape, dtype in outs],
        in_specs=[pl.BlockSpec(memory_space=place(i)) for i in range(len(operands))],
        out_specs=[
            pl.BlockSpec(memory_space=pl.ANY if i in outs_outside else pltpu.VMEM) for i in range(len(outs))
        ],
        scratch_shapes=[one if not isinstance(one, tuple) else pltpu.VMEM(*one) for one in scratch],
        input_output_aliases=aliases or {},
        compiler_params=pltpu.CompilerParams(vmem_limit_bytes=20 * 2**20),
        cost_estimate=pl.CostEstimate(flops=flops, bytes_accessed=0, transcendentals=0),
    )(*(pltpu.with_memory_space_constraint(x, pltpu.HBM) if i in hbm else x for i, x in enumerate(operands)))


def columns_local(measured, slices, kernel_taps, angle_freq, chosen):
    rows, cols = slices.shape[1], slices.shape[3]
    length = measured.shape[3]
    half = (kernel_taps.shape[1] - 1) // 2
    wide, mid, width = rows + 4 * half, rows + 2 * half, cols + LANES
    count = lax.axis_size("rows")
    outer_pairs = [(i, j) for i in range(count) if 0 <= (j := i - 1 + 2 * (i % 2)) < count]
    inner_pairs = [(i, i + 1 - 2 * (i % 2)) for i in range(count)]
    side_pairs = [(i, 1 - i) for i in range(lax.axis_size("ang"))]
    edge = 6 * half
    outer, inner, across = call(
        functools.partial(edges_kernel, half),
        [((3 * half, 2, cols), BF16), ((3 * half, 2, cols), BF16), ((4 * rows + 16, LANES), BF16)],
        (slices, angle_freq.T, chosen), hbm=(0, 1), scalars=(2,), outs_outside=(0, 1),
        scratch=[((2, rows, 2, LANES), BF16), (angle_freq.shape[::-1], F32), pltpu.SemaphoreType.DMA((6,))],
    )
    outer_got = lax.ppermute(outer, "rows", outer_pairs)
    across_got = lax.ppermute(across, "ang", side_pairs)
    inner_got = lax.ppermute(inner, "rows", inner_pairs)
    meas_outer, meas_inner = call(
        measured_kernel, [((rows // 2, 2, width), BF16)] * 2, (measured, across), hbm=(0,), outside=(1,),
        outs_outside=(0, 1), scratch=[pltpu.SemaphoreType.DMA((4,))],
    )
    outer_meas = lax.ppermute(meas_outer, "ang", side_pairs)
    inner_meas = lax.ppermute(meas_inner, "ang", side_pairs)
    row_real, row_imag, row_half, row_half_adj, row_adj, col_taps, split_far, split_meas = call(
        functools.partial(matrices_kernel, rows),
        [
            ((mid, 2 * wide), F32), ((mid, 2 * wide), F32), ((rows, 2 * rows), BF16), ((2 * rows, rows), BF16),
            ((2 * mid, 2 * rows), BF16), ((10, 4 * LANES, 2 * LANES), BF16), ((2 * mid, 2 * mid), BF16),
            ((rows, rows), BF16),
        ],
        (kernel_taps,), flops=MATS_FLOPS,
    )
    strip, inner_strip = call(
        functools.partial(strip_kernel, half), [((edge, LANES), BF16)] * 2, (across_got, row_half), outside=(1,),
        flops=STRIP_FLOPS,
    )
    corner_got = lax.ppermute(strip, "rows", outer_pairs)
    across_inner = lax.ppermute(inner_strip, "rows", inner_pairs)
    row_near, row_near_adj, row_edge, waves = call(
        functools.partial(phases_kernel, half, length),
        [((4 * mid, 2 * wide), BF16), ((2 * wide, 4 * mid), BF16), ((8 * half, 4 * half), BF16), ((8, width), F32)],
        (row_real, row_imag, across, across_got),
    )
    state = [
        ((2 * mid, width), F32), ((2, 2 * mid, width), BF16), ((2, 2 * mid, width), BF16),
        ((2, 2 * rows, width), BF16), ((2 * mid, width + LANES), F32), ((4 * mid, cols), BF16),
    ]
    leaving_shape = ((2, rows, width), BF16)
    near_slab, far_raw, far_slab, field, after, back, far_sum, into, outer_sums = call(
        functools.partial(outer_kernel, half),
        [((2 * wide, width), BF16), ((2 * mid, width + LANES), BF16), *state, ((edge, cols), BF16)],
        (
            slices, outer_got, inner_got, across_got, corner_got, across_inner, measured, outer_meas,
            row_near, row_half, row_half_adj, row_edge, col_taps, split_far, split_meas, waves,
        ),
        scratch=[
            ((2, 2 * rows, width + LANES), BF16), ((2, rows, width + LANES), BF16), leaving_shape,
            ((2, rows, width + LANES), BF16), ((2, 4 * half, width + LANES), BF16),
        ],
        flops=OWN_FLOPS,
    )
    outer_back = lax.ppermute(outer_sums, "rows", outer_pairs)
    far_slab, field, after, back, far_sum, into, inner_sums, inner_far = call(
        functools.partial(inner_kernel, half),
        [*state, ((4 * half, cols), BF16), ((2 * half, cols), BF16)],
        (
            near_slab, far_raw, measured, inner_meas, far_slab, field, after, back, far_sum, into,
            row_near, row_half, row_adj, row_near_adj, col_taps, split_far, split_meas, waves,
        ),
        aliases={4: 0, 5: 1, 6: 2, 7: 3, 8: 4, 9: 5},
        scratch=[
            ((2, 4 * half, width + LANES), BF16), ((2, rows, width + LANES), BF16), leaving_shape,
            ((2, rows, width + LANES), BF16), ((2, 2 * rows, width + LANES), BF16),
        ],
        flops=INNER_FLOPS,
    )
    inner_back = lax.ppermute(inner_sums, "rows", inner_pairs)
    inner_far_back = lax.ppermute(inner_far, "rows", inner_pairs)
    near, far, near_edge, far_edge = call(
        functools.partial(sums_kernel, half),
        [
            ((rows, 2, cols), F32), ((rows, 2, cols), F32), ((2 * half, 2, cols), F32), ((half, 2, cols), F32),
        ],
        (into, far_sum, row_near_adj, inner_back, inner_far_back), outs_outside=(0, 1),
        scratch=[((rows, 2, cols), F32), ((rows, 2, cols), F32), pltpu.SemaphoreType.DMA((2,))],
    )
    near, far = call(
        functools.partial(finish_kernel, half),
        [((rows, 2, cols), F32)] * 2,
        (near, far, near_edge, far_edge, outer_back), outside=(0, 1), outs_outside=(0, 1), aliases={0: 0, 1: 1},
        scratch=[((2 * half, 2, cols), F32), ((half, 2, cols), F32), pltpu.SemaphoreType.DMA((2,))],
    )
    return near, far


def with_halo(block, sides, width):
    for axis, dim in sides:
        count = lax.axis_size(axis)
        forward = [(i, i + 1) for i in range(count - 1)]
        backward = [(target, source) for source, target in forward]
        low = lax.ppermute(
            lax.slice_in_dim(block, block.shape[dim] - width, None, axis=dim), axis, forward
        )
        high = lax.ppermute(lax.slice_in_dim(block, 0, width, axis=dim), axis, backward)
        block = jnp.concatenate([low, block, high], axis=dim)
    return block


def toeplitz(row_taps, out_width):
    tap_count = row_taps.shape[0]
    window = out_width + tap_count - 1
    padded = jnp.concatenate([row_taps, jnp.zeros((out_width,), row_taps.dtype)])
    tiled = jnp.tile(padded, out_width)[: out_width * window]
    return tiled.reshape(out_width, window).T


def kernel_pair(kernel_taps, out_width):
    return jnp.concatenate(
        [toeplitz(kernel_taps[0], out_width), toeplitz(kernel_taps[1], out_width)], axis=1
    )


def adjoint_taps(kernel_taps):
    return jnp.stack([kernel_taps[0][::-1], -kernel_taps[1][::-1]])


def correlate_columns(field, kernel):
    window, doubled = kernel.shape
    tile_len = doubled // 2
    half_taps = (window - tile_len) // 2
    leading, comps, length = field.shape
    blocks = length // tile_len
    padded = jnp.pad(field, ((0, 0), (0, 0), (half_taps, tile_len - half_taps)))
    main_part = padded[:, :, :length].reshape(leading, comps, blocks, tile_len)
    tail_part = padded[:, :, tile_len : tile_len + length].reshape(
        leading, comps, blocks, tile_len
    )[..., : 2 * half_taps]
    windows = jnp.concatenate([main_part, tail_part], axis=3)
    product = jnp.einsum("rpnw,wk->rpnk", windows, kernel, preferred_element_type=jnp.float32)
    real_part = product[:, 0, :, :tile_len] - product[:, 1, :, tile_len:]
    imag_part = product[:, 0, :, tile_len:] + product[:, 1, :, :tile_len]
    return (
        jnp.stack([real_part, imag_part], axis=1)
        .reshape(leading, comps, length)
        .astype(jnp.bfloat16)
    )


def band_rows(padded, band):
    out_rows = band.shape[1] // 2
    product = jnp.einsum("jpc,jk->kpc", padded, band, preferred_element_type=jnp.float32)
    real_part = product[:out_rows, 0] - product[out_rows:, 1]
    imag_part = product[out_rows:, 0] + product[:out_rows, 1]
    return jnp.stack([real_part, imag_part], axis=1).astype(jnp.bfloat16)


def complex_times(left, right):
    left = left.astype(jnp.float32)
    right = right.astype(jnp.float32)
    real_part = left[:, 0] * right[:, 0] - left[:, 1] * right[:, 1]
    imag_part = left[:, 0] * right[:, 1] + left[:, 1] * right[:, 0]
    return jnp.stack([real_part, imag_part], axis=1)


def conjugate_times(left, right):
    left = left.astype(jnp.float32)
    right = right.astype(jnp.float32)
    real_part = left[:, 0] * right[:, 0] + left[:, 1] * right[:, 1]
    imag_part = left[:, 0] * right[:, 1] - left[:, 1] * right[:, 0]
    return jnp.stack([real_part, imag_part], axis=1)


def incident(freq, row_pos, col_pos, length):
    scale = 2.0 * math.pi / length
    phase = scale * (freq[0] * row_pos[:, None] + freq[1] * col_pos[None, :])
    return jnp.stack([jnp.cos(phase), jnp.sin(phase)], axis=1)


def local(measured, slices, kernel_taps, angle_freq, chosen):
    rows_dev = measured.shape[1]
    length = measured.shape[3]
    half_taps = (kernel_taps.shape[1] - 1) // 2
    backward_taps = adjoint_taps(kernel_taps)
    forward_kernel = kernel_pair(kernel_taps, 128)
    adjoint_kernel = kernel_pair(backward_taps, 128)
    forward_band = kernel_pair(kernel_taps, rows_dev)
    adjoint_band = kernel_pair(backward_taps, rows_dev)
    gathered = lax.all_gather(slices, "ang", axis=3, tiled=True)
    near_slab = gathered[0]
    far_slab = gathered[1]
    start = lax.axis_index("rows") * rows_dev
    row_pos = (start + jnp.arange(rows_dev, dtype=jnp.int32)).astype(jnp.float32)
    col_pos = jnp.arange(length).astype(jnp.float32)
    onehot = (chosen[:, None] == jnp.arange(angle_freq.shape[0], dtype=jnp.int32)[None, :]).astype(
        jnp.float32
    )
    freqs = jnp.dot(onehot, angle_freq, precision=lax.Precision.HIGHEST)

    def along_rows(field, band):
        padded = with_halo(field, (("rows", 0),), half_taps)
        result = band_rows(padded, band)
        return result

    member = 0
    entering = incident(freqs[member], row_pos, col_pos, length)
    entry0 = complex_times(near_slab, entering).astype(jnp.bfloat16)
    inner = along_rows(correlate_columns(entry0, forward_kernel), forward_band)
    entry1 = complex_times(far_slab, inner).astype(jnp.bfloat16)
    exit_field = along_rows(correlate_columns(entry1, forward_kernel), forward_band)
    residue = (exit_field.astype(jnp.float32) - measured[member].astype(jnp.float32)).astype(
        jnp.bfloat16
    )
    back_far = correlate_columns(along_rows(residue, adjoint_band), adjoint_kernel)
    grad_far = conjugate_times(inner, back_far)
    carried_list = [conjugate_times(far_slab, back_far).astype(jnp.bfloat16)]
    member = 0
    entering = incident(freqs[member], row_pos, col_pos, length)
    back_near = correlate_columns(along_rows(carried_list[member], adjoint_band), adjoint_kernel)
    grad_near = conjugate_times(entering, back_near)
    near_total, far_total = (
        lax.psum_scatter(
            grad_near.astype(jnp.bfloat16), "ang", scatter_dimension=2, tiled=True
        ).astype(jnp.float32),
        lax.psum_scatter(
            grad_far.astype(jnp.bfloat16), "ang", scatter_dimension=2, tiled=True
        ).astype(jnp.float32),
    )
    return (near_total, far_total)


def pick(measured, slices, kernel_taps, angle_freq, chosen):
    rows, cols = slices.shape[1], slices.shape[3]
    taps = kernel_taps.shape[1]
    fits = (
        lax.axis_size("ang") == 2
        and lax.axis_size("rows") % 2 == 0
        and 2 * (taps - 1) == LANES
        and rows >= taps - 1
        and rows % LANES == 0
        and cols % (2 * LANES) == 0
    )
    run = columns_local if fits else local
    return run(measured, slices, kernel_taps, angle_freq, chosen)


def solution(mesh):
    return jax.shard_map(
        pick,
        mesh=mesh,
        in_specs=(P("ang", "rows", None, None), P(None, "rows", None, "ang"), P(), P(), P("ang")),
        out_specs=(P("rows", None, "ang"), P("rows", None, "ang")),
        check_vma=False,
    )
```

```python
import functools
import math

import jax
import jax.numpy as jnp
from jax import lax
from jax.experimental import pallas as pl
from jax.experimental.pallas import tpu as pltpu
from jax.sharding import PartitionSpec as P

LANES = 128
BF16 = jnp.bfloat16
STRIP_FLOPS = 17 * 10**8
INNER_FLOPS = 0
MATS_FLOPS = 0
OWN_FLOPS = 5 * 10**9
F32 = jnp.float32


def dot(left, right):
    return jnp.dot(left, right, preferred_element_type=F32)


def iota(shape, dim):
    return lax.broadcasted_iota(jnp.int32, shape, dim)


def lane_chunks(width, step=2 * LANES):
    return [(at, min(step, width - at)) for at in range(0, width, step)]


def edges_kernel(half, slices, angle_freq, chosen, outer, across, strips, table, sems):
    rows, cols = slices.shape[1], slices.shape[3]
    parity = lax.axis_index("rows") % 2
    side = lax.axis_index("ang")
    lane = pl.multiple_of((1 - side) * (cols - LANES), LANES)
    copies = [(angle_freq, table), (slices.at[:, :, :, pl.ds(lane, LANES)], strips)]
    for slab, at, size in ((0, 0, 2 * half), (1, 2 * half, half)):
        copies.append((slices.at[slab, pl.ds(parity * (rows - size), size)], outer.at[pl.ds(at, size)]))
    copies = [pltpu.make_async_copy(frm, to, sems.at[i]) for i, (frm, to) in enumerate(copies)]
    for copy in copies:
        copy.start()
    for copy in copies[:2]:
        copy.wait()
    for slab in range(2):
        across[slab * 2 * rows : (slab + 1) * 2 * rows] = strips[slab].reshape(2 * rows, LANES)
    row = iota((16, LANES), 0)
    block = jnp.zeros((16, LANES), F32)
    entry = jnp.where(iota(table.shape, 1) == chosen[0], table[...], 0.0)
    freqs = jnp.sum(entry, axis=1, keepdims=True)
    for part in range(2):
        rest = jnp.broadcast_to(freqs[part : part + 1], (16, LANES))
        for piece in range(3):
            rounded = rest.astype(BF16).astype(F32)
            block = jnp.where(row == 3 * part + piece, rounded, block)
            rest = rest - rounded
    across[4 * rows :] = block.astype(BF16)
    for copy in copies[2:]:
        copy.wait()


def sent_frequencies(across):
    sent = across[across.shape[0] - 16 :].astype(F32)
    return [(sent[i : i + 1] + sent[i + 1 : i + 2] + sent[i + 2 : i + 3])[:, :1] for i in (0, 3)]


def strip_kernel(half, across, row_half, strip):
    rows = (across.shape[0] - 16) // 4
    parity = lax.axis_index("rows") % 2
    begin = 0
    for slab, size in ((0, 4 * half), (1, 2 * half)):
        frm = slab * 2 * rows + parity * (2 * rows - size)
        strip[begin : begin + size] = across[pl.ds(pl.multiple_of(frm, 16), size)]
        begin += size


def inner_edge_kernel(half, slices, across, strip, edge):
    rows, cols = slices.shape[1], slices.shape[3]
    other = 1 - lax.axis_index("rows") % 2
    begin = 0
    for slab, size in ((0, 2 * half), (1, half)):
        there = slice(begin, begin + 2 * size)
        edge[there, :cols] = slices[slab, pl.ds(other * (rows - size), size)].reshape(2 * size, cols)
        frm = slab * 2 * rows + other * 2 * (rows - size)
        edge[there, cols:] = across[pl.ds(pl.multiple_of(frm, 16), 2 * size)]
        begin += 2 * size


def measured_kernel(measured, sent, outer, inner, sems):
    size, cols = outer.shape[0], measured.shape[3] // 2
    parity = lax.axis_index("rows") % 2
    side = lax.axis_index("ang")
    copies = []
    for late, out in ((parity, outer), (1 - parity, inner)):
        for frm, at, lanes in (((1 - side) * cols, 0, cols), (cols - (1 - side) * LANES, cols, LANES)):
            here = pl.ds(pl.multiple_of(frm, LANES), lanes)
            there = measured.at[0, pl.ds(late * size, size), :, here]
            copies.append(pltpu.make_async_copy(there, out.at[:, :, at : at + lanes], sems.at[len(copies)]))
    for copy in copies:
        copy.start()
    for copy in copies:
        copy.wait()


def own_window(measured, late, at, size):
    half_rows, cols = measured.shape[1] // 2, measured.shape[3] // 2
    rows = pl.ds(late * half_rows, half_rows)
    first, second = (at, cols + at) if at < cols else (cols, cols - LANES)
    left = measured[0, rows, :, first : first + size].reshape(2 * half_rows, size)
    right = measured[0, rows, :, second : second + size].reshape(2 * half_rows, size)
    return jnp.where(lax.axis_index("ang") == 0, left, right)


def got_window(window, at, size):
    return window[:, :, at : at + size].reshape(2 * window.shape[0], size)


def skewed(base, count, stride):
    width = base.shape[1]
    return pltpu.roll(jnp.broadcast_to(base, (count, width)), 0, 1, stride=stride, stride_axis=0)


def matrices_kernel(
    rows, length, taps, across,
    row_real, row_imag, row_half, row_half_adj, row_adj, col_taps, split_far, split_meas,
    row_near, row_near_adj, row_edge, waves,
):
    count = taps.shape[1]
    half = (count - 1) // 2
    wide = rows + 4 * half
    mid = rows + 2 * half
    table = jnp.concatenate(
        [jnp.concatenate([taps[...], jnp.zeros((2, LANES - count), BF16)], axis=1),
         jnp.zeros((14, LANES), BF16)], axis=0,
    )

    def spread(width, place):
        tap = iota((LANES, width), 0)
        lane = iota((LANES, width), 1)
        hit = jnp.logical_and(lane == place(tap), tap < count)
        return dot(table, jnp.where(hit, 1.0, 0.0).astype(BF16))

    even = spread(2 * wide, lambda tap: 2 * tap)
    odd = spread(2 * wide, lambda tap: 2 * tap + 1)
    row_real[...] = skewed(even[0:1] - odd[1:2], mid, 2)
    row_imag[...] = skewed(even[1:2] + odd[0:1], mid, 2)

    add_phases(half, length, 0, across, row_real, row_imag, row_near, row_near_adj, row_edge, waves)

    low = spread(2 * mid, lambda tap: tap)
    high = spread(2 * mid, lambda tap: mid + tap)
    full = jnp.concatenate(
        [skewed(low[0:1] - high[1:2], rows, 1), skewed(low[1:2] + high[0:1], rows, 1)], axis=0
    )
    row_adj[...] = full.T.astype(BF16)
    low = spread(2 * rows, lambda tap: tap)
    high = spread(2 * rows, lambda tap: rows + tap)
    full = jnp.concatenate(
        [skewed(low[0:1] - high[1:2], rows // 2, 1), skewed(low[1:2] + high[0:1], rows // 2, 1)], axis=0
    )
    row_half[...] = full.astype(BF16)
    row_half_adj[...] = full.T.astype(BF16)

    window = 2 * LANES
    source = iota((window, LANES), 0)
    target = iota((window, LANES), 1)
    same_side = (source < LANES) == (target < LANES - half)
    left_only = source < window - half
    right_only = source >= LANES - half
    everything = source >= 0
    at = 0
    for adjoint in (False, True):
        for offset, masks in ((0, (everything, same_side)), (2 * half, (everything, left_only, right_only))):
            if adjoint:
                base = spread(window, lambda tap: (window - offset - (count - 1) + tap) % window)
            else:
                base = spread(window, lambda tap: (window - offset - tap) % window)
            re = skewed(base[0:1], window, 1)[:, :LANES]
            im = skewed(base[1:2], window, 1)[:, :LANES]
            im = -im if adjoint else im
            for mask in masks:
                mre = jnp.where(mask, re, 0.0).astype(BF16)
                mim = jnp.where(mask, im, 0.0).astype(BF16)
                col_taps[at, :window, :LANES] = mre
                col_taps[at, :window, LANES:] = mim
                col_taps[at, window:, :LANES] = -mim
                col_taps[at, window:, LANES:] = mre
                at += 1

    for out in (split_far, split_meas):
        size = out.shape[0]
        to, frm = iota((size, size), 0), iota((size, size), 1)
        out[...] = jnp.where(frm == 2 * (to % (size // 2)) + to // (size // 2), 1.0, 0.0).astype(BF16)


def add_phases(half, length, member, sent, row_real, row_imag, row_near, row_near_adj, row_edge, waves):
    mid, wide = row_real.shape[0], row_real.shape[1] // 2
    rows, cols = mid - 2 * half, waves.shape[1] - LANES
    side = lax.axis_index("ang")
    freq_row, freq_col = sent_frequencies(sent)
    scale = 2.0 * math.pi / length
    lane = iota((1, cols + LANES), 1)
    col = jnp.where(side == 0, lane, jnp.where(lane < cols, lane + cols, lane - LANES)).astype(F32)
    phase = scale * (freq_col * col)
    waves[2 * member : 2 * member + 1] = jnp.cos(phase)
    waves[2 * member + 1 : 2 * member + 2] = jnp.sin(phase)
    start = lax.axis_index("rows") * rows - 2 * half
    row = (start + iota((1, 2 * wide), 1) // 2).astype(F32)
    phase = scale * (freq_row * row)
    cos, sin = jnp.cos(phase), jnp.sin(phase)
    re = row_real[...] * cos - row_imag[...] * sin
    im = row_imag[...] * cos + row_real[...] * sin
    full = jnp.concatenate([re, im], axis=0)
    at = member * 2 * mid
    row_near[at : at + 2 * mid] = full.astype(BF16)
    row_near_adj[:, at : at + 2 * mid] = full.T.astype(BF16)
    for part in range(2):
        low, high = 4 * half, 2 * wide - 4 * half
        near = full[part * mid : part * mid + 2 * half, :low]
        far = full[part * mid + mid - 2 * half : (part + 1) * mid, high:]
        edge = jnp.where(lax.axis_index("rows") % 2 == 0, near, far)
        row_edge[(2 * member + part) * 2 * half : (2 * member + part + 1) * 2 * half] = edge.astype(BF16)


def phases_kernel(
    half, length, row_real, row_imag, across, near_in, near_adj_in, edge_in, waves_in,
    row_near, row_near_adj, row_edge, waves,
):
    add_phases(half, length, 1, across, row_real, row_imag, row_near, row_near_adj, row_edge, waves)


class Tiles:
    def __init__(self, cols):
        self.count = cols // LANES + 1
        self.width = self.count * LANES
        self.cut = self.count - 1 - lax.axis_index("ang")
        self.after = lax.rem(self.cut + 1, self.count)

    def ahead(self, j, base):
        return base + jnp.where(j == self.cut, 1, 0) if j >= self.count - 2 else base

    def back(self, j, base):
        if 0 < j < self.count - 2:
            return base
        return base + jnp.where(j == self.cut, 1, jnp.where(j == self.after, 2, 0))


def tile(j):
    return slice(j * LANES, (j + 1) * LANES)


def pair(j):
    return slice(j * LANES, (j + 2) * LANES)


class Rows:
    def __init__(self, first, count, parts):
        self.first, self.count, self.parts = first, count, parts

    def at(self, part, top=0):
        first = top + part * self.parts + self.first
        return pl.ds(first if isinstance(first, int) else pl.multiple_of(first, 16), self.count)

    def read(self, ref, lanes, top=0):
        return jnp.concatenate([ref[self.at(0, top), lanes], ref[self.at(1, top), lanes]], axis=0)

    def pairs(self, ref, j, top=0):
        return jnp.concatenate([ref[self.at(0, top), pair(j)], ref[self.at(1, top), pair(j)]], axis=1)

    def write(self, ref, lanes, both, top=0):
        ref[self.at(0, top), lanes] = both[: self.count]
        ref[self.at(1, top), lanes] = both[self.count :]


def column_step(tiles, index, col_taps, load, store, count, limit=512):
    groups, room = [], 0
    for j in range(count):
        which = index(j)
        plain = isinstance(which, int)
        if plain and groups and isinstance(groups[-1][0], int) and room > 0:
            groups[-1][1].append(j)
        else:
            groups.append((which, [j]))
            room = limit
        room -= load(j).shape[0] if plain else limit
    for which, members in groups:
        parts = [load(j) for j in members]
        size = parts[0].shape[0]
        y = dot(jnp.concatenate(parts, axis=0), col_taps[which])
        for at, j in enumerate(members):
            store(j, y[at * size : (at + 1) * size])


def forward_rows(
    tiles, part, leave, near_slab, near_lanes, far_slab, row_near, row_half, col_taps, waves, entry, field, after, narrow, leaving,
):
    mid, width = part.parts, tiles.width
    size = part.count
    for at, lanes in lane_chunks(width):
        here = slice(at, at + lanes)
        left = jnp.concatenate(
            [row_near[part.at(comp, member * 2 * mid), near_lanes] for member in range(2) for comp in range(2)], axis=0
        )
        result = dot(left, near_slab[:, here])
        for member in range(2):
            re = result[2 * member * size : (2 * member + 1) * size]
            im = result[(2 * member + 1) * size : (2 * member + 2) * size]
            vr, vi = waves[2 * member : 2 * member + 1, here], waves[2 * member + 1 : 2 * member + 2, here]
            entry[member, :size, here] = (re * vr - im * vi).astype(BF16)
            entry[member, size:, here] = (re * vi + im * vr).astype(BF16)
    entry[:, :, width:] = entry[:, :, :LANES]

    def load(j):
        return jnp.concatenate(
            [
                jnp.concatenate([entry[member, :size, pair(j)], entry[member, size:, pair(j)]], axis=1)
                for member in range(2)
            ],
            axis=0,
        )

    def store(j, y):
        y = y.astype(BF16)
        far = part.read(far_slab, tile(j))
        sr, si = far[:size], far[size:]
        for member in range(2):
            re, im = y[member * size : (member + 1) * size, :LANES], y[member * size : (member + 1) * size, LANES:]
            part.write(field.at[member], tile(j), jnp.concatenate([re, im], axis=0))
            re, im = re.astype(F32), im.astype(F32)
            both = jnp.concatenate([sr * re - si * im, sr * im + si * re], axis=0)
            part.write(after.at[member], tile(j), both.astype(BF16))

    column_step(tiles, lambda j: tiles.ahead(j, 0), col_taps, load, store, tiles.count)

    source = Rows(leave.first, 2 * leave.count, mid)
    for at, lanes in lane_chunks(width):
        here = slice(at, at + lanes)
        for member in range(2):
            y = dot(row_half[...], source.read(after.at[member], here)).astype(BF16)
            narrow[member, :, LANES + at : LANES + at + lanes] = y
    narrow[:, :, :LANES] = narrow[:, :, width:]
    size2 = leave.count

    def load2(j):
        return jnp.concatenate(
            [
                jnp.concatenate([narrow[member, :size2, pair(j)], narrow[member, size2:, pair(j)]], axis=1)
                for member in range(2)
            ],
            axis=0,
        )

    def store2(j, y):
        y = y.astype(BF16)
        for member in range(2):
            here = slice(member * size2, (member + 1) * size2)
            leaving[member, :size2, tile(j)] = y[here, :LANES]
            leaving[member, size2:, tile(j)] = y[here, LANES:]

    column_step(tiles, lambda j: tiles.back(j, 2), col_taps, load2, store2, tiles.count)


def residue_rows(tiles, members, windows, leave, split_meas, col_taps, leaving, residue, back):
    size = leave.count
    for member, window in zip(members, windows):
        for at, lanes in lane_chunks(tiles.width):
            here = slice(at, at + lanes)
            meas = dot(split_meas[...], window(at, lanes))
            residue[member, :, here] = (leaving[member, :, here].astype(F32) - meas).astype(BF16)
        residue[member, :, tiles.width :] = residue[member, :, :LANES]

    def load(j):
        return jnp.concatenate(
            [
                jnp.concatenate([residue[member, :size, pair(j)], residue[member, size:, pair(j)]], axis=1)
                for member in members
            ],
            axis=0,
        )

    def store(j, y):
        y = y.astype(BF16)
        for k, member in enumerate(members):
            here = slice(k * size, (k + 1) * size)
            leave.write(back.at[member], tile(j), jnp.concatenate([y[here, :LANES], y[here, LANES:]], axis=0))

    column_step(tiles, lambda j: tiles.ahead(j, 5), col_taps, load, store, tiles.count)


def backward_rows(tiles, members, part, left, right, field, far_slab, col_taps, waves, carry, far_sum, into):
    size, mid = part.count, part.parts
    for at, lanes in lane_chunks(tiles.width):
        here = slice(at, at + lanes)
        there = slice(LANES + at, LANES + at + lanes)
        far = part.read(far_slab, here)
        sr, si = far[:size], far[size:]
        total = None
        for member in members:
            y = dot(left, right(member, here))
            br, bi = y[:size], y[size:]
            inner = part.read(field.at[member], here).astype(F32)
            ir, ii = inner[:size], inner[size:]
            carry[member, :size, there] = (sr * br + si * bi).astype(BF16)
            carry[member, size:, there] = (sr * bi - si * br).astype(BF16)
            term = jnp.concatenate([ir * br + ii * bi, ir * bi - ii * br], axis=0)
            total = term if total is None else total + term
        part.write(far_sum, there, total)
    for member in members:
        carry[member, :, :LANES] = carry[member, :, tiles.width :]

    def load(j):
        return jnp.concatenate(
            [
                jnp.concatenate([carry[member, :size, pair(j)], carry[member, size:, pair(j)]], axis=1)
                for member in members
            ],
            axis=0,
        )

    def store(j, y):
        for k, member in enumerate(members):
            re, im = y[k * size : (k + 1) * size, :LANES], y[k * size : (k + 1) * size, LANES:]
            vr, vi = waves[2 * member : 2 * member + 1, tile(j)], waves[2 * member + 1 : 2 * member + 2, tile(j)]
            both = jnp.concatenate([re * vr + im * vi, im * vr - re * vi], axis=0)
            part.write(into, tile(j), both.astype(BF16), member * 2 * mid)

    column_step(tiles, lambda j: tiles.back(j, 7), col_taps, load, store, tiles.count - 1)


def split_rows(tiles, part, split, far_raw, far_slab, half):
    for j in range(tiles.count):
        part.write(far_slab, tile(j), dot(split[...], far_raw[:, pair(j)])[:, half : half + LANES])


def far_margin(tiles, half, part, far_sum, sums):
    for j in range(tiles.count - 1):
        y = part.read(far_sum, pair(j))[:, LANES - half : 2 * LANES - half]
        sums[:, tile(j)] = y.astype(BF16)


def outer_kernel(
    half,
    slices, outer, across, corner, measured, measured_got,
    row_near, row_half, row_half_adj, row_edge, col_taps, split_far, split_meas, waves,
    far_slab, field, after, back, far_sum, into, sums,
    near_raw, far_raw, entry, narrow, leaving, residue, carry,
):
    rows, cols = slices.shape[1], slices.shape[3]
    tiles = Tiles(cols)
    width = tiles.width
    mid = rows + 2 * half
    parity = lax.axis_index("rows") % 2

    for slab, ref, margin in ((0, near_raw, 4 * half), (1, far_raw, 2 * half)):
        own = ref.shape[0] - margin
        begin = 0 if slab == 0 else 4 * half
        first = parity * (rows - own // 2)
        at = pl.ds(pl.multiple_of((1 - parity) * margin, 16), own)
        ref[at, :cols] = slices[slab, pl.ds(first, own // 2)].reshape(own, cols)
        ref[at, cols:width] = across[pl.ds(pl.multiple_of(slab * 2 * rows + 2 * first, 16), own)]
        at = pl.ds(pl.multiple_of(parity * own, 16), margin)
        ref[at, :cols] = outer[begin // 2 : (begin + margin) // 2].reshape(margin, cols)
        ref[at, cols:width] = corner[begin : begin + margin]
    far_raw[:, width:] = far_raw[:, :LANES]

    part = Rows(parity * (rows // 2), rows, mid)
    source = Rows(parity * (rows // 2), rows // 2, mid)
    leave = Rows(parity * (rows // 2), rows // 2, rows)
    edge = Rows(parity * rows, 2 * half, mid)
    pick = Rows(parity * 2 * half, 2 * half, rows)
    split_rows(tiles, part, split_far, far_raw, far_slab, half)
    lanes = pl.ds(pl.multiple_of(parity * 4 * half, LANES), near_raw.shape[0])
    forward_rows(
        tiles, part, source, near_raw, lanes, far_slab, row_near, row_half, col_taps, waves, entry, field, after,
        narrow, leaving,
    )
    windows = (functools.partial(own_window, measured, parity), functools.partial(got_window, measured_got))
    residue_rows(tiles, (0, 1), windows, leave, split_meas, col_taps, leaving, residue, back)
    backward_rows(
        tiles, (0, 1), edge, pick.read(row_half_adj, slice(None)), lambda one, here: leave.read(back.at[one], here),
        field, far_slab, col_taps, waves, carry, far_sum, into,
    )
    far_sum[:, :LANES] = far_sum[:, width:]
    left = row_edge[...].T
    for at, size in lane_chunks(cols):
        here = slice(at, at + size)
        right = jnp.concatenate([edge.read(into, here, member * 2 * mid) for member in range(2)], axis=0)
        sums[: 4 * half, here] = dot(left, right).astype(BF16)
    far_margin(tiles, half, Rows(parity * (rows + half), half, mid), far_sum, sums.at[4 * half :])


def inner_kernel(
    half,
    slices, inner, across, measured, measured_got, far_slab_in, field_in, after_in, back_in, far_in, into_in,
    row_near, row_half, row_adj, row_near_adj, col_taps, split_meas, waves,
    far_slab, field, after, back, far_sum, into, sums, far_sums,
    near_raw, far_raw, entry, narrow, leaving, residue, carry,
):
    cols = into.shape[1]
    tiles = Tiles(cols)
    mid = far_sum.shape[0] // 2
    rows = mid - 2 * half
    other = 1 - lax.axis_index("rows") % 2
    part = Rows(other * rows, 2 * half, mid)
    source = Rows(other * (rows // 2), rows // 2, mid)
    leave = Rows(other * (rows // 2), rows // 2, rows)

    for slab, ref, margin in ((0, near_raw, 4 * half), (1, far_raw, 2 * half)):
        own = ref.shape[0] - margin
        begin = 0 if slab == 0 else 4 * half
        first = other * (rows - own // 2)
        at = pl.ds(pl.multiple_of((1 - other) * margin, 16), own)
        ref[at, :cols] = slices[slab, pl.ds(first, own // 2)].reshape(own, cols)
        ref[at, cols : tiles.width] = across[pl.ds(pl.multiple_of(slab * 2 * rows + 2 * first, 16), own)]
        ref[pl.ds(pl.multiple_of(other * own, 16), margin), : tiles.width] = inner[begin : begin + margin]
    far_raw[:, tiles.width :] = far_raw[:, :LANES]

    split_rows(tiles, part, split_meas, far_raw, far_slab, half)
    lanes = pl.ds(pl.multiple_of(other * 2 * rows, LANES), near_raw.shape[0])
    forward_rows(
        tiles, part, source, near_raw, lanes, far_slab, row_near, row_half, col_taps, waves, entry, field, after,
        narrow, leaving,
    )
    windows = (functools.partial(own_window, measured, other), functools.partial(got_window, measured_got))
    residue_rows(tiles, (0, 1), windows, leave, split_meas, col_taps, leaving, residue, back)
    rest = Rows(other * 2 * half, rows, mid)
    left = jnp.concatenate([row_adj[rest.at(0), :], row_adj[rest.at(1), :]], axis=0)
    backward_rows(
        tiles, (0, 1), rest, left, lambda one, here: back[one, :, here], field, far_slab, col_taps, waves, carry,
        far_sum, into,
    )
    far_sum[:, :LANES] = far_sum[:, tiles.width :]
    at = pl.ds(pl.multiple_of(other * 2 * (rows + 2 * half), 16), 4 * half)
    for first, size in lane_chunks(cols):
        here = slice(first, first + size)
        sums[:, here] = dot(row_near_adj[at, :], into[:, here]).astype(BF16)
    far_margin(tiles, half, Rows(other * (rows + half), half, mid), far_sum, far_sums)


def sums_kernel(half, into, far_sum, row_near_adj, near, far):
    cols = into.shape[1]
    mid = far_sum.shape[0] // 2
    rows = mid - 2 * half
    margin = 4 * half
    for at, size in lane_chunks(cols):
        here = slice(at, at + size)
        near[:, here] = dot(row_near_adj[margin : margin + 2 * rows], into[:, here])
    for j in range(cols // LANES):
        for comp in range(2):
            top = comp * mid + half
            far[comp, :, tile(j)] = far_sum[top : top + rows, pair(j)][:, LANES - half : 2 * LANES - half]


def inner_sums_kernel(half, near_sum, far_sum, inner, inner_far, near, far, near_rows, far_rows, sems):
    rows, cols = near.shape[0], near.shape[2]
    other = 1 - lax.axis_index("rows") % 2
    at = pl.ds(pl.multiple_of(other * (2 * rows - 4 * half), 16), 4 * half)
    near_rows[...] = (near_sum[at] + inner[...].astype(F32)).reshape(2 * half, 2, cols)
    near_copy = pltpu.make_async_copy(near_rows, near.at[pl.ds(other * (rows - 2 * half), 2 * half)], sems.at[0])
    near_copy.start()
    at = pl.ds(pl.multiple_of(other * (rows - half), 16), half)
    for comp in range(2):
        far_rows[pl.ds((1 - other) * half, rows - 2 * half), comp, :] = far_sum[comp, half : rows - half]
        added = far_sum[comp, at] + inner_far[comp * half : (comp + 1) * half].astype(F32)
        far_rows[pl.ds(other * (rows - 2 * half), half), comp, :] = added
    far_copy = pltpu.make_async_copy(far_rows, far.at[pl.ds(other * half, rows - half)], sems.at[1])
    far_copy.start()
    near_copy.wait()
    far_copy.wait()


def finish_kernel(half, near_in, far_in, near_sum, far_sum, outer, near, far, near_rows, far_rows, sems):
    rows, cols = near.shape[0], near.shape[2]
    parity = lax.axis_index("rows") % 2
    margin = 4 * half
    at = pl.ds(pl.multiple_of(parity * (2 * rows - margin), 16), margin)
    near_rows[...] = (near_sum[at] + outer[:margin].astype(F32)).reshape(2 * half, 2, cols)
    near_copy = pltpu.make_async_copy(near_rows, near.at[pl.ds(parity * (rows - 2 * half), 2 * half)], sems.at[0])
    near_copy.start()
    at = pl.ds(pl.multiple_of(parity * (rows - half), 16), half)
    for comp in range(2):
        got = outer[margin + comp * half : margin + (comp + 1) * half].astype(F32)
        far_rows[:, comp, :] = far_sum[comp, at] + got
    far_copy = pltpu.make_async_copy(far_rows, far.at[pl.ds(parity * (rows - half), half)], sems.at[1])
    far_copy.start()
    near_copy.wait()
    far_copy.wait()


def call(kernel, outs, operands, hbm=(), scalars=(), outside=(), outs_outside=(), scratch=(), aliases=None, flops=0):
    def place(i):
        if i in scalars:
            return pltpu.SMEM
        return pltpu.HBM if i in hbm else pl.ANY if i in outside else pltpu.VMEM

    return pl.pallas_call(
        kernel,
        out_shape=[jax.ShapeDtypeStruct(shape, dtype) for shape, dtype in outs],
        in_specs=[pl.BlockSpec(memory_space=place(i)) for i in range(len(operands))],
        out_specs=[
            pl.BlockSpec(memory_space=pl.ANY if i in outs_outside else pltpu.VMEM) for i in range(len(outs))
        ],
        scratch_shapes=[one if not isinstance(one, tuple) else pltpu.VMEM(*one) for one in scratch],
        input_output_aliases=aliases or {},
        compiler_params=pltpu.CompilerParams(vmem_limit_bytes=20 * 2**20),
        cost_estimate=pl.CostEstimate(flops=flops, bytes_accessed=0, transcendentals=0),
    )(*(pltpu.with_memory_space_constraint(x, pltpu.HBM) if i in hbm else x for i, x in enumerate(operands)))


def columns_local(measured, slices, kernel_taps, angle_freq, chosen):
    rows, cols = slices.shape[1], slices.shape[3]
    length = measured.shape[3]
    half = (kernel_taps.shape[1] - 1) // 2
    wide, mid, width = rows + 4 * half, rows + 2 * half, cols + LANES
    count = lax.axis_size("rows")
    outer_pairs = [(i, j) for i in range(count) if 0 <= (j := i - 1 + 2 * (i % 2)) < count]
    inner_pairs = [(i, i + 1 - 2 * (i % 2)) for i in range(count)]
    side_pairs = [(i, 1 - i) for i in range(lax.axis_size("ang"))]
    edge = 6 * half
    outer, across = call(
        functools.partial(edges_kernel, half),
        [((3 * half, 2, cols), BF16), ((4 * rows + 16, LANES), BF16)],
        (slices, angle_freq.T, chosen), hbm=(0, 1), scalars=(2,), outs_outside=(0,),
        scratch=[((2, rows, 2, LANES), BF16), (angle_freq.shape[::-1], F32), pltpu.SemaphoreType.DMA((4,))],
    )
    outer_got = lax.ppermute(outer, "rows", outer_pairs)
    across_got = lax.ppermute(across, "ang", side_pairs)
    meas_outer, meas_inner = call(
        measured_kernel, [((rows // 2, 2, width), BF16)] * 2, (measured, across), hbm=(0,), outside=(1,),
        outs_outside=(0, 1), scratch=[pltpu.SemaphoreType.DMA((4,))],
    )
    outer_meas = lax.ppermute(meas_outer, "ang", side_pairs)
    inner_meas = lax.ppermute(meas_inner, "ang", side_pairs)
    phased = [
        ((4 * mid, 2 * wide), BF16), ((2 * wide, 4 * mid), BF16), ((8 * half, 4 * half), BF16), ((8, width), F32),
    ]
    row_real, row_imag, row_half, row_half_adj, row_adj, col_taps, split_far, split_meas, *partial = call(
        functools.partial(matrices_kernel, rows, length),
        [
            ((mid, 2 * wide), F32), ((mid, 2 * wide), F32), ((rows, 2 * rows), BF16), ((2 * rows, rows), BF16),
            ((2 * mid, 2 * rows), BF16), ((10, 4 * LANES, 2 * LANES), BF16), ((2 * rows, 2 * rows), BF16),
            ((rows, rows), BF16), *phased,
        ],
        (kernel_taps, across), flops=MATS_FLOPS,
    )
    (strip,) = call(
        functools.partial(strip_kernel, half), [((edge, LANES), BF16)], (across_got, row_half), outside=(1,),
        flops=STRIP_FLOPS,
    )
    corner_got = lax.ppermute(strip, "rows", outer_pairs)
    (inner,) = call(
        functools.partial(inner_edge_kernel, half), [((edge, width), BF16)], (slices, across_got, strip), outside=(2,),
    )
    inner_got = lax.ppermute(inner, "rows", inner_pairs)
    row_near, row_near_adj, row_edge, waves = call(
        functools.partial(phases_kernel, half, length), phased, (row_real, row_imag, across_got, *partial),
        aliases={3: 0, 4: 1, 5: 2, 6: 3},
    )
    state = [
        ((2 * mid, width), F32), ((2, 2 * mid, width), BF16), ((2, 2 * mid, width), BF16),
        ((2, 2 * rows, width), BF16), ((2 * mid, width + LANES), F32), ((4 * mid, cols), BF16),
    ]
    leaving_shape = ((2, rows, width), BF16)
    far_slab, field, after, back, far_sum, into, outer_sums = call(
        functools.partial(outer_kernel, half),
        [*state, ((edge, cols), BF16)],
        (
            slices, outer_got, across_got, corner_got, measured, outer_meas,
            row_near, row_half, row_half_adj, row_edge, col_taps, split_far, split_meas, waves,
        ),
        scratch=[
            ((2 * rows + 4 * half, width), BF16), ((2 * rows, width + LANES), BF16),
            ((2, 2 * rows, width + LANES), BF16), ((2, rows, width + LANES), BF16), leaving_shape,
            ((2, rows, width + LANES), BF16), ((2, 4 * half, width + LANES), BF16),
        ],
        flops=OWN_FLOPS,
    )
    outer_back = lax.ppermute(outer_sums, "rows", outer_pairs)
    far_slab, field, after, back, far_sum, into, inner_sums, inner_far = call(
        functools.partial(inner_kernel, half),
        [*state, ((4 * half, cols), BF16), ((2 * half, cols), BF16)],
        (
            slices, inner_got, across_got, measured, inner_meas, far_slab, field, after, back, far_sum, into,
            row_near, row_half, row_adj, row_near_adj, col_taps, split_meas, waves,
        ),
        aliases={5: 0, 6: 1, 7: 2, 8: 3, 9: 4, 10: 5},
        scratch=[
            ((rows + 4 * half, width), BF16), ((4 * half, width + LANES), BF16),
            ((2, 4 * half, width + LANES), BF16), ((2, rows, width + LANES), BF16), leaving_shape,
            ((2, rows, width + LANES), BF16), ((2, 2 * rows, width + LANES), BF16),
        ],
        flops=INNER_FLOPS,
    )
    inner_back = lax.ppermute(inner_sums, "rows", inner_pairs)
    inner_far_back = lax.ppermute(inner_far, "rows", inner_pairs)
    near_sum, far_own = call(
        functools.partial(sums_kernel, half), [((2 * rows, cols), F32), ((2, rows, cols), F32)],
        (into, far_sum, row_near_adj),
    )
    near, far = call(
        functools.partial(inner_sums_kernel, half), [((rows, 2, cols), F32)] * 2,
        (near_sum, far_own, inner_back, inner_far_back), outs_outside=(0, 1),
        scratch=[((2 * half, 2, cols), F32), ((rows - half, 2, cols), F32), pltpu.SemaphoreType.DMA((2,))],
    )
    near, far = call(
        functools.partial(finish_kernel, half), [((rows, 2, cols), F32)] * 2,
        (near, far, near_sum, far_own, outer_back), outside=(0, 1), outs_outside=(0, 1), aliases={0: 0, 1: 1},
        scratch=[((2 * half, 2, cols), F32), ((half, 2, cols), F32), pltpu.SemaphoreType.DMA((2,))],
    )
    return near, far


def with_halo(block, sides, width):
    for axis, dim in sides:
        count = lax.axis_size(axis)
        forward = [(i, i + 1) for i in range(count - 1)]
        backward = [(target, source) for source, target in forward]
        low = lax.ppermute(
            lax.slice_in_dim(block, block.shape[dim] - width, None, axis=dim), axis, forward
        )
        high = lax.ppermute(lax.slice_in_dim(block, 0, width, axis=dim), axis, backward)
        block = jnp.concatenate([low, block, high], axis=dim)
    return block


def toeplitz(row_taps, out_width):
    tap_count = row_taps.shape[0]
    window = out_width + tap_count - 1
    padded = jnp.concatenate([row_taps, jnp.zeros((out_width,), row_taps.dtype)])
    tiled = jnp.tile(padded, out_width)[: out_width * window]
    return tiled.reshape(out_width, window).T


def kernel_pair(kernel_taps, out_width):
    return jnp.concatenate(
        [toeplitz(kernel_taps[0], out_width), toeplitz(kernel_taps[1], out_width)], axis=1
    )


def adjoint_taps(kernel_taps):
    return jnp.stack([kernel_taps[0][::-1], -kernel_taps[1][::-1]])


def correlate_columns(field, kernel):
    window, doubled = kernel.shape
    tile_len = doubled // 2
    half_taps = (window - tile_len) // 2
    leading, comps, length = field.shape
    blocks = length // tile_len
    padded = jnp.pad(field, ((0, 0), (0, 0), (half_taps, tile_len - half_taps)))
    main_part = padded[:, :, :length].reshape(leading, comps, blocks, tile_len)
    tail_part = padded[:, :, tile_len : tile_len + length].reshape(
        leading, comps, blocks, tile_len
    )[..., : 2 * half_taps]
    windows = jnp.concatenate([main_part, tail_part], axis=3)
    product = jnp.einsum("rpnw,wk->rpnk", windows, kernel, preferred_element_type=jnp.float32)
    real_part = product[:, 0, :, :tile_len] - product[:, 1, :, tile_len:]
    imag_part = product[:, 0, :, tile_len:] + product[:, 1, :, :tile_len]
    return (
        jnp.stack([real_part, imag_part], axis=1)
        .reshape(leading, comps, length)
        .astype(jnp.bfloat16)
    )


def band_rows(padded, band):
    out_rows = band.shape[1] // 2
    product = jnp.einsum("jpc,jk->kpc", padded, band, preferred_element_type=jnp.float32)
    real_part = product[:out_rows, 0] - product[out_rows:, 1]
    imag_part = product[out_rows:, 0] + product[:out_rows, 1]
    return jnp.stack([real_part, imag_part], axis=1).astype(jnp.bfloat16)


def complex_times(left, right):
    left = left.astype(jnp.float32)
    right = right.astype(jnp.float32)
    real_part = left[:, 0] * right[:, 0] - left[:, 1] * right[:, 1]
    imag_part = left[:, 0] * right[:, 1] + left[:, 1] * right[:, 0]
    return jnp.stack([real_part, imag_part], axis=1)


def conjugate_times(left, right):
    left = left.astype(jnp.float32)
    right = right.astype(jnp.float32)
    real_part = left[:, 0] * right[:, 0] + left[:, 1] * right[:, 1]
    imag_part = left[:, 0] * right[:, 1] - left[:, 1] * right[:, 0]
    return jnp.stack([real_part, imag_part], axis=1)


def incident(freq, row_pos, col_pos, length):
    scale = 2.0 * math.pi / length
    phase = scale * (freq[0] * row_pos[:, None] + freq[1] * col_pos[None, :])
    return jnp.stack([jnp.cos(phase), jnp.sin(phase)], axis=1)


def local(measured, slices, kernel_taps, angle_freq, chosen):
    rows_dev = measured.shape[1]
    length = measured.shape[3]
    half_taps = (kernel_taps.shape[1] - 1) // 2
    backward_taps = adjoint_taps(kernel_taps)
    forward_kernel = kernel_pair(kernel_taps, 128)
    adjoint_kernel = kernel_pair(backward_taps, 128)
    forward_band = kernel_pair(kernel_taps, rows_dev)
    adjoint_band = kernel_pair(backward_taps, rows_dev)
    gathered = lax.all_gather(slices, "ang", axis=3, tiled=True)
    near_slab = gathered[0]
    far_slab = gathered[1]
    start = lax.axis_index("rows") * rows_dev
    row_pos = (start + jnp.arange(rows_dev, dtype=jnp.int32)).astype(jnp.float32)
    col_pos = jnp.arange(length).astype(jnp.float32)
    onehot = (chosen[:, None] == jnp.arange(angle_freq.shape[0], dtype=jnp.int32)[None, :]).astype(
        jnp.float32
    )
    freqs = jnp.dot(onehot, angle_freq, precision=lax.Precision.HIGHEST)

    def along_rows(field, band):
        padded = with_halo(field, (("rows", 0),), half_taps)
        result = band_rows(padded, band)
        return result

    member = 0
    entering = incident(freqs[member], row_pos, col_pos, length)
    entry0 = complex_times(near_slab, entering).astype(jnp.bfloat16)
    inner = along_rows(correlate_columns(entry0, forward_kernel), forward_band)
    entry1 = complex_times(far_slab, inner).astype(jnp.bfloat16)
    exit_field = along_rows(correlate_columns(entry1, forward_kernel), forward_band)
    residue = (exit_field.astype(jnp.float32) - measured[member].astype(jnp.float32)).astype(
        jnp.bfloat16
    )
    back_far = correlate_columns(along_rows(residue, adjoint_band), adjoint_kernel)
    grad_far = conjugate_times(inner, back_far)
    carried_list = [conjugate_times(far_slab, back_far).astype(jnp.bfloat16)]
    member = 0
    entering = incident(freqs[member], row_pos, col_pos, length)
    back_near = correlate_columns(along_rows(carried_list[member], adjoint_band), adjoint_kernel)
    grad_near = conjugate_times(entering, back_near)
    near_total, far_total = (
        lax.psum_scatter(
            grad_near.astype(jnp.bfloat16), "ang", scatter_dimension=2, tiled=True
        ).astype(jnp.float32),
        lax.psum_scatter(
            grad_far.astype(jnp.bfloat16), "ang", scatter_dimension=2, tiled=True
        ).astype(jnp.float32),
    )
    return (near_total, far_total)


def pick(measured, slices, kernel_taps, angle_freq, chosen):
    rows, cols = slices.shape[1], slices.shape[3]
    taps = kernel_taps.shape[1]
    fits = (
        lax.axis_size("ang") == 2
        and lax.axis_size("rows") % 2 == 0
        and 2 * (taps - 1) == LANES
        and rows >= taps - 1
        and rows % LANES == 0
        and cols % (2 * LANES) == 0
    )
    run = columns_local if fits else local
    return run(measured, slices, kernel_taps, angle_freq, chosen)


def solution(mesh):
    return jax.shard_map(
        pick,
        mesh=mesh,
        in_specs=(P("ang", "rows", None, None), P(None, "rows", None, "ang"), P(), P(), P("ang")),
        out_specs=(P("rows", None, "ang"), P("rows", None, "ang")),
        check_vma=False,
    )
```

```python
import functools
import math

import jax
import jax.numpy as jnp
from jax import lax
from jax.experimental import pallas as pl
from jax.experimental.pallas import tpu as pltpu
from jax.sharding import PartitionSpec as P

LANES = 128
BF16 = jnp.bfloat16
INNER_FLOPS = 0
FORWARD_FLOPS = 24 * 10**8
BACKWARD_FLOPS = 10**9
MEASURED_FLOPS = 4 * 10**9
F32 = jnp.float32


def dot(left, right):
    return jnp.dot(left, right, preferred_element_type=F32)


def iota(shape, dim):
    return lax.broadcasted_iota(jnp.int32, shape, dim)


def lane_chunks(width, step=2 * LANES):
    return [(at, min(step, width - at)) for at in range(0, width, step)]


def edges_kernel(half, slices, angle_freq, outer, early, across, table, strips, sems):
    rows, cols = slices.shape[1], slices.shape[3]
    parity = lax.axis_index("rows") % 2
    side = lax.axis_index("ang")
    lane = pl.multiple_of((1 - side) * (cols - LANES), LANES)
    copies = [(angle_freq, table), (slices.at[:, :, :, pl.ds(lane, LANES)], strips)]
    for slab, at, size in ((0, 0, 2 * half), (1, 2 * half, half)):
        copies.append((slices.at[slab, pl.ds(parity * (rows - size), size)], outer.at[pl.ds(at, size)]))
    copies = [pltpu.make_async_copy(frm, to, sems.at[i]) for i, (frm, to) in enumerate(copies)]
    for copy in copies:
        copy.start()
    for copy in copies[:2]:
        copy.wait()
    begin, rest = 0, 0
    for slab, size in ((0, 2 * half), (1, half)):
        there = strips[slab, pl.ds(parity * (rows - size), size)]
        early[begin : begin + 2 * size] = there.reshape(2 * size, LANES)
        there = strips[slab, pl.ds((1 - parity) * size, rows - size)]
        across[rest : rest + 2 * (rows - size)] = there.reshape(2 * (rows - size), LANES)
        begin, rest = begin + 2 * size, rest + 2 * (rows - size)
    early[begin:] = jnp.zeros((16, LANES), BF16)
    for copy in copies[2:]:
        copy.wait()


def frequencies_kernel(table, chosen, early_in, early):
    row = iota((16, LANES), 0)
    block = jnp.zeros((16, LANES), F32)
    entry = jnp.where(iota(table.shape, 1) == chosen[0], table[...], 0.0)
    freqs = jnp.sum(entry, axis=1, keepdims=True)
    for part in range(2):
        rest = jnp.broadcast_to(freqs[part : part + 1], (16, LANES))
        for piece in range(3):
            rounded = rest.astype(BF16).astype(F32)
            block = jnp.where(row == 3 * part + piece, rounded, block)
            rest = rest - rounded
    early[early.shape[0] - 16 :] = block.astype(BF16)


def sent_frequencies(across):
    sent = across[across.shape[0] - 16 :].astype(F32)
    return [(sent[i : i + 1] + sent[i + 1 : i + 2] + sent[i + 2 : i + 3])[:, :1] for i in (0, 3)]


def inner_edge_kernel(half, slices, across, sent, edge):
    rows, cols = slices.shape[1], slices.shape[3]
    other = 1 - lax.axis_index("rows") % 2
    begin = 0
    for slab, size in ((0, 2 * half), (1, half)):
        there = slice(begin, begin + 2 * size)
        edge[there, :cols] = slices[slab, pl.ds(other * (rows - size), size)].reshape(2 * size, cols)
        begin += 2 * size
    edge[: 4 * half, cols:] = across[inner_rows(half, rows, other, 0)]
    edge[4 * half :, cols:] = across[inner_rows(half, rows, other, 1)]


def inner_rows(half, rows, other, slab):
    if slab == 0:
        return pl.ds(pl.multiple_of(other * (2 * rows - 8 * half), 16), 4 * half)
    return pl.ds(pl.multiple_of(2 * rows - 4 * half + other * (2 * rows - 4 * half), 16), 2 * half)


def measured_kernel(measured, sent, outer, inner, sems):
    size, cols = outer.shape[0], measured.shape[3] // 2
    parity = lax.axis_index("rows") % 2
    side = lax.axis_index("ang")
    copies = []
    for late, out in ((parity, outer), (1 - parity, inner)):
        for frm, at, lanes in (((1 - side) * cols, 0, cols), (cols - (1 - side) * LANES, cols, LANES)):
            here = pl.ds(pl.multiple_of(frm, LANES), lanes)
            there = measured.at[0, pl.ds(late * size, size), :, here]
            copies.append(pltpu.make_async_copy(there, out.at[:, :, at : at + lanes], sems.at[len(copies)]))
    for copy in copies:
        copy.start()
    for copy in copies:
        copy.wait()


def own_window(measured, late, at, size):
    half_rows, cols = measured.shape[1] // 2, measured.shape[3] // 2
    rows = pl.ds(late * half_rows, half_rows)
    first, second = (at, cols + at) if at < cols else (cols, cols - LANES)
    left = measured[0, rows, :, first : first + size].reshape(2 * half_rows, size)
    right = measured[0, rows, :, second : second + size].reshape(2 * half_rows, size)
    return jnp.where(lax.axis_index("ang") == 0, left, right)


def got_window(window, at, size):
    return window[:, :, at : at + size].reshape(2 * window.shape[0], size)


def skewed(base, count, stride):
    width = base.shape[1]
    return pltpu.roll(jnp.broadcast_to(base, (count, width)), 0, 1, stride=stride, stride_axis=0)


def matrices_kernel(
    rows, length, taps, across,
    row_real, row_imag, row_half, row_half_adj, row_adj, col_taps, split_far, split_meas,
    row_near, row_near_adj, row_edge, waves,
):
    count = taps.shape[1]
    half = (count - 1) // 2
    wide = rows + 4 * half
    mid = rows + 2 * half
    table = jnp.concatenate(
        [jnp.concatenate([taps[...], jnp.zeros((2, LANES - count), BF16)], axis=1),
         jnp.zeros((14, LANES), BF16)], axis=0,
    )

    def spread(width, place):
        tap = iota((LANES, width), 0)
        lane = iota((LANES, width), 1)
        hit = jnp.logical_and(lane == place(tap), tap < count)
        return dot(table, jnp.where(hit, 1.0, 0.0).astype(BF16))

    even = spread(2 * wide, lambda tap: 2 * tap)
    odd = spread(2 * wide, lambda tap: 2 * tap + 1)
    row_real[...] = skewed(even[0:1] - odd[1:2], mid, 2)
    row_imag[...] = skewed(even[1:2] + odd[0:1], mid, 2)

    add_phases(half, length, 0, across, row_real, row_imag, row_near, row_near_adj, row_edge, waves)

    low = spread(2 * mid, lambda tap: tap)
    high = spread(2 * mid, lambda tap: mid + tap)
    full = jnp.concatenate(
        [skewed(low[0:1] - high[1:2], rows, 1), skewed(low[1:2] + high[0:1], rows, 1)], axis=0
    )
    row_adj[...] = full.T.astype(BF16)
    low = spread(2 * rows, lambda tap: tap)
    high = spread(2 * rows, lambda tap: rows + tap)
    full = jnp.concatenate(
        [skewed(low[0:1] - high[1:2], rows // 2, 1), skewed(low[1:2] + high[0:1], rows // 2, 1)], axis=0
    )
    row_half[...] = full.astype(BF16)
    row_half_adj[...] = full.T.astype(BF16)

    window = 2 * LANES
    source = iota((window, LANES), 0)
    target = iota((window, LANES), 1)
    same_side = (source < LANES) == (target < LANES - half)
    left_only = source < window - half
    right_only = source >= LANES - half
    everything = source >= 0
    at = 0
    for adjoint in (False, True):
        for offset, masks in ((0, (everything, same_side)), (2 * half, (everything, left_only, right_only))):
            if adjoint:
                base = spread(window, lambda tap: (window - offset - (count - 1) + tap) % window)
            else:
                base = spread(window, lambda tap: (window - offset - tap) % window)
            re = skewed(base[0:1], window, 1)[:, :LANES]
            im = skewed(base[1:2], window, 1)[:, :LANES]
            im = -im if adjoint else im
            for mask in masks:
                mre = jnp.where(mask, re, 0.0).astype(BF16)
                mim = jnp.where(mask, im, 0.0).astype(BF16)
                col_taps[at, :window, :LANES] = mre
                col_taps[at, :window, LANES:] = mim
                col_taps[at, window:, :LANES] = -mim
                col_taps[at, window:, LANES:] = mre
                at += 1

    for out in (split_far, split_meas):
        size = out.shape[0]
        to, frm = iota((size, size), 0), iota((size, size), 1)
        out[...] = jnp.where(frm == 2 * (to % (size // 2)) + to // (size // 2), 1.0, 0.0).astype(BF16)


def add_phases(half, length, member, sent, row_real, row_imag, row_near, row_near_adj, row_edge, waves):
    mid, wide = row_real.shape[0], row_real.shape[1] // 2
    rows, cols = mid - 2 * half, waves.shape[1] - LANES
    side = lax.axis_index("ang")
    freq_row, freq_col = sent_frequencies(sent)
    scale = 2.0 * math.pi / length
    lane = iota((1, cols + LANES), 1)
    col = jnp.where(side == 0, lane, jnp.where(lane < cols, lane + cols, lane - LANES)).astype(F32)
    phase = scale * (freq_col * col)
    waves[2 * member : 2 * member + 1] = jnp.cos(phase)
    waves[2 * member + 1 : 2 * member + 2] = jnp.sin(phase)
    start = lax.axis_index("rows") * rows - 2 * half
    row = (start + iota((1, 2 * wide), 1) // 2).astype(F32)
    phase = scale * (freq_row * row)
    cos, sin = jnp.cos(phase), jnp.sin(phase)
    re = row_real[...] * cos - row_imag[...] * sin
    im = row_imag[...] * cos + row_real[...] * sin
    full = jnp.concatenate([re, im], axis=0)
    at = member * 2 * mid
    row_near[at : at + 2 * mid] = full.astype(BF16)
    row_near_adj[:, at : at + 2 * mid] = full.T.astype(BF16)
    for part in range(2):
        low, high = 4 * half, 2 * wide - 4 * half
        near = full[part * mid : part * mid + 2 * half, :low]
        far = full[part * mid + mid - 2 * half : (part + 1) * mid, high:]
        edge = jnp.where(lax.axis_index("rows") % 2 == 0, near, far)
        row_edge[(2 * member + part) * 2 * half : (2 * member + part + 1) * 2 * half] = edge.astype(BF16)


def phases_kernel(
    half, length, row_real, row_imag, across, near_in, near_adj_in, edge_in, waves_in,
    row_near, row_near_adj, row_edge, waves,
):
    add_phases(half, length, 1, across, row_real, row_imag, row_near, row_near_adj, row_edge, waves)


class Tiles:
    def __init__(self, cols):
        self.count = cols // LANES + 1
        self.width = self.count * LANES
        self.cut = self.count - 1 - lax.axis_index("ang")
        self.after = lax.rem(self.cut + 1, self.count)

    def ahead(self, j, base):
        return base + jnp.where(j == self.cut, 1, 0) if j >= self.count - 2 else base

    def back(self, j, base):
        if 0 < j < self.count - 2:
            return base
        return base + jnp.where(j == self.cut, 1, jnp.where(j == self.after, 2, 0))


def tile(j):
    return slice(j * LANES, (j + 1) * LANES)


def pair(j):
    return slice(j * LANES, (j + 2) * LANES)


class Rows:
    def __init__(self, first, count, parts):
        self.first, self.count, self.parts = first, count, parts

    def at(self, part, top=0):
        first = top + part * self.parts + self.first
        return pl.ds(first if isinstance(first, int) else pl.multiple_of(first, 16), self.count)

    def read(self, ref, lanes, top=0):
        return jnp.concatenate([ref[self.at(0, top), lanes], ref[self.at(1, top), lanes]], axis=0)

    def pairs(self, ref, j, top=0):
        return jnp.concatenate([ref[self.at(0, top), pair(j)], ref[self.at(1, top), pair(j)]], axis=1)

    def write(self, ref, lanes, both, top=0):
        ref[self.at(0, top), lanes] = both[: self.count]
        ref[self.at(1, top), lanes] = both[self.count :]


def column_step(tiles, index, col_taps, load, store, count, limit=512):
    groups, room = [], 0
    for j in range(count):
        which = index(j)
        plain = isinstance(which, int)
        if plain and groups and isinstance(groups[-1][0], int) and room > 0:
            groups[-1][1].append(j)
        else:
            groups.append((which, [j]))
            room = limit
        room -= load(j).shape[0] if plain else limit
    for which, members in groups:
        parts = [load(j) for j in members]
        size = parts[0].shape[0]
        y = dot(jnp.concatenate(parts, axis=0), col_taps[which])
        for at, j in enumerate(members):
            store(j, y[at * size : (at + 1) * size])


def forward_rows(
    tiles, part, leave, near_slab, near_lanes, far_slab, row_near, row_half, col_taps, waves, entry, field, after, narrow, leaving,
):
    mid, width = part.parts, tiles.width
    size = part.count
    for at, lanes in lane_chunks(width):
        here = slice(at, at + lanes)
        left = jnp.concatenate(
            [row_near[part.at(comp, member * 2 * mid), near_lanes] for member in range(2) for comp in range(2)], axis=0
        )
        result = dot(left, near_slab[:, here])
        for member in range(2):
            re = result[2 * member * size : (2 * member + 1) * size]
            im = result[(2 * member + 1) * size : (2 * member + 2) * size]
            vr, vi = waves[2 * member : 2 * member + 1, here], waves[2 * member + 1 : 2 * member + 2, here]
            entry[member, :size, here] = (re * vr - im * vi).astype(BF16)
            entry[member, size:, here] = (re * vi + im * vr).astype(BF16)
    entry[:, :, width:] = entry[:, :, :LANES]

    def load(j):
        return jnp.concatenate(
            [
                jnp.concatenate([entry[member, :size, pair(j)], entry[member, size:, pair(j)]], axis=1)
                for member in range(2)
            ],
            axis=0,
        )

    def store(j, y):
        far = part.read(far_slab, tile(j))
        sr, si = far[:size], far[size:]
        for member in range(2):
            re, im = y[member * size : (member + 1) * size, :LANES], y[member * size : (member + 1) * size, LANES:]
            part.write(field.at[member], tile(j), jnp.concatenate([re, im], axis=0).astype(BF16))
            both = jnp.concatenate([sr * re - si * im, sr * im + si * re], axis=0)
            part.write(after.at[member], tile(j), both.astype(BF16))

    column_step(tiles, lambda j: tiles.ahead(j, 0), col_taps, load, store, tiles.count)

    source = Rows(leave.first, 2 * leave.count, mid)
    for at, lanes in lane_chunks(width):
        here = slice(at, at + lanes)
        for member in range(2):
            y = dot(row_half[...], source.read(after.at[member], here)).astype(BF16)
            narrow[member, :, LANES + at : LANES + at + lanes] = y
    narrow[:, :, :LANES] = narrow[:, :, width:]
    size2 = leave.count

    def load2(j):
        return jnp.concatenate(
            [
                jnp.concatenate([narrow[member, :size2, pair(j)], narrow[member, size2:, pair(j)]], axis=1)
                for member in range(2)
            ],
            axis=0,
        )

    def store2(j, y):
        y = y.astype(BF16)
        for member in range(2):
            here = slice(member * size2, (member + 1) * size2)
            leaving[member, :size2, tile(j)] = y[here, :LANES]
            leaving[member, size2:, tile(j)] = y[here, LANES:]

    column_step(tiles, lambda j: tiles.back(j, 2), col_taps, load2, store2, tiles.count)


def residue_rows(tiles, members, measured, leave, col_taps, leaving, residue, back):
    size = leave.count
    for member in members:
        for at, lanes in lane_chunks(tiles.width):
            here = slice(at, at + lanes)
            leaves = leaving[member, :, here].astype(F32)
            residue[member, :, here] = (leaves - measured(member, at, lanes)).astype(BF16)
        residue[member, :, tiles.width :] = residue[member, :, :LANES]

    def load(j):
        return jnp.concatenate(
            [
                jnp.concatenate([residue[member, :size, pair(j)], residue[member, size:, pair(j)]], axis=1)
                for member in members
            ],
            axis=0,
        )

    def store(j, y):
        y = y.astype(BF16)
        for k, member in enumerate(members):
            here = slice(k * size, (k + 1) * size)
            leave.write(back.at[member], tile(j), jnp.concatenate([y[here, :LANES], y[here, LANES:]], axis=0))

    column_step(tiles, lambda j: tiles.ahead(j, 5), col_taps, load, store, tiles.count)


def backward_rows(tiles, members, part, left, right, field, far_slab, col_taps, waves, carry, far_sum, into):
    size, mid = part.count, part.parts
    for at, lanes in lane_chunks(tiles.width):
        here = slice(at, at + lanes)
        there = slice(LANES + at, LANES + at + lanes)
        far = part.read(far_slab, here)
        sr, si = far[:size], far[size:]
        total = None
        for member in members:
            y = dot(left, right(member, here))
            br, bi = y[:size], y[size:]
            inner = part.read(field.at[member], here).astype(F32)
            ir, ii = inner[:size], inner[size:]
            carry[member, :size, there] = (sr * br + si * bi).astype(BF16)
            carry[member, size:, there] = (sr * bi - si * br).astype(BF16)
            term = jnp.concatenate([ir * br + ii * bi, ir * bi - ii * br], axis=0)
            total = term if total is None else total + term
        part.write(far_sum, there, total)
    for member in members:
        carry[member, :, :LANES] = carry[member, :, tiles.width :]

    def load(j):
        return jnp.concatenate(
            [
                jnp.concatenate([carry[member, :size, pair(j)], carry[member, size:, pair(j)]], axis=1)
                for member in members
            ],
            axis=0,
        )

    def store(j, y):
        for k, member in enumerate(members):
            re, im = y[k * size : (k + 1) * size, :LANES], y[k * size : (k + 1) * size, LANES:]
            vr, vi = waves[2 * member : 2 * member + 1, tile(j)], waves[2 * member + 1 : 2 * member + 2, tile(j)]
            both = jnp.concatenate([re * vr + im * vi, im * vr - re * vi], axis=0)
            part.write(into, tile(j), both.astype(BF16), member * 2 * mid)

    column_step(tiles, lambda j: tiles.back(j, 7), col_taps, load, store, tiles.count - 1)


def split_rows(tiles, part, split, far_raw, far_slab, half):
    for j in range(tiles.count):
        part.write(far_slab, tile(j), dot(split[...], far_raw[:, pair(j)])[:, half : half + LANES])


def far_margin(tiles, half, part, far_sum, sums):
    for j in range(tiles.count - 1):
        y = part.read(far_sum, pair(j))[:, LANES - half : 2 * LANES - half]
        sums[:, tile(j)] = y.astype(BF16)


def outer_forward_kernel(
    half,
    slices, outer, early, across, corner,
    row_near, row_half, col_taps, split_far, waves,
    far_slab, field, after, leaving,
    near_raw, far_raw, entry, narrow,
):
    rows, cols = slices.shape[1], slices.shape[3]
    tiles = Tiles(cols)
    width = tiles.width
    mid = rows + 2 * half
    parity = lax.axis_index("rows") % 2

    begin, rest = 0, 0
    for slab, ref, margin in ((0, near_raw, 4 * half), (1, far_raw, 2 * half)):
        own = ref.shape[0] - margin
        first = parity * (rows - own // 2)
        at = pl.ds(pl.multiple_of((1 - parity) * margin, 16), own)
        ref[at, :cols] = slices[slab, pl.ds(first, own // 2)].reshape(own, cols)
        at = pl.ds(pl.multiple_of(margin + parity * (own - 2 * margin), 16), margin)
        ref[at, cols:width] = early[begin : begin + margin]
        at = pl.ds(pl.multiple_of((1 - parity) * 2 * margin, 16), own - margin)
        frm = pl.ds(pl.multiple_of(rest + parity * (2 * rows - own), 16), own - margin)
        ref[at, cols:width] = across[frm]
        at = pl.ds(pl.multiple_of(parity * own, 16), margin)
        ref[at, :cols] = outer[begin // 2 : (begin + margin) // 2].reshape(margin, cols)
        ref[at, cols:width] = corner[begin : begin + margin]
        begin, rest = begin + margin, rest + 2 * rows - margin
    far_raw[:, width:] = far_raw[:, :LANES]

    part = Rows(parity * (rows // 2), rows, mid)
    source = Rows(parity * (rows // 2), rows // 2, mid)
    split_rows(tiles, part, split_far, far_raw, far_slab, half)
    lanes = pl.ds(pl.multiple_of(parity * 4 * half, LANES), near_raw.shape[0])
    forward_rows(
        tiles, part, source, near_raw, lanes, far_slab, row_near, row_half, col_taps, waves, entry, field, after,
        narrow, leaving,
    )


def outer_backward_kernel(
    half,
    far_slab, field, leaving, measured, measured_got,
    row_half_adj, row_edge, col_taps, split_meas, waves,
    back, far_sum, into, sums,
    residue, carry,
):
    cols = into.shape[1]
    tiles = Tiles(cols)
    mid = far_sum.shape[0] // 2
    rows = mid - 2 * half
    parity = lax.axis_index("rows") % 2
    leave = Rows(parity * (rows // 2), rows // 2, rows)
    edge = Rows(parity * rows, 2 * half, mid)
    pick = Rows(parity * 2 * half, 2 * half, rows)
    windows = (functools.partial(own_window, measured, parity), functools.partial(got_window, measured_got))

    def parts(member, at, size):
        return dot(split_meas[...], windows[member](at, size))

    residue_rows(tiles, (0, 1), parts, leave, col_taps, leaving, residue, back)
    backward_rows(
        tiles, (0, 1), edge, pick.read(row_half_adj, slice(None)), lambda one, here: leave.read(back.at[one], here),
        field, far_slab, col_taps, waves, carry, far_sum, into,
    )
    far_sum[:, :LANES] = far_sum[:, tiles.width :]
    left = row_edge[...].T
    for at, size in lane_chunks(cols):
        here = slice(at, at + size)
        right = jnp.concatenate([edge.read(into, here, member * 2 * mid) for member in range(2)], axis=0)
        sums[: 4 * half, here] = dot(left, right).astype(BF16)
    far_margin(tiles, half, Rows(parity * (rows + half), half, mid), far_sum, sums.at[4 * half :])


def inner_measured_kernel(measured, measured_got, split_meas, sent, parts):
    other = 1 - lax.axis_index("rows") % 2
    windows = (functools.partial(own_window, measured, other), functools.partial(got_window, measured_got))
    for member in range(2):
        for at, size in lane_chunks(parts.shape[2]):
            parts[member, :, at : at + size] = dot(split_meas[...], windows[member](at, size))


def inner_kernel(
    half,
    slices, inner, across, measured, far_slab_in, field_in, after_in, back_in, far_in, into_in,
    row_near, row_half, row_adj, row_near_adj, col_taps, split_meas, waves,
    far_slab, field, after, back, far_sum, into, sums, far_sums,
    near_raw, far_raw, entry, narrow, leaving, residue, carry,
):
    cols = into.shape[1]
    tiles = Tiles(cols)
    mid = far_sum.shape[0] // 2
    rows = mid - 2 * half
    other = 1 - lax.axis_index("rows") % 2
    part = Rows(other * rows, 2 * half, mid)
    source = Rows(other * (rows // 2), rows // 2, mid)
    leave = Rows(other * (rows // 2), rows // 2, rows)

    for slab, ref, margin in ((0, near_raw, 4 * half), (1, far_raw, 2 * half)):
        own = ref.shape[0] - margin
        begin = 0 if slab == 0 else 4 * half
        first = other * (rows - own // 2)
        at = pl.ds(pl.multiple_of((1 - other) * margin, 16), own)
        ref[at, :cols] = slices[slab, pl.ds(first, own // 2)].reshape(own, cols)
        ref[at, cols : tiles.width] = across[inner_rows(half, rows, other, slab)]
        ref[pl.ds(pl.multiple_of(other * own, 16), margin), : tiles.width] = inner[begin : begin + margin]
    far_raw[:, tiles.width :] = far_raw[:, :LANES]

    split_rows(tiles, part, split_meas, far_raw, far_slab, half)
    lanes = pl.ds(pl.multiple_of(other * 2 * rows, LANES), near_raw.shape[0])
    forward_rows(
        tiles, part, source, near_raw, lanes, far_slab, row_near, row_half, col_taps, waves, entry, field, after,
        narrow, leaving,
    )
    residue_rows(
        tiles, (0, 1), lambda member, at, size: measured[member, :, at : at + size], leave, col_taps, leaving,
        residue, back,
    )
    rest = Rows(other * 2 * half, rows, mid)
    left = jnp.concatenate([row_adj[rest.at(0), :], row_adj[rest.at(1), :]], axis=0)
    backward_rows(
        tiles, (0, 1), rest, left, lambda one, here: back[one, :, here], field, far_slab, col_taps, waves, carry,
        far_sum, into,
    )
    far_sum[:, :LANES] = far_sum[:, tiles.width :]
    at = pl.ds(pl.multiple_of(other * 2 * (rows + 2 * half), 16), 4 * half)
    for first, size in lane_chunks(cols):
        here = slice(first, first + size)
        sums[:, here] = dot(row_near_adj[at, :], into[:, here]).astype(BF16)
    far_margin(tiles, half, Rows(other * (rows + half), half, mid), far_sum, far_sums)


def sums_kernel(half, into, far_sum, row_near_adj, near, far):
    cols = into.shape[1]
    mid = far_sum.shape[0] // 2
    rows = mid - 2 * half
    margin = 4 * half
    for at, size in lane_chunks(cols):
        here = slice(at, at + size)
        near[:, here] = dot(row_near_adj[margin : margin + 2 * rows], into[:, here])
    for j in range(cols // LANES):
        for comp in range(2):
            top = comp * mid + half
            far[comp, :, tile(j)] = far_sum[top : top + rows, pair(j)][:, LANES - half : 2 * LANES - half]


def inner_sums_kernel(half, near_sum, far_sum, inner, inner_far, near, far, near_rows, far_rows, sems):
    rows, cols = near.shape[0], near.shape[2]
    other = 1 - lax.axis_index("rows") % 2
    at = pl.ds(pl.multiple_of(other * (2 * rows - 4 * half), 16), 4 * half)
    near_rows[...] = (near_sum[at] + inner[...].astype(F32)).reshape(2 * half, 2, cols)
    near_copy = pltpu.make_async_copy(near_rows, near.at[pl.ds(other * (rows - 2 * half), 2 * half)], sems.at[0])
    near_copy.start()
    at = pl.ds(pl.multiple_of(other * (rows - half), 16), half)
    for comp in range(2):
        far_rows[pl.ds((1 - other) * half, rows - 2 * half), comp, :] = far_sum[comp, half : rows - half]
        added = far_sum[comp, at] + inner_far[comp * half : (comp + 1) * half].astype(F32)
        far_rows[pl.ds(other * (rows - 2 * half), half), comp, :] = added
    far_copy = pltpu.make_async_copy(far_rows, far.at[pl.ds(other * half, rows - half)], sems.at[1])
    far_copy.start()
    near_copy.wait()
    far_copy.wait()


def finish_kernel(half, near_in, far_in, near_sum, far_sum, outer, near, far, near_rows, far_rows, sems):
    rows, cols = near.shape[0], near.shape[2]
    parity = lax.axis_index("rows") % 2
    margin = 4 * half
    at = pl.ds(pl.multiple_of(parity * (2 * rows - margin), 16), margin)
    copies = []
    for piece in range(2):
        at = pl.ds(pl.multiple_of(parity * (2 * rows - margin) + piece * 2 * half, 16), 2 * half)
        added = near_sum[at] + outer[piece * 2 * half : (piece + 1) * 2 * half].astype(F32)
        here = pl.ds(piece * half, half)
        near_rows[here] = added.reshape(half, 2, cols)
        there = near.at[pl.ds(parity * (rows - 2 * half) + piece * half, half)]
        copies.append(pltpu.make_async_copy(near_rows.at[here], there, sems.at[piece]))
        copies[-1].start()
    at = pl.ds(pl.multiple_of(parity * (rows - half), 16), half)
    for comp in range(2):
        got = outer[margin + comp * half : margin + (comp + 1) * half].astype(F32)
        far_rows[:, comp, :] = far_sum[comp, at] + got
    far_copy = pltpu.make_async_copy(far_rows, far.at[pl.ds(parity * (rows - half), half)], sems.at[2])
    far_copy.start()
    for copy in copies:
        copy.wait()
    far_copy.wait()


def call(kernel, outs, operands, hbm=(), scalars=(), outside=(), outs_outside=(), scratch=(), aliases=None, flops=0):
    def place(i):
        if i in scalars:
            return pltpu.SMEM
        return pltpu.HBM if i in hbm else pl.ANY if i in outside else pltpu.VMEM

    return pl.pallas_call(
        kernel,
        out_shape=[jax.ShapeDtypeStruct(shape, dtype) for shape, dtype in outs],
        in_specs=[pl.BlockSpec(memory_space=place(i)) for i in range(len(operands))],
        out_specs=[
            pl.BlockSpec(memory_space=pl.ANY if i in outs_outside else pltpu.VMEM) for i in range(len(outs))
        ],
        scratch_shapes=[one if not isinstance(one, tuple) else pltpu.VMEM(*one) for one in scratch],
        input_output_aliases=aliases or {},
        compiler_params=pltpu.CompilerParams(vmem_limit_bytes=20 * 2**20),
        cost_estimate=pl.CostEstimate(flops=flops, bytes_accessed=0, transcendentals=0),
    )(*(pltpu.with_memory_space_constraint(x, pltpu.HBM) if i in hbm else x for i, x in enumerate(operands)))


def columns_local(measured, slices, kernel_taps, angle_freq, chosen):
    rows, cols = slices.shape[1], slices.shape[3]
    length = measured.shape[3]
    half = (kernel_taps.shape[1] - 1) // 2
    wide, mid, width = rows + 4 * half, rows + 2 * half, cols + LANES
    count = lax.axis_size("rows")
    outer_pairs = [(i, j) for i in range(count) if 0 <= (j := i - 1 + 2 * (i % 2)) < count]
    inner_pairs = [(i, i + 1 - 2 * (i % 2)) for i in range(count)]
    side_pairs = [(i, 1 - i) for i in range(lax.axis_size("ang"))]
    edge = 6 * half
    outer, early, across, table = call(
        functools.partial(edges_kernel, half),
        [
            ((3 * half, 2, cols), BF16), ((edge + 16, LANES), BF16), ((4 * rows - edge, LANES), BF16),
            (angle_freq.shape[::-1], F32),
        ],
        (slices, angle_freq.T), hbm=(0, 1), outs_outside=(0,),
        scratch=[((2, rows, 2, LANES), BF16), pltpu.SemaphoreType.DMA((4,))],
    )
    (early,) = call(
        frequencies_kernel, [((edge + 16, LANES), BF16)], (table, chosen, early), scalars=(1,), aliases={2: 0},
    )
    outer_got = lax.ppermute(outer, "rows", outer_pairs)
    early_got = lax.ppermute(early, "ang", side_pairs)
    across_got = lax.ppermute(across, "ang", side_pairs)
    corner_got = lax.ppermute(early_got, "rows", outer_pairs)
    meas_outer, meas_inner = call(
        measured_kernel, [((rows // 2, 2, width), BF16)] * 2, (measured, across), hbm=(0,), outside=(1,),
        outs_outside=(0, 1), scratch=[pltpu.SemaphoreType.DMA((4,))],
    )
    outer_meas = lax.ppermute(meas_outer, "ang", side_pairs)
    inner_meas = lax.ppermute(meas_inner, "ang", side_pairs)
    phased = [
        ((4 * mid, 2 * wide), BF16), ((2 * wide, 4 * mid), BF16), ((8 * half, 4 * half), BF16), ((8, width), F32),
    ]
    row_real, row_imag, row_half, row_half_adj, row_adj, col_taps, split_far, split_meas, *partial = call(
        functools.partial(matrices_kernel, rows, length),
        [
            ((mid, 2 * wide), F32), ((mid, 2 * wide), F32), ((rows, 2 * rows), BF16), ((2 * rows, rows), BF16),
            ((2 * mid, 2 * rows), BF16), ((10, 4 * LANES, 2 * LANES), BF16), ((2 * rows, 2 * rows), BF16),
            ((rows, rows), BF16), *phased,
        ],
        (kernel_taps, early),
    )
    (inner,) = call(
        functools.partial(inner_edge_kernel, half), [((edge, width), BF16)], (slices, across_got, row_half), outside=(2,),
    )
    inner_got = lax.ppermute(inner, "rows", inner_pairs)
    row_near, row_near_adj, row_edge, waves = call(
        functools.partial(phases_kernel, half, length), phased, (row_real, row_imag, early_got, *partial),
        aliases={3: 0, 4: 1, 5: 2, 6: 3},
    )
    state = [
        ((2 * mid, width), F32), ((2, 2 * mid, width), BF16), ((2, 2 * mid, width), BF16),
        ((2, 2 * rows, width), BF16), ((2 * mid, width + LANES), F32), ((4 * mid, cols), BF16),
    ]
    leaving_shape = ((2, rows, width), BF16)
    far_slab, field, after, leaving = call(
        functools.partial(outer_forward_kernel, half),
        [*state[:3], leaving_shape],
        (slices, outer_got, early_got, across_got, corner_got, row_near, row_half, col_taps, split_far, waves),
        scratch=[
            ((2 * rows + 4 * half, width), BF16), ((2 * rows, width + LANES), BF16),
            ((2, 2 * rows, width + LANES), BF16), ((2, rows, width + LANES), BF16),
        ],
        flops=FORWARD_FLOPS,
    )
    back, far_sum, into, outer_sums = call(
        functools.partial(outer_backward_kernel, half),
        [*state[3:], ((edge, cols), BF16)],
        (
            far_slab, field, leaving, measured, outer_meas,
            row_half_adj, row_edge, col_taps, split_meas, waves,
        ),
        scratch=[((2, rows, width + LANES), BF16), ((2, 4 * half, width + LANES), BF16)],
        flops=BACKWARD_FLOPS,
    )
    outer_back = lax.ppermute(outer_sums, "rows", outer_pairs)
    (inner_parts,) = call(
        inner_measured_kernel, [((2, rows, width), F32)], (measured, inner_meas, split_meas, outer_sums), outside=(3,),
        flops=MEASURED_FLOPS,
    )
    far_slab, field, after, back, far_sum, into, inner_sums, inner_far = call(
        functools.partial(inner_kernel, half),
        [*state, ((4 * half, cols), BF16), ((2 * half, cols), BF16)],
        (
            slices, inner_got, across_got, inner_parts, far_slab, field, after, back, far_sum, into,
            row_near, row_half, row_adj, row_near_adj, col_taps, split_meas, waves,
        ),
        aliases={4: 0, 5: 1, 6: 2, 7: 3, 8: 4, 9: 5},
        scratch=[
            ((rows + 4 * half, width), BF16), ((4 * half, width + LANES), BF16),
            ((2, 4 * half, width + LANES), BF16), ((2, rows, width + LANES), BF16), leaving_shape,
            ((2, rows, width + LANES), BF16), ((2, 2 * rows, width + LANES), BF16),
        ],
        flops=INNER_FLOPS,
    )
    inner_back = lax.ppermute(inner_sums, "rows", inner_pairs)
    inner_far_back = lax.ppermute(inner_far, "rows", inner_pairs)
    near_sum, far_own = call(
        functools.partial(sums_kernel, half), [((2 * rows, cols), F32), ((2, rows, cols), F32)],
        (into, far_sum, row_near_adj),
    )
    near, far = call(
        functools.partial(inner_sums_kernel, half), [((rows, 2, cols), F32)] * 2,
        (near_sum, far_own, inner_back, inner_far_back), outs_outside=(0, 1),
        scratch=[((2 * half, 2, cols), F32), ((rows - half, 2, cols), F32), pltpu.SemaphoreType.DMA((2,))],
    )
    near, far = call(
        functools.partial(finish_kernel, half), [((rows, 2, cols), F32)] * 2,
        (near, far, near_sum, far_own, outer_back), outside=(0, 1), outs_outside=(0, 1), aliases={0: 0, 1: 1},
        scratch=[((2 * half, 2, cols), F32), ((half, 2, cols), F32), pltpu.SemaphoreType.DMA((3,))],
    )
    return near, far


def with_halo(block, sides, width):
    for axis, dim in sides:
        count = lax.axis_size(axis)
        forward = [(i, i + 1) for i in range(count - 1)]
        backward = [(target, source) for source, target in forward]
        low = lax.ppermute(
            lax.slice_in_dim(block, block.shape[dim] - width, None, axis=dim), axis, forward
        )
        high = lax.ppermute(lax.slice_in_dim(block, 0, width, axis=dim), axis, backward)
        block = jnp.concatenate([low, block, high], axis=dim)
    return block


def toeplitz(row_taps, out_width):
    tap_count = row_taps.shape[0]
    window = out_width + tap_count - 1
    padded = jnp.concatenate([row_taps, jnp.zeros((out_width,), row_taps.dtype)])
    tiled = jnp.tile(padded, out_width)[: out_width * window]
    return tiled.reshape(out_width, window).T


def kernel_pair(kernel_taps, out_width):
    return jnp.concatenate(
        [toeplitz(kernel_taps[0], out_width), toeplitz(kernel_taps[1], out_width)], axis=1
    )


def adjoint_taps(kernel_taps):
    return jnp.stack([kernel_taps[0][::-1], -kernel_taps[1][::-1]])


def correlate_columns(field, kernel):
    window, doubled = kernel.shape
    tile_len = doubled // 2
    half_taps = (window - tile_len) // 2
    leading, comps, length = field.shape
    blocks = length // tile_len
    padded = jnp.pad(field, ((0, 0), (0, 0), (half_taps, tile_len - half_taps)))
    main_part = padded[:, :, :length].reshape(leading, comps, blocks, tile_len)
    tail_part = padded[:, :, tile_len : tile_len + length].reshape(
        leading, comps, blocks, tile_len
    )[..., : 2 * half_taps]
    windows = jnp.concatenate([main_part, tail_part], axis=3)
    product = jnp.einsum("rpnw,wk->rpnk", windows, kernel, preferred_element_type=jnp.float32)
    real_part = product[:, 0, :, :tile_len] - product[:, 1, :, tile_len:]
    imag_part = product[:, 0, :, tile_len:] + product[:, 1, :, :tile_len]
    return (
        jnp.stack([real_part, imag_part], axis=1)
        .reshape(leading, comps, length)
        .astype(jnp.bfloat16)
    )


def band_rows(padded, band):
    out_rows = band.shape[1] // 2
    product = jnp.einsum("jpc,jk->kpc", padded, band, preferred_element_type=jnp.float32)
    real_part = product[:out_rows, 0] - product[out_rows:, 1]
    imag_part = product[out_rows:, 0] + product[:out_rows, 1]
    return jnp.stack([real_part, imag_part], axis=1).astype(jnp.bfloat16)


def complex_times(left, right):
    left = left.astype(jnp.float32)
    right = right.astype(jnp.float32)
    real_part = left[:, 0] * right[:, 0] - left[:, 1] * right[:, 1]
    imag_part = left[:, 0] * right[:, 1] + left[:, 1] * right[:, 0]
    return jnp.stack([real_part, imag_part], axis=1)


def conjugate_times(left, right):
    left = left.astype(jnp.float32)
    right = right.astype(jnp.float32)
    real_part = left[:, 0] * right[:, 0] + left[:, 1] * right[:, 1]
    imag_part = left[:, 0] * right[:, 1] - left[:, 1] * right[:, 0]
    return jnp.stack([real_part, imag_part], axis=1)


def incident(freq, row_pos, col_pos, length):
    scale = 2.0 * math.pi / length
    phase = scale * (freq[0] * row_pos[:, None] + freq[1] * col_pos[None, :])
    return jnp.stack([jnp.cos(phase), jnp.sin(phase)], axis=1)


def local(measured, slices, kernel_taps, angle_freq, chosen):
    rows_dev = measured.shape[1]
    length = measured.shape[3]
    half_taps = (kernel_taps.shape[1] - 1) // 2
    backward_taps = adjoint_taps(kernel_taps)
    forward_kernel = kernel_pair(kernel_taps, 128)
    adjoint_kernel = kernel_pair(backward_taps, 128)
    forward_band = kernel_pair(kernel_taps, rows_dev)
    adjoint_band = kernel_pair(backward_taps, rows_dev)
    gathered = lax.all_gather(slices, "ang", axis=3, tiled=True)
    near_slab = gathered[0]
    far_slab = gathered[1]
    start = lax.axis_index("rows") * rows_dev
    row_pos = (start + jnp.arange(rows_dev, dtype=jnp.int32)).astype(jnp.float32)
    col_pos = jnp.arange(length).astype(jnp.float32)
    onehot = (chosen[:, None] == jnp.arange(angle_freq.shape[0], dtype=jnp.int32)[None, :]).astype(
        jnp.float32
    )
    freqs = jnp.dot(onehot, angle_freq, precision=lax.Precision.HIGHEST)

    def along_rows(field, band):
        padded = with_halo(field, (("rows", 0),), half_taps)
        result = band_rows(padded, band)
        return result

    member = 0
    entering = incident(freqs[member], row_pos, col_pos, length)
    entry0 = complex_times(near_slab, entering).astype(jnp.bfloat16)
    inner = along_rows(correlate_columns(entry0, forward_kernel), forward_band)
    entry1 = complex_times(far_slab, inner).astype(jnp.bfloat16)
    exit_field = along_rows(correlate_columns(entry1, forward_kernel), forward_band)
    residue = (exit_field.astype(jnp.float32) - measured[member].astype(jnp.float32)).astype(
        jnp.bfloat16
    )
    back_far = correlate_columns(along_rows(residue, adjoint_band), adjoint_kernel)
    grad_far = conjugate_times(inner, back_far)
    carried_list = [conjugate_times(far_slab, back_far).astype(jnp.bfloat16)]
    member = 0
    entering = incident(freqs[member], row_pos, col_pos, length)
    back_near = correlate_columns(along_rows(carried_list[member], adjoint_band), adjoint_kernel)
    grad_near = conjugate_times(entering, back_near)
    near_total, far_total = (
        lax.psum_scatter(
            grad_near.astype(jnp.bfloat16), "ang", scatter_dimension=2, tiled=True
        ).astype(jnp.float32),
        lax.psum_scatter(
            grad_far.astype(jnp.bfloat16), "ang", scatter_dimension=2, tiled=True
        ).astype(jnp.float32),
    )
    return (near_total, far_total)


def pick(measured, slices, kernel_taps, angle_freq, chosen):
    rows, cols = slices.shape[1], slices.shape[3]
    taps = kernel_taps.shape[1]
    fits = (
        lax.axis_size("ang") == 2
        and lax.axis_size("rows") % 2 == 0
        and 2 * (taps - 1) == LANES
        and rows >= taps - 1
        and rows % LANES == 0
        and cols % (2 * LANES) == 0
    )
    run = columns_local if fits else local
    return run(measured, slices, kernel_taps, angle_freq, chosen)


def solution(mesh):
    return jax.shard_map(
        pick,
        mesh=mesh,
        in_specs=(P("ang", "rows", None, None), P(None, "rows", None, "ang"), P(), P(), P("ang")),
        out_specs=(P("rows", None, "ang"), P("rows", None, "ang")),
        check_vma=False,
    )
```

```python
import functools
import math

import jax
import jax.numpy as jnp
from jax import lax
from jax.experimental import pallas as pl
from jax.experimental.pallas import tpu as pltpu
from jax.sharding import PartitionSpec as P

LANES = 128
BF16 = jnp.bfloat16
INNER_FLOPS = 0
FORWARD_FLOPS = 24 * 10**8
BACKWARD_FLOPS = 10**9
MEASURED_FLOPS = 4 * 10**9
F32 = jnp.float32


def dot(left, right):
    return jnp.dot(left, right, preferred_element_type=F32)


def iota(shape, dim):
    return lax.broadcasted_iota(jnp.int32, shape, dim)


def lane_chunks(width, step=2 * LANES):
    return [(at, min(step, width - at)) for at in range(0, width, step)]


def edges_kernel(half, slices, angle_freq, outer, early, across, table, strips, sems):
    rows, cols = slices.shape[1], slices.shape[3]
    parity = lax.axis_index("rows") % 2
    side = lax.axis_index("ang")
    lane = pl.multiple_of((1 - side) * (cols - LANES), LANES)
    copies = [(angle_freq, table), (slices.at[:, :, :, pl.ds(lane, LANES)], strips)]
    for slab, at, size in ((0, 0, 2 * half), (1, 2 * half, half)):
        copies.append((slices.at[slab, pl.ds(parity * (rows - size), size)], outer.at[pl.ds(at, size)]))
    copies = [pltpu.make_async_copy(frm, to, sems.at[i]) for i, (frm, to) in enumerate(copies)]
    for copy in copies:
        copy.start()
    for copy in copies[:2]:
        copy.wait()
    begin, rest = 0, 0
    for slab, size in ((0, 2 * half), (1, half)):
        there = strips[slab, pl.ds(parity * (rows - size), size)]
        early[begin : begin + 2 * size] = there.reshape(2 * size, LANES)
        there = strips[slab, pl.ds((1 - parity) * size, rows - size)]
        across[rest : rest + 2 * (rows - size)] = there.reshape(2 * (rows - size), LANES)
        begin, rest = begin + 2 * size, rest + 2 * (rows - size)
    early[begin:] = jnp.zeros((16, LANES), BF16)
    for copy in copies[2:]:
        copy.wait()


def frequencies_kernel(table, chosen, early_in, early):
    row = iota((16, LANES), 0)
    block = jnp.zeros((16, LANES), F32)
    entry = jnp.where(iota(table.shape, 1) == chosen[0], table[...], 0.0)
    freqs = jnp.sum(entry, axis=1, keepdims=True)
    for part in range(2):
        rest = jnp.broadcast_to(freqs[part : part + 1], (16, LANES))
        for piece in range(3):
            rounded = rest.astype(BF16).astype(F32)
            block = jnp.where(row == 3 * part + piece, rounded, block)
            rest = rest - rounded
    early[early.shape[0] - 16 :] = block.astype(BF16)


def sent_frequencies(across):
    sent = across[across.shape[0] - 16 :].astype(F32)
    return [(sent[i : i + 1] + sent[i + 1 : i + 2] + sent[i + 2 : i + 3])[:, :1] for i in (0, 3)]


def inner_edge_kernel(half, slices, across, sent, edge):
    rows, cols = slices.shape[1], slices.shape[3]
    other = 1 - lax.axis_index("rows") % 2
    begin = 0
    for slab, size in ((0, 2 * half), (1, half)):
        there = slice(begin, begin + 2 * size)
        edge[there, :cols] = slices[slab, pl.ds(other * (rows - size), size)].reshape(2 * size, cols)
        begin += 2 * size
    edge[: 4 * half, cols:] = across[inner_rows(half, rows, other, 0)]
    edge[4 * half :, cols:] = across[inner_rows(half, rows, other, 1)]


def inner_rows(half, rows, other, slab):
    if slab == 0:
        return pl.ds(pl.multiple_of(other * (2 * rows - 8 * half), 16), 4 * half)
    return pl.ds(pl.multiple_of(2 * rows - 4 * half + other * (2 * rows - 4 * half), 16), 2 * half)


def measured_kernel(measured, sent, outer, inner, sems):
    size, cols = outer.shape[0], measured.shape[3] // 2
    parity = lax.axis_index("rows") % 2
    side = lax.axis_index("ang")
    copies = []
    for late, out in ((parity, outer), (1 - parity, inner)):
        for frm, at, lanes in (((1 - side) * cols, 0, cols), (cols - (1 - side) * LANES, cols, LANES)):
            here = pl.ds(pl.multiple_of(frm, LANES), lanes)
            there = measured.at[0, pl.ds(late * size, size), :, here]
            copies.append(pltpu.make_async_copy(there, out.at[:, :, at : at + lanes], sems.at[len(copies)]))
    for copy in copies:
        copy.start()
    for copy in copies:
        copy.wait()


def own_window(measured, late, at, size):
    half_rows, cols = measured.shape[1] // 2, measured.shape[3] // 2
    rows = pl.ds(late * half_rows, half_rows)
    first, second = (at, cols + at) if at < cols else (cols, cols - LANES)
    left = measured[0, rows, :, first : first + size].reshape(2 * half_rows, size)
    right = measured[0, rows, :, second : second + size].reshape(2 * half_rows, size)
    return jnp.where(lax.axis_index("ang") == 0, left, right)


def got_window(window, at, size):
    return window[:, :, at : at + size].reshape(2 * window.shape[0], size)


def skewed(base, count, stride):
    width = base.shape[1]
    return pltpu.roll(jnp.broadcast_to(base, (count, width)), 0, 1, stride=stride, stride_axis=0)


def matrices_kernel(
    rows, length, taps, across,
    row_real, row_imag, row_half, row_half_adj, row_adj, col_taps, split_far, split_meas,
    row_near, row_near_adj, row_edge, waves,
):
    count = taps.shape[1]
    half = (count - 1) // 2
    wide = rows + 4 * half
    mid = rows + 2 * half
    table = jnp.concatenate(
        [jnp.concatenate([taps[...], jnp.zeros((2, LANES - count), BF16)], axis=1),
         jnp.zeros((14, LANES), BF16)], axis=0,
    )

    def spread(width, place):
        tap = iota((LANES, width), 0)
        lane = iota((LANES, width), 1)
        hit = jnp.logical_and(lane == place(tap), tap < count)
        return dot(table, jnp.where(hit, 1.0, 0.0).astype(BF16))

    even = spread(2 * wide, lambda tap: 2 * tap)
    odd = spread(2 * wide, lambda tap: 2 * tap + 1)
    row_real[...] = skewed(even[0:1] - odd[1:2], mid, 2)
    row_imag[...] = skewed(even[1:2] + odd[0:1], mid, 2)

    add_phases(half, length, 0, across, row_real, row_imag, row_near, row_near_adj, row_edge, waves)

    low = spread(2 * mid, lambda tap: tap)
    high = spread(2 * mid, lambda tap: mid + tap)
    full = jnp.concatenate(
        [skewed(low[0:1] - high[1:2], rows, 1), skewed(low[1:2] + high[0:1], rows, 1)], axis=0
    )
    row_adj[...] = full.T.astype(BF16)
    low = spread(2 * rows, lambda tap: tap)
    high = spread(2 * rows, lambda tap: rows + tap)
    full = jnp.concatenate(
        [skewed(low[0:1] - high[1:2], rows // 2, 1), skewed(low[1:2] + high[0:1], rows // 2, 1)], axis=0
    )
    row_half[...] = full.astype(BF16)
    row_half_adj[...] = full.T.astype(BF16)

    window = 2 * LANES
    source = iota((window, LANES), 0)
    target = iota((window, LANES), 1)
    same_side = (source < LANES) == (target < LANES - half)
    left_only = source < window - half
    right_only = source >= LANES - half
    everything = source >= 0
    at = 0
    for adjoint in (False, True):
        for offset, masks in ((0, (everything, same_side)), (2 * half, (everything, left_only, right_only))):
            if adjoint:
                base = spread(window, lambda tap: (window - offset - (count - 1) + tap) % window)
            else:
                base = spread(window, lambda tap: (window - offset - tap) % window)
            re = skewed(base[0:1], window, 1)[:, :LANES]
            im = skewed(base[1:2], window, 1)[:, :LANES]
            im = -im if adjoint else im
            for mask in masks:
                mre = jnp.where(mask, re, 0.0).astype(BF16)
                mim = jnp.where(mask, im, 0.0).astype(BF16)
                col_taps[at, :window, :LANES] = mre
                col_taps[at, :window, LANES:] = mim
                col_taps[at, window:, :LANES] = -mim
                col_taps[at, window:, LANES:] = mre
                at += 1

    for out in (split_far, split_meas):
        size = out.shape[0]
        to, frm = iota((size, size), 0), iota((size, size), 1)
        out[...] = jnp.where(frm == 2 * (to % (size // 2)) + to // (size // 2), 1.0, 0.0).astype(BF16)


def add_phases(half, length, member, sent, row_real, row_imag, row_near, row_near_adj, row_edge, waves):
    mid, wide = row_real.shape[0], row_real.shape[1] // 2
    rows, cols = mid - 2 * half, waves.shape[1] - LANES
    side = lax.axis_index("ang")
    freq_row, freq_col = sent_frequencies(sent)
    scale = 2.0 * math.pi / length
    lane = iota((1, cols + LANES), 1)
    col = jnp.where(side == 0, lane, jnp.where(lane < cols, lane + cols, lane - LANES)).astype(F32)
    phase = scale * (freq_col * col)
    waves[2 * member : 2 * member + 1] = jnp.cos(phase)
    waves[2 * member + 1 : 2 * member + 2] = jnp.sin(phase)
    start = lax.axis_index("rows") * rows - 2 * half
    row = (start + iota((1, 2 * wide), 1) // 2).astype(F32)
    phase = scale * (freq_row * row)
    cos, sin = jnp.cos(phase), jnp.sin(phase)
    re = row_real[...] * cos - row_imag[...] * sin
    im = row_imag[...] * cos + row_real[...] * sin
    full = jnp.concatenate([re, im], axis=0)
    at = member * 2 * mid
    row_near[at : at + 2 * mid] = full.astype(BF16)
    row_near_adj[:, at : at + 2 * mid] = full.T.astype(BF16)
    for part in range(2):
        low, high = 4 * half, 2 * wide - 4 * half
        near = full[part * mid : part * mid + 2 * half, :low]
        far = full[part * mid + mid - 2 * half : (part + 1) * mid, high:]
        edge = jnp.where(lax.axis_index("rows") % 2 == 0, near, far)
        row_edge[(2 * member + part) * 2 * half : (2 * member + part + 1) * 2 * half] = edge.astype(BF16)


def phases_kernel(
    half, length, row_real, row_imag, across, near_in, near_adj_in, edge_in, waves_in,
    row_near, row_near_adj, row_edge, waves,
):
    add_phases(half, length, 1, across, row_real, row_imag, row_near, row_near_adj, row_edge, waves)


class Tiles:
    def __init__(self, cols):
        self.count = cols // LANES + 1
        self.width = self.count * LANES
        self.cut = self.count - 1 - lax.axis_index("ang")
        self.after = lax.rem(self.cut + 1, self.count)

    def ahead(self, j, base):
        return base + jnp.where(j == self.cut, 1, 0) if j >= self.count - 2 else base

    def back(self, j, base):
        if 0 < j < self.count - 2:
            return base
        return base + jnp.where(j == self.cut, 1, jnp.where(j == self.after, 2, 0))


def tile(j):
    return slice(j * LANES, (j + 1) * LANES)


def pair(j):
    return slice(j * LANES, (j + 2) * LANES)


class Rows:
    def __init__(self, first, count, parts):
        self.first, self.count, self.parts = first, count, parts

    def at(self, part, top=0):
        first = top + part * self.parts + self.first
        return pl.ds(first if isinstance(first, int) else pl.multiple_of(first, 16), self.count)

    def read(self, ref, lanes, top=0):
        return jnp.concatenate([ref[self.at(0, top), lanes], ref[self.at(1, top), lanes]], axis=0)

    def pairs(self, ref, j, top=0):
        return jnp.concatenate([ref[self.at(0, top), pair(j)], ref[self.at(1, top), pair(j)]], axis=1)

    def write(self, ref, lanes, both, top=0):
        ref[self.at(0, top), lanes] = both[: self.count]
        ref[self.at(1, top), lanes] = both[self.count :]


def column_step(tiles, index, col_taps, load, store, count, limit=256):
    groups, room = [], 0
    for j in range(count):
        which = index(j)
        plain = isinstance(which, int)
        if plain and groups and isinstance(groups[-1][0], int) and room > 0:
            groups[-1][1].append(j)
        else:
            groups.append((which, [j]))
            room = limit
        room -= load(j).shape[0] if plain else limit
    for which, members in groups:
        parts = [load(j) for j in members]
        size = parts[0].shape[0]
        y = dot(jnp.concatenate(parts, axis=0), col_taps[which])
        for at, j in enumerate(members):
            store(j, y[at * size : (at + 1) * size])


def forward_rows(
    tiles, part, leave, near_slab, near_first, far_slab, row_near, row_half, col_taps, waves, entry, field, after, narrow, leaving,
):
    mid, width = part.parts, tiles.width
    size = part.count
    block = near_slab.shape[0] // 2 - size
    for top in range(0, size, block):
        rows = Rows(part.first + top, block, mid)
        lefts = pl.ds(pl.multiple_of(near_first + 2 * top, LANES), 4 * block)
        left = jnp.concatenate(
            [row_near[rows.at(comp, member * 2 * mid), lefts] for member in range(2) for comp in range(2)], axis=0
        )
        for at, lanes in lane_chunks(width):
            here = slice(at, at + lanes)
            result = dot(left, near_slab[2 * top : 2 * top + 4 * block, here])
            for member in range(2):
                re = result[2 * member * block : (2 * member + 1) * block]
                im = result[(2 * member + 1) * block : (2 * member + 2) * block]
                vr, vi = waves[2 * member : 2 * member + 1, here], waves[2 * member + 1 : 2 * member + 2, here]
                entry[member, top : top + block, here] = (re * vr - im * vi).astype(BF16)
                entry[member, size + top : size + top + block, here] = (re * vi + im * vr).astype(BF16)
    entry[:, :, width:] = entry[:, :, :LANES]

    def load(j):
        return jnp.concatenate(
            [
                jnp.concatenate([entry[member, :size, pair(j)], entry[member, size:, pair(j)]], axis=1)
                for member in range(2)
            ],
            axis=0,
        )

    def store(j, y):
        far = part.read(far_slab, tile(j))
        sr, si = far[:size], far[size:]
        for member in range(2):
            re, im = y[member * size : (member + 1) * size, :LANES], y[member * size : (member + 1) * size, LANES:]
            part.write(field.at[member], tile(j), jnp.concatenate([re, im], axis=0).astype(BF16))
            both = jnp.concatenate([sr * re - si * im, sr * im + si * re], axis=0)
            part.write(after.at[member], tile(j), both.astype(BF16))

    column_step(tiles, lambda j: tiles.ahead(j, 0), col_taps, load, store, tiles.count)

    source = Rows(leave.first, 2 * leave.count, mid)
    for at, lanes in lane_chunks(width):
        here = slice(at, at + lanes)
        for member in range(2):
            y = dot(row_half[...], source.read(after.at[member], here)).astype(BF16)
            narrow[member, :, LANES + at : LANES + at + lanes] = y
    narrow[:, :, :LANES] = narrow[:, :, width:]
    size2 = leave.count

    def load2(j):
        return jnp.concatenate(
            [
                jnp.concatenate([narrow[member, :size2, pair(j)], narrow[member, size2:, pair(j)]], axis=1)
                for member in range(2)
            ],
            axis=0,
        )

    def store2(j, y):
        y = y.astype(BF16)
        for member in range(2):
            here = slice(member * size2, (member + 1) * size2)
            leaving[member, :size2, tile(j)] = y[here, :LANES]
            leaving[member, size2:, tile(j)] = y[here, LANES:]

    column_step(tiles, lambda j: tiles.back(j, 2), col_taps, load2, store2, tiles.count)


def residue_rows(tiles, members, measured, leave, col_taps, leaving, residue, back):
    size = leave.count
    for member in members:
        for at, lanes in lane_chunks(tiles.width):
            here = slice(at, at + lanes)
            leaves = leaving[member, :, here].astype(F32)
            residue[member, :, here] = (leaves - measured(member, at, lanes)).astype(BF16)
        residue[member, :, tiles.width :] = residue[member, :, :LANES]

    def load(j):
        return jnp.concatenate(
            [
                jnp.concatenate([residue[member, :size, pair(j)], residue[member, size:, pair(j)]], axis=1)
                for member in members
            ],
            axis=0,
        )

    def store(j, y):
        y = y.astype(BF16)
        for k, member in enumerate(members):
            here = slice(k * size, (k + 1) * size)
            leave.write(back.at[member], tile(j), jnp.concatenate([y[here, :LANES], y[here, LANES:]], axis=0))

    column_step(tiles, lambda j: tiles.ahead(j, 5), col_taps, load, store, tiles.count)


def backward_rows(tiles, members, part, left, right, field, far_slab, col_taps, waves, carry, far_sum, into):
    size, mid = part.count, part.parts
    for at, lanes in lane_chunks(tiles.width):
        here = slice(at, at + lanes)
        there = slice(LANES + at, LANES + at + lanes)
        far = part.read(far_slab, here)
        sr, si = far[:size], far[size:]
        total = None
        for member in members:
            y = dot(left, right(member, here))
            br, bi = y[:size], y[size:]
            inner = part.read(field.at[member], here).astype(F32)
            ir, ii = inner[:size], inner[size:]
            carry[member, :size, there] = (sr * br + si * bi).astype(BF16)
            carry[member, size:, there] = (sr * bi - si * br).astype(BF16)
            term = jnp.concatenate([ir * br + ii * bi, ir * bi - ii * br], axis=0)
            total = term if total is None else total + term
        part.write(far_sum, there, total)
    for member in members:
        carry[member, :, :LANES] = carry[member, :, tiles.width :]

    def load(j):
        return jnp.concatenate(
            [
                jnp.concatenate([carry[member, :size, pair(j)], carry[member, size:, pair(j)]], axis=1)
                for member in members
            ],
            axis=0,
        )

    def store(j, y):
        for k, member in enumerate(members):
            re, im = y[k * size : (k + 1) * size, :LANES], y[k * size : (k + 1) * size, LANES:]
            vr, vi = waves[2 * member : 2 * member + 1, tile(j)], waves[2 * member + 1 : 2 * member + 2, tile(j)]
            both = jnp.concatenate([re * vr + im * vi, im * vr - re * vi], axis=0)
            part.write(into, tile(j), both.astype(BF16), member * 2 * mid)

    column_step(tiles, lambda j: tiles.back(j, 7), col_taps, load, store, tiles.count - 1)


def split_rows(tiles, part, split, far_raw, far_slab, half):
    for at, lanes in lane_chunks(tiles.width):
        window = far_raw[:, at : at + lanes + LANES]
        part.write(far_slab, slice(at, at + lanes), dot(split[...], window[:, half : half + lanes]))


def far_margin(tiles, half, part, far_sum, sums):
    for j in range(tiles.count - 1):
        y = part.read(far_sum, pair(j))[:, LANES - half : 2 * LANES - half]
        sums[:, tile(j)] = y.astype(BF16)


def outer_forward_kernel(
    half,
    slices, outer, early, across, corner,
    row_near, row_half, col_taps, split_far, waves,
    far_slab, field, after, leaving,
    near_raw, far_raw, entry, narrow,
):
    rows, cols = slices.shape[1], slices.shape[3]
    tiles = Tiles(cols)
    width = tiles.width
    mid = rows + 2 * half
    parity = lax.axis_index("rows") % 2

    begin, rest = 0, 0
    for slab, ref, margin in ((0, near_raw, 4 * half), (1, far_raw, 2 * half)):
        own = ref.shape[0] - margin
        first = parity * (rows - own // 2)
        at = pl.ds(pl.multiple_of((1 - parity) * margin, 16), own)
        ref[at, :cols] = slices[slab, pl.ds(first, own // 2)].reshape(own, cols)
        at = pl.ds(pl.multiple_of(margin + parity * (own - 2 * margin), 16), margin)
        ref[at, cols:width] = early[begin : begin + margin]
        at = pl.ds(pl.multiple_of((1 - parity) * 2 * margin, 16), own - margin)
        frm = pl.ds(pl.multiple_of(rest + parity * (2 * rows - own), 16), own - margin)
        ref[at, cols:width] = across[frm]
        at = pl.ds(pl.multiple_of(parity * own, 16), margin)
        ref[at, :cols] = outer[begin // 2 : (begin + margin) // 2].reshape(margin, cols)
        ref[at, cols:width] = corner[begin : begin + margin]
        begin, rest = begin + margin, rest + 2 * rows - margin
    far_raw[:, width:] = far_raw[:, :LANES]

    part = Rows(parity * (rows // 2), rows, mid)
    source = Rows(parity * (rows // 2), rows // 2, mid)
    split_rows(tiles, part, split_far, far_raw, far_slab, half)
    forward_rows(
        tiles, part, source, near_raw, parity * 4 * half, far_slab, row_near, row_half, col_taps, waves, entry, field, after,
        narrow, leaving,
    )


def outer_backward_kernel(
    half,
    far_slab, field, leaving, measured, measured_got,
    row_half_adj, row_edge, col_taps, split_meas, waves,
    back, far_sum, into, sums,
    residue, carry,
):
    cols = into.shape[1]
    tiles = Tiles(cols)
    mid = far_sum.shape[0] // 2
    rows = mid - 2 * half
    parity = lax.axis_index("rows") % 2
    leave = Rows(parity * (rows // 2), rows // 2, rows)
    edge = Rows(parity * rows, 2 * half, mid)
    pick = Rows(parity * 2 * half, 2 * half, rows)
    windows = (functools.partial(own_window, measured, parity), functools.partial(got_window, measured_got))

    def parts(member, at, size):
        return dot(split_meas[...], windows[member](at, size))

    residue_rows(tiles, (0, 1), parts, leave, col_taps, leaving, residue, back)
    backward_rows(
        tiles, (0, 1), edge, pick.read(row_half_adj, slice(None)), lambda one, here: leave.read(back.at[one], here),
        field, far_slab, col_taps, waves, carry, far_sum, into,
    )
    far_sum[:, :LANES] = far_sum[:, tiles.width :]
    left = row_edge[...].T
    for at, size in lane_chunks(cols):
        here = slice(at, at + size)
        right = jnp.concatenate([edge.read(into, here, member * 2 * mid) for member in range(2)], axis=0)
        sums[: 4 * half, here] = dot(left, right).astype(BF16)
    far_margin(tiles, half, Rows(parity * (rows + half), half, mid), far_sum, sums.at[4 * half :])


def inner_measured_kernel(measured, measured_got, split_meas, sent, parts):
    other = 1 - lax.axis_index("rows") % 2
    windows = (functools.partial(own_window, measured, other), functools.partial(got_window, measured_got))
    for member in range(2):
        for at, size in lane_chunks(parts.shape[2]):
            parts[member, :, at : at + size] = dot(split_meas[...], windows[member](at, size))


def inner_kernel(
    half,
    slices, inner, across, measured, far_slab_in, field_in, after_in, back_in, far_in, into_in,
    row_near, row_half, row_adj, row_near_adj, col_taps, split_meas, waves,
    far_slab, field, after, back, far_sum, into, sums, far_sums,
    near_raw, far_raw, entry, narrow, leaving, residue, carry,
):
    cols = into.shape[1]
    tiles = Tiles(cols)
    mid = far_sum.shape[0] // 2
    rows = mid - 2 * half
    other = 1 - lax.axis_index("rows") % 2
    part = Rows(other * rows, 2 * half, mid)
    source = Rows(other * (rows // 2), rows // 2, mid)
    leave = Rows(other * (rows // 2), rows // 2, rows)

    for slab, ref, margin in ((0, near_raw, 4 * half), (1, far_raw, 2 * half)):
        own = ref.shape[0] - margin
        begin = 0 if slab == 0 else 4 * half
        first = other * (rows - own // 2)
        at = pl.ds(pl.multiple_of((1 - other) * margin, 16), own)
        ref[at, :cols] = slices[slab, pl.ds(first, own // 2)].reshape(own, cols)
        ref[at, cols : tiles.width] = across[inner_rows(half, rows, other, slab)]
        ref[pl.ds(pl.multiple_of(other * own, 16), margin), : tiles.width] = inner[begin : begin + margin]
    far_raw[:, tiles.width :] = far_raw[:, :LANES]

    split_rows(tiles, part, split_meas, far_raw, far_slab, half)
    forward_rows(
        tiles, part, source, near_raw, other * 2 * rows, far_slab, row_near, row_half, col_taps, waves, entry, field, after,
        narrow, leaving,
    )
    residue_rows(
        tiles, (0, 1), lambda member, at, size: measured[member, :, at : at + size], leave, col_taps, leaving,
        residue, back,
    )
    rest = Rows(other * 2 * half, rows, mid)
    left = jnp.concatenate([row_adj[rest.at(0), :], row_adj[rest.at(1), :]], axis=0)
    backward_rows(
        tiles, (0, 1), rest, left, lambda one, here: back[one, :, here], field, far_slab, col_taps, waves, carry,
        far_sum, into,
    )
    far_sum[:, :LANES] = far_sum[:, tiles.width :]
    at = pl.ds(pl.multiple_of(other * 2 * (rows + 2 * half), 16), 4 * half)
    for first, size in lane_chunks(cols):
        here = slice(first, first + size)
        sums[:, here] = dot(row_near_adj[at, :], into[:, here]).astype(BF16)
    far_margin(tiles, half, Rows(other * (rows + half), half, mid), far_sum, far_sums)


def sums_kernel(half, into, far_sum, row_near_adj, near, far):
    cols = into.shape[1]
    mid = far_sum.shape[0] // 2
    rows = mid - 2 * half
    margin = 4 * half
    for at, size in lane_chunks(cols):
        here = slice(at, at + size)
        near[:, here] = dot(row_near_adj[margin : margin + 2 * rows], into[:, here])
    for j in range(cols // LANES):
        for comp in range(2):
            top = comp * mid + half
            far[comp, :, tile(j)] = far_sum[top : top + rows, pair(j)][:, LANES - half : 2 * LANES - half]


def inner_sums_kernel(half, near_sum, far_sum, inner, inner_far, near, far, near_rows, far_rows, sems):
    rows, cols = near.shape[0], near.shape[2]
    other = 1 - lax.axis_index("rows") % 2
    at = pl.ds(pl.multiple_of(other * (2 * rows - 4 * half), 16), 4 * half)
    near_rows[...] = (near_sum[at] + inner[...].astype(F32)).reshape(2 * half, 2, cols)
    near_copy = pltpu.make_async_copy(near_rows, near.at[pl.ds(other * (rows - 2 * half), 2 * half)], sems.at[0])
    near_copy.start()
    at = pl.ds(pl.multiple_of(other * (rows - half), 16), half)
    for comp in range(2):
        far_rows[pl.ds((1 - other) * half, rows - 2 * half), comp, :] = far_sum[comp, half : rows - half]
        added = far_sum[comp, at] + inner_far[comp * half : (comp + 1) * half].astype(F32)
        far_rows[pl.ds(other * (rows - 2 * half), half), comp, :] = added
    far_copy = pltpu.make_async_copy(far_rows, far.at[pl.ds(other * half, rows - half)], sems.at[1])
    far_copy.start()
    near_copy.wait()
    far_copy.wait()


def finish_kernel(half, near_in, far_in, near_sum, far_sum, outer, near, far, near_rows, far_rows, sems):
    rows, cols = near.shape[0], near.shape[2]
    parity = lax.axis_index("rows") % 2
    margin = 4 * half
    at = pl.ds(pl.multiple_of(parity * (2 * rows - margin), 16), margin)
    copies = []
    for piece in range(2):
        at = pl.ds(pl.multiple_of(parity * (2 * rows - margin) + piece * 2 * half, 16), 2 * half)
        added = near_sum[at] + outer[piece * 2 * half : (piece + 1) * 2 * half].astype(F32)
        here = pl.ds(piece * half, half)
        near_rows[here] = added.reshape(half, 2, cols)
        there = near.at[pl.ds(parity * (rows - 2 * half) + piece * half, half)]
        copies.append(pltpu.make_async_copy(near_rows.at[here], there, sems.at[piece]))
        copies[-1].start()
    at = pl.ds(pl.multiple_of(parity * (rows - half), 16), half)
    for comp in range(2):
        got = outer[margin + comp * half : margin + (comp + 1) * half].astype(F32)
        far_rows[:, comp, :] = far_sum[comp, at] + got
    far_copy = pltpu.make_async_copy(far_rows, far.at[pl.ds(parity * (rows - half), half)], sems.at[2])
    far_copy.start()
    for copy in copies:
        copy.wait()
    far_copy.wait()


def call(kernel, outs, operands, hbm=(), scalars=(), outside=(), outs_outside=(), scratch=(), aliases=None, flops=0):
    def place(i):
        if i in scalars:
            return pltpu.SMEM
        return pltpu.HBM if i in hbm else pl.ANY if i in outside else pltpu.VMEM

    return pl.pallas_call(
        kernel,
        out_shape=[jax.ShapeDtypeStruct(shape, dtype) for shape, dtype in outs],
        in_specs=[pl.BlockSpec(memory_space=place(i)) for i in range(len(operands))],
        out_specs=[
            pl.BlockSpec(memory_space=pl.ANY if i in outs_outside else pltpu.VMEM) for i in range(len(outs))
        ],
        scratch_shapes=[one if not isinstance(one, tuple) else pltpu.VMEM(*one) for one in scratch],
        input_output_aliases=aliases or {},
        compiler_params=pltpu.CompilerParams(vmem_limit_bytes=20 * 2**20),
        cost_estimate=pl.CostEstimate(flops=flops, bytes_accessed=0, transcendentals=0),
    )(*(pltpu.with_memory_space_constraint(x, pltpu.HBM) if i in hbm else x for i, x in enumerate(operands)))


def columns_local(measured, slices, kernel_taps, angle_freq, chosen):
    rows, cols = slices.shape[1], slices.shape[3]
    length = measured.shape[3]
    half = (kernel_taps.shape[1] - 1) // 2
    wide, mid, width = rows + 4 * half, rows + 2 * half, cols + LANES
    count = lax.axis_size("rows")
    outer_pairs = [(i, j) for i in range(count) if 0 <= (j := i - 1 + 2 * (i % 2)) < count]
    inner_pairs = [(i, i + 1 - 2 * (i % 2)) for i in range(count)]
    side_pairs = [(i, 1 - i) for i in range(lax.axis_size("ang"))]
    edge = 6 * half
    outer, early, across, table = call(
        functools.partial(edges_kernel, half),
        [
            ((3 * half, 2, cols), BF16), ((edge + 16, LANES), BF16), ((4 * rows - edge, LANES), BF16),
            (angle_freq.shape[::-1], F32),
        ],
        (slices, angle_freq.T), hbm=(0, 1), outs_outside=(0,),
        scratch=[((2, rows, 2, LANES), BF16), pltpu.SemaphoreType.DMA((4,))],
    )
    (early,) = call(
        frequencies_kernel, [((edge + 16, LANES), BF16)], (table, chosen, early), scalars=(1,), aliases={2: 0},
    )
    outer_got = lax.ppermute(outer, "rows", outer_pairs)
    early_got = lax.ppermute(early, "ang", side_pairs)
    across_got = lax.ppermute(across, "ang", side_pairs)
    corner_got = lax.ppermute(early_got, "rows", outer_pairs)
    meas_outer, meas_inner = call(
        measured_kernel, [((rows // 2, 2, width), BF16)] * 2, (measured, across), hbm=(0,), outside=(1,),
        outs_outside=(0, 1), scratch=[pltpu.SemaphoreType.DMA((4,))],
    )
    outer_meas = lax.ppermute(meas_outer, "ang", side_pairs)
    inner_meas = lax.ppermute(meas_inner, "ang", side_pairs)
    phased = [
        ((4 * mid, 2 * wide), BF16), ((2 * wide, 4 * mid), BF16), ((8 * half, 4 * half), BF16), ((8, width), F32),
    ]
    row_real, row_imag, row_half, row_half_adj, row_adj, col_taps, split_far, split_meas, *partial = call(
        functools.partial(matrices_kernel, rows, length),
        [
            ((mid, 2 * wide), F32), ((mid, 2 * wide), F32), ((rows, 2 * rows), BF16), ((2 * rows, rows), BF16),
            ((2 * mid, 2 * rows), BF16), ((10, 4 * LANES, 2 * LANES), BF16), ((2 * rows, 2 * rows), BF16),
            ((rows, rows), BF16), *phased,
        ],
        (kernel_taps, early),
    )
    (inner,) = call(
        functools.partial(inner_edge_kernel, half), [((edge, width), BF16)], (slices, across_got, row_half), outside=(2,),
    )
    inner_got = lax.ppermute(inner, "rows", inner_pairs)
    row_near, row_near_adj, row_edge, waves = call(
        functools.partial(phases_kernel, half, length), phased, (row_real, row_imag, early_got, *partial),
        aliases={3: 0, 4: 1, 5: 2, 6: 3},
    )
    state = [
        ((2 * mid, width), F32), ((2, 2 * mid, width), BF16), ((2, 2 * mid, width), BF16),
        ((2, 2 * rows, width), BF16), ((2 * mid, width + LANES), F32), ((4 * mid, cols), BF16),
    ]
    leaving_shape = ((2, rows, width), BF16)
    far_slab, field, after, leaving = call(
        functools.partial(outer_forward_kernel, half),
        [*state[:3], leaving_shape],
        (slices, outer_got, early_got, across_got, corner_got, row_near, row_half, col_taps, split_far, waves),
        scratch=[
            ((2 * rows + 4 * half, width), BF16), ((2 * rows, width + LANES), BF16),
            ((2, 2 * rows, width + LANES), BF16), ((2, rows, width + LANES), BF16),
        ],
        flops=FORWARD_FLOPS,
    )
    back, far_sum, into, outer_sums = call(
        functools.partial(outer_backward_kernel, half),
        [*state[3:], ((edge, cols), BF16)],
        (
            far_slab, field, leaving, measured, outer_meas,
            row_half_adj, row_edge, col_taps, split_meas, waves,
        ),
        scratch=[((2, rows, width + LANES), BF16), ((2, 4 * half, width + LANES), BF16)],
        flops=BACKWARD_FLOPS,
    )
    outer_back = lax.ppermute(outer_sums, "rows", outer_pairs)
    (inner_parts,) = call(
        inner_measured_kernel, [((2, rows, width), F32)], (measured, inner_meas, split_meas, outer_sums), outside=(3,),
        flops=MEASURED_FLOPS,
    )
    far_slab, field, after, back, far_sum, into, inner_sums, inner_far = call(
        functools.partial(inner_kernel, half),
        [*state, ((4 * half, cols), BF16), ((2 * half, cols), BF16)],
        (
            slices, inner_got, across_got, inner_parts, far_slab, field, after, back, far_sum, into,
            row_near, row_half, row_adj, row_near_adj, col_taps, split_meas, waves,
        ),
        aliases={4: 0, 5: 1, 6: 2, 7: 3, 8: 4, 9: 5},
        scratch=[
            ((rows + 4 * half, width), BF16), ((4 * half, width + LANES), BF16),
            ((2, 4 * half, width + LANES), BF16), ((2, rows, width + LANES), BF16), leaving_shape,
            ((2, rows, width + LANES), BF16), ((2, 2 * rows, width + LANES), BF16),
        ],
        flops=INNER_FLOPS,
    )
    inner_back = lax.ppermute(inner_sums, "rows", inner_pairs)
    inner_far_back = lax.ppermute(inner_far, "rows", inner_pairs)
    near_sum, far_own = call(
        functools.partial(sums_kernel, half), [((2 * rows, cols), F32), ((2, rows, cols), F32)],
        (into, far_sum, row_near_adj),
    )
    near, far = call(
        functools.partial(inner_sums_kernel, half), [((rows, 2, cols), F32)] * 2,
        (near_sum, far_own, inner_back, inner_far_back), outs_outside=(0, 1),
        scratch=[((2 * half, 2, cols), F32), ((rows - half, 2, cols), F32), pltpu.SemaphoreType.DMA((2,))],
    )
    near, far = call(
        functools.partial(finish_kernel, half), [((rows, 2, cols), F32)] * 2,
        (near, far, near_sum, far_own, outer_back), outside=(0, 1), outs_outside=(0, 1), aliases={0: 0, 1: 1},
        scratch=[((2 * half, 2, cols), F32), ((half, 2, cols), F32), pltpu.SemaphoreType.DMA((3,))],
    )
    return near, far


def with_halo(block, sides, width):
    for axis, dim in sides:
        count = lax.axis_size(axis)
        forward = [(i, i + 1) for i in range(count - 1)]
        backward = [(target, source) for source, target in forward]
        low = lax.ppermute(
            lax.slice_in_dim(block, block.shape[dim] - width, None, axis=dim), axis, forward
        )
        high = lax.ppermute(lax.slice_in_dim(block, 0, width, axis=dim), axis, backward)
        block = jnp.concatenate([low, block, high], axis=dim)
    return block


def toeplitz(row_taps, out_width):
    tap_count = row_taps.shape[0]
    window = out_width + tap_count - 1
    padded = jnp.concatenate([row_taps, jnp.zeros((out_width,), row_taps.dtype)])
    tiled = jnp.tile(padded, out_width)[: out_width * window]
    return tiled.reshape(out_width, window).T


def kernel_pair(kernel_taps, out_width):
    return jnp.concatenate(
        [toeplitz(kernel_taps[0], out_width), toeplitz(kernel_taps[1], out_width)], axis=1
    )


def adjoint_taps(kernel_taps):
    return jnp.stack([kernel_taps[0][::-1], -kernel_taps[1][::-1]])


def correlate_columns(field, kernel):
    window, doubled = kernel.shape
    tile_len = doubled // 2
    half_taps = (window - tile_len) // 2
    leading, comps, length = field.shape
    blocks = length // tile_len
    padded = jnp.pad(field, ((0, 0), (0, 0), (half_taps, tile_len - half_taps)))
    main_part = padded[:, :, :length].reshape(leading, comps, blocks, tile_len)
    tail_part = padded[:, :, tile_len : tile_len + length].reshape(
        leading, comps, blocks, tile_len
    )[..., : 2 * half_taps]
    windows = jnp.concatenate([main_part, tail_part], axis=3)
    product = jnp.einsum("rpnw,wk->rpnk", windows, kernel, preferred_element_type=jnp.float32)
    real_part = product[:, 0, :, :tile_len] - product[:, 1, :, tile_len:]
    imag_part = product[:, 0, :, tile_len:] + product[:, 1, :, :tile_len]
    return (
        jnp.stack([real_part, imag_part], axis=1)
        .reshape(leading, comps, length)
        .astype(jnp.bfloat16)
    )


def band_rows(padded, band):
    out_rows = band.shape[1] // 2
    product = jnp.einsum("jpc,jk->kpc", padded, band, preferred_element_type=jnp.float32)
    real_part = product[:out_rows, 0] - product[out_rows:, 1]
    imag_part = product[out_rows:, 0] + product[:out_rows, 1]
    return jnp.stack([real_part, imag_part], axis=1).astype(jnp.bfloat16)


def complex_times(left, right):
    left = left.astype(jnp.float32)
    right = right.astype(jnp.float32)
    real_part = left[:, 0] * right[:, 0] - left[:, 1] * right[:, 1]
    imag_part = left[:, 0] * right[:, 1] + left[:, 1] * right[:, 0]
    return jnp.stack([real_part, imag_part], axis=1)


def conjugate_times(left, right):
    left = left.astype(jnp.float32)
    right = right.astype(jnp.float32)
    real_part = left[:, 0] * right[:, 0] + left[:, 1] * right[:, 1]
    imag_part = left[:, 0] * right[:, 1] - left[:, 1] * right[:, 0]
    return jnp.stack([real_part, imag_part], axis=1)


def incident(freq, row_pos, col_pos, length):
    scale = 2.0 * math.pi / length
    phase = scale * (freq[0] * row_pos[:, None] + freq[1] * col_pos[None, :])
    return jnp.stack([jnp.cos(phase), jnp.sin(phase)], axis=1)


def local(measured, slices, kernel_taps, angle_freq, chosen):
    rows_dev = measured.shape[1]
    length = measured.shape[3]
    half_taps = (kernel_taps.shape[1] - 1) // 2
    backward_taps = adjoint_taps(kernel_taps)
    forward_kernel = kernel_pair(kernel_taps, 128)
    adjoint_kernel = kernel_pair(backward_taps, 128)
    forward_band = kernel_pair(kernel_taps, rows_dev)
    adjoint_band = kernel_pair(backward_taps, rows_dev)
    gathered = lax.all_gather(slices, "ang", axis=3, tiled=True)
    near_slab = gathered[0]
    far_slab = gathered[1]
    start = lax.axis_index("rows") * rows_dev
    row_pos = (start + jnp.arange(rows_dev, dtype=jnp.int32)).astype(jnp.float32)
    col_pos = jnp.arange(length).astype(jnp.float32)
    onehot = (chosen[:, None] == jnp.arange(angle_freq.shape[0], dtype=jnp.int32)[None, :]).astype(
        jnp.float32
    )
    freqs = jnp.dot(onehot, angle_freq, precision=lax.Precision.HIGHEST)

    def along_rows(field, band):
        padded = with_halo(field, (("rows", 0),), half_taps)
        result = band_rows(padded, band)
        return result

    member = 0
    entering = incident(freqs[member], row_pos, col_pos, length)
    entry0 = complex_times(near_slab, entering).astype(jnp.bfloat16)
    inner = along_rows(correlate_columns(entry0, forward_kernel), forward_band)
    entry1 = complex_times(far_slab, inner).astype(jnp.bfloat16)
    exit_field = along_rows(correlate_columns(entry1, forward_kernel), forward_band)
    residue = (exit_field.astype(jnp.float32) - measured[member].astype(jnp.float32)).astype(
        jnp.bfloat16
    )
    back_far = correlate_columns(along_rows(residue, adjoint_band), adjoint_kernel)
    grad_far = conjugate_times(inner, back_far)
    carried_list = [conjugate_times(far_slab, back_far).astype(jnp.bfloat16)]
    member = 0
    entering = incident(freqs[member], row_pos, col_pos, length)
    back_near = correlate_columns(along_rows(carried_list[member], adjoint_band), adjoint_kernel)
    grad_near = conjugate_times(entering, back_near)
    near_total, far_total = (
        lax.psum_scatter(
            grad_near.astype(jnp.bfloat16), "ang", scatter_dimension=2, tiled=True
        ).astype(jnp.float32),
        lax.psum_scatter(
            grad_far.astype(jnp.bfloat16), "ang", scatter_dimension=2, tiled=True
        ).astype(jnp.float32),
    )
    return (near_total, far_total)


def pick(measured, slices, kernel_taps, angle_freq, chosen):
    rows, cols = slices.shape[1], slices.shape[3]
    taps = kernel_taps.shape[1]
    fits = (
        lax.axis_size("ang") == 2
        and lax.axis_size("rows") % 2 == 0
        and 2 * (taps - 1) == LANES
        and rows >= taps - 1
        and rows % LANES == 0
        and cols % (2 * LANES) == 0
    )
    run = columns_local if fits else local
    return run(measured, slices, kernel_taps, angle_freq, chosen)


def solution(mesh):
    return jax.shard_map(
        pick,
        mesh=mesh,
        in_specs=(P("ang", "rows", None, None), P(None, "rows", None, "ang"), P(), P(), P("ang")),
        out_specs=(P("rows", None, "ang"), P("rows", None, "ang")),
        check_vma=False,
    )
```

```python
import functools
import math

import jax
import jax.numpy as jnp
from jax import lax
from jax.experimental import pallas as pl
from jax.experimental.pallas import tpu as pltpu
from jax.sharding import PartitionSpec as P

LANES = 128
BF16 = jnp.bfloat16
INNER_FLOPS = 0
FORWARD_FLOPS = 24 * 10**8
BACKWARD_FLOPS = 10**9
MEASURED_FLOPS = 4 * 10**9
F32 = jnp.float32


def dot(left, right):
    return jnp.dot(left, right, preferred_element_type=F32)


def iota(shape, dim):
    return lax.broadcasted_iota(jnp.int32, shape, dim)


def lane_chunks(width, step=2 * LANES):
    return [(at, min(step, width - at)) for at in range(0, width, step)]


def edges_kernel(half, slices, angle_freq, outer, early, across, table, strips, sems):
    rows, cols = slices.shape[1], slices.shape[3]
    parity = lax.axis_index("rows") % 2
    side = lax.axis_index("ang")
    lane = pl.multiple_of((1 - side) * (cols - LANES), LANES)
    copies = [(angle_freq, table), (slices.at[:, :, :, pl.ds(lane, LANES)], strips)]
    for slab, at, size in ((0, 0, 2 * half), (1, 2 * half, half)):
        copies.append((slices.at[slab, pl.ds(parity * (rows - size), size)], outer.at[pl.ds(at, size)]))
    copies = [pltpu.make_async_copy(frm, to, sems.at[i]) for i, (frm, to) in enumerate(copies)]
    for copy in copies:
        copy.start()
    for copy in copies[:2]:
        copy.wait()
    begin, rest = 0, 0
    for slab, size in ((0, 2 * half), (1, half)):
        there = strips[slab, pl.ds(parity * (rows - size), size)]
        early[begin : begin + 2 * size] = there.reshape(2 * size, LANES)
        there = strips[slab, pl.ds((1 - parity) * size, rows - size)]
        across[rest : rest + 2 * (rows - size)] = there.reshape(2 * (rows - size), LANES)
        begin, rest = begin + 2 * size, rest + 2 * (rows - size)
    early[begin:] = jnp.zeros((16, LANES), BF16)
    for copy in copies[2:]:
        copy.wait()


def frequencies_kernel(table, chosen, early_in, measured, early):
    row = iota((16, LANES), 0)
    block = jnp.zeros((16, LANES), F32)
    entry = jnp.where(iota(table.shape, 1) == chosen[0], table[...], 0.0)
    freqs = jnp.sum(entry, axis=1, keepdims=True)
    for part in range(2):
        rest = jnp.broadcast_to(freqs[part : part + 1], (16, LANES))
        for piece in range(3):
            rounded = rest.astype(BF16).astype(F32)
            block = jnp.where(row == 3 * part + piece, rounded, block)
            rest = rest - rounded
    early[early.shape[0] - 16 :] = block.astype(BF16)


def sent_frequencies(across):
    sent = across[across.shape[0] - 16 :].astype(F32)
    return [(sent[i : i + 1] + sent[i + 1 : i + 2] + sent[i + 2 : i + 3])[:, :1] for i in (0, 3)]


def inner_edge_kernel(half, slices, across, sent, edge):
    rows, cols = slices.shape[1], slices.shape[3]
    other = 1 - lax.axis_index("rows") % 2
    begin = 0
    for slab, size in ((0, 2 * half), (1, half)):
        there = slice(begin, begin + 2 * size)
        edge[there, :cols] = slices[slab, pl.ds(other * (rows - size), size)].reshape(2 * size, cols)
        begin += 2 * size
    edge[: 4 * half, cols:] = across[inner_rows(half, rows, other, 0)]
    edge[4 * half :, cols:] = across[inner_rows(half, rows, other, 1)]


def inner_rows(half, rows, other, slab):
    if slab == 0:
        return pl.ds(pl.multiple_of(other * (2 * rows - 8 * half), 16), 4 * half)
    return pl.ds(pl.multiple_of(2 * rows - 4 * half + other * (2 * rows - 4 * half), 16), 2 * half)


def measured_kernel(measured, sent, outer, inner):
    size, cols = outer.shape[0] // 2, measured.shape[3] // 2
    parity = lax.axis_index("rows") % 2
    side = lax.axis_index("ang")
    for late, out in ((parity, outer), (1 - parity, inner)):
        rows = pl.ds(late * size, size)
        for at, first, second in ((0, cols, 0), (cols, cols - LANES, cols)):
            lanes = cols if at == 0 else LANES
            left = measured[0, rows, :, first : first + lanes].reshape(2 * size, lanes)
            right = measured[0, rows, :, second : second + lanes].reshape(2 * size, lanes)
            out[:, at : at + lanes] = jnp.where(side == 0, left, right)


def own_window(measured, late, at, size):
    half_rows, cols = measured.shape[1] // 2, measured.shape[3] // 2
    rows = pl.ds(late * half_rows, half_rows)
    first, second = (at, cols + at) if at < cols else (cols, cols - LANES)
    left = measured[0, rows, :, first : first + size].reshape(2 * half_rows, size)
    right = measured[0, rows, :, second : second + size].reshape(2 * half_rows, size)
    return jnp.where(lax.axis_index("ang") == 0, left, right)


def got_window(window, at, size):
    return window[:, at : at + size]


def skewed(base, count, stride):
    width = base.shape[1]
    return pltpu.roll(jnp.broadcast_to(base, (count, width)), 0, 1, stride=stride, stride_axis=0)


def matrices_kernel(
    rows, length, taps, across,
    row_real, row_imag, row_half, row_half_adj, row_adj, col_taps, split_far, split_meas,
    row_near, row_near_adj, row_edge, waves,
):
    count = taps.shape[1]
    half = (count - 1) // 2
    wide = rows + 4 * half
    mid = rows + 2 * half
    table = jnp.concatenate(
        [jnp.concatenate([taps[...], jnp.zeros((2, LANES - count), BF16)], axis=1),
         jnp.zeros((14, LANES), BF16)], axis=0,
    )

    def spread(width, place):
        tap = iota((LANES, width), 0)
        lane = iota((LANES, width), 1)
        hit = jnp.logical_and(lane == place(tap), tap < count)
        return dot(table, jnp.where(hit, 1.0, 0.0).astype(BF16))

    even = spread(2 * wide, lambda tap: 2 * tap)
    odd = spread(2 * wide, lambda tap: 2 * tap + 1)
    row_real[...] = skewed(even[0:1] - odd[1:2], mid, 2)
    row_imag[...] = skewed(even[1:2] + odd[0:1], mid, 2)

    add_phases(half, length, 0, across, row_real, row_imag, row_near, row_near_adj, row_edge, waves)

    low = spread(2 * mid, lambda tap: tap)
    high = spread(2 * mid, lambda tap: mid + tap)
    full = jnp.concatenate(
        [skewed(low[0:1] - high[1:2], rows, 1), skewed(low[1:2] + high[0:1], rows, 1)], axis=0
    )
    row_adj[...] = full.T.astype(BF16)
    low = spread(2 * rows, lambda tap: tap)
    high = spread(2 * rows, lambda tap: rows + tap)
    full = jnp.concatenate(
        [skewed(low[0:1] - high[1:2], rows // 2, 1), skewed(low[1:2] + high[0:1], rows // 2, 1)], axis=0
    )
    row_half[...] = full.astype(BF16)
    row_half_adj[...] = full.T.astype(BF16)

    window = 2 * LANES
    source = iota((window, LANES), 0)
    target = iota((window, LANES), 1)
    same_side = (source < LANES) == (target < LANES - half)
    left_only = source < window - half
    right_only = source >= LANES - half
    everything = source >= 0
    at = 0
    for adjoint in (False, True):
        for offset, masks in ((0, (everything, same_side)), (2 * half, (everything, left_only, right_only))):
            if adjoint:
                base = spread(window, lambda tap: (window - offset - (count - 1) + tap) % window)
            else:
                base = spread(window, lambda tap: (window - offset - tap) % window)
            re = skewed(base[0:1], window, 1)[:, :LANES]
            im = skewed(base[1:2], window, 1)[:, :LANES]
            im = -im if adjoint else im
            for mask in masks:
                mre = jnp.where(mask, re, 0.0).astype(BF16)
                mim = jnp.where(mask, im, 0.0).astype(BF16)
                col_taps[at, :window, :LANES] = mre
                col_taps[at, :window, LANES:] = mim
                col_taps[at, window:, :LANES] = -mim
                col_taps[at, window:, LANES:] = mre
                at += 1

    for out in (split_far, split_meas):
        size = out.shape[0]
        to, frm = iota((size, size), 0), iota((size, size), 1)
        out[...] = jnp.where(frm == 2 * (to % (size // 2)) + to // (size // 2), 1.0, 0.0).astype(BF16)


def add_phases(half, length, member, sent, row_real, row_imag, row_near, row_near_adj, row_edge, waves):
    mid, wide = row_real.shape[0], row_real.shape[1] // 2
    rows, cols = mid - 2 * half, waves.shape[1] - LANES
    side = lax.axis_index("ang")
    freq_row, freq_col = sent_frequencies(sent)
    scale = 2.0 * math.pi / length
    lane = iota((1, cols + LANES), 1)
    col = jnp.where(side == 0, lane, jnp.where(lane < cols, lane + cols, lane - LANES)).astype(F32)
    phase = scale * (freq_col * col)
    waves[2 * member : 2 * member + 1] = jnp.cos(phase)
    waves[2 * member + 1 : 2 * member + 2] = jnp.sin(phase)
    start = lax.axis_index("rows") * rows - 2 * half
    row = (start + iota((1, 2 * wide), 1) // 2).astype(F32)
    phase = scale * (freq_row * row)
    cos, sin = jnp.cos(phase), jnp.sin(phase)
    re = row_real[...] * cos - row_imag[...] * sin
    im = row_imag[...] * cos + row_real[...] * sin
    full = jnp.concatenate([re, im], axis=0)
    at = member * 2 * mid
    row_near[at : at + 2 * mid] = full.astype(BF16)
    row_near_adj[:, at : at + 2 * mid] = full.T.astype(BF16)
    for part in range(2):
        low, high = 4 * half, 2 * wide - 4 * half
        near = full[part * mid : part * mid + 2 * half, :low]
        far = full[part * mid + mid - 2 * half : (part + 1) * mid, high:]
        edge = jnp.where(lax.axis_index("rows") % 2 == 0, near, far)
        row_edge[(2 * member + part) * 2 * half : (2 * member + part + 1) * 2 * half] = edge.astype(BF16)


def phases_kernel(
    half, length, row_real, row_imag, across, near_in, near_adj_in, edge_in, waves_in,
    row_near, row_near_adj, row_edge, waves,
):
    add_phases(half, length, 1, across, row_real, row_imag, row_near, row_near_adj, row_edge, waves)


class Tiles:
    def __init__(self, cols):
        self.count = cols // LANES + 1
        self.width = self.count * LANES
        self.cut = self.count - 1 - lax.axis_index("ang")
        self.after = lax.rem(self.cut + 1, self.count)

    def ahead(self, j, base):
        return base + jnp.where(j == self.cut, 1, 0) if j >= self.count - 2 else base

    def back(self, j, base):
        if 0 < j < self.count - 2:
            return base
        return base + jnp.where(j == self.cut, 1, jnp.where(j == self.after, 2, 0))


def tile(j):
    return slice(j * LANES, (j + 1) * LANES)


def pair(j):
    return slice(j * LANES, (j + 2) * LANES)


class Rows:
    def __init__(self, first, count, parts):
        self.first, self.count, self.parts = first, count, parts

    def at(self, part, top=0):
        first = top + part * self.parts + self.first
        return pl.ds(first if isinstance(first, int) else pl.multiple_of(first, 16), self.count)

    def read(self, ref, lanes, top=0):
        return jnp.concatenate([ref[self.at(0, top), lanes], ref[self.at(1, top), lanes]], axis=0)

    def pairs(self, ref, j, top=0):
        return jnp.concatenate([ref[self.at(0, top), pair(j)], ref[self.at(1, top), pair(j)]], axis=1)

    def write(self, ref, lanes, both, top=0):
        ref[self.at(0, top), lanes] = both[: self.count]
        ref[self.at(1, top), lanes] = both[self.count :]


def column_step(tiles, index, col_taps, load, store, count, limit=256):
    groups, room = [], 0
    for j in range(count):
        which = index(j)
        plain = isinstance(which, int)
        if plain and groups and isinstance(groups[-1][0], int) and room > 0:
            groups[-1][1].append(j)
        else:
            groups.append((which, [j]))
            room = limit
        room -= load(j).shape[0] if plain else limit
    for which, members in groups:
        parts = [load(j) for j in members]
        size = parts[0].shape[0]
        y = dot(jnp.concatenate(parts, axis=0), col_taps[which])
        for at, j in enumerate(members):
            store(j, y[at * size : (at + 1) * size])


def forward_rows(
    tiles, part, leave, near_slab, near_first, far_slab, row_near, row_half, col_taps, waves, entry, field, after, narrow, leaving,
):
    mid, width = part.parts, tiles.width
    size = part.count
    block = near_slab.shape[0] // 2 - size
    for top in range(0, size, block):
        rows = Rows(part.first + top, block, mid)
        lefts = pl.ds(pl.multiple_of(near_first + 2 * top, LANES), 4 * block)
        left = jnp.concatenate(
            [row_near[rows.at(comp, member * 2 * mid), lefts] for member in range(2) for comp in range(2)], axis=0
        )
        for at, lanes in lane_chunks(width):
            here = slice(at, at + lanes)
            result = dot(left, near_slab[2 * top : 2 * top + 4 * block, here])
            for member in range(2):
                re = result[2 * member * block : (2 * member + 1) * block]
                im = result[(2 * member + 1) * block : (2 * member + 2) * block]
                vr, vi = waves[2 * member : 2 * member + 1, here], waves[2 * member + 1 : 2 * member + 2, here]
                entry[member, top : top + block, here] = (re * vr - im * vi).astype(BF16)
                entry[member, size + top : size + top + block, here] = (re * vi + im * vr).astype(BF16)
    entry[:, :, width:] = entry[:, :, :LANES]

    def load(j):
        return jnp.concatenate(
            [
                jnp.concatenate([entry[member, :size, pair(j)], entry[member, size:, pair(j)]], axis=1)
                for member in range(2)
            ],
            axis=0,
        )

    def store(j, y):
        far = part.read(far_slab, tile(j))
        sr, si = far[:size], far[size:]
        for member in range(2):
            re, im = y[member * size : (member + 1) * size, :LANES], y[member * size : (member + 1) * size, LANES:]
            part.write(field.at[member], tile(j), jnp.concatenate([re, im], axis=0).astype(BF16))
            both = jnp.concatenate([sr * re - si * im, sr * im + si * re], axis=0)
            part.write(after.at[member], tile(j), both.astype(BF16))

    column_step(tiles, lambda j: tiles.ahead(j, 0), col_taps, load, store, tiles.count)

    source = Rows(leave.first, 2 * leave.count, mid)
    for at, lanes in lane_chunks(width):
        here = slice(at, at + lanes)
        for member in range(2):
            y = dot(row_half[...], source.read(after.at[member], here)).astype(BF16)
            narrow[member, :, LANES + at : LANES + at + lanes] = y
    narrow[:, :, :LANES] = narrow[:, :, width:]
    size2 = leave.count

    def load2(j):
        return jnp.concatenate(
            [
                jnp.concatenate([narrow[member, :size2, pair(j)], narrow[member, size2:, pair(j)]], axis=1)
                for member in range(2)
            ],
            axis=0,
        )

    def store2(j, y):
        y = y.astype(BF16)
        for member in range(2):
            here = slice(member * size2, (member + 1) * size2)
            leaving[member, :size2, tile(j)] = y[here, :LANES]
            leaving[member, size2:, tile(j)] = y[here, LANES:]

    column_step(tiles, lambda j: tiles.back(j, 2), col_taps, load2, store2, tiles.count)


def residue_rows(tiles, members, measured, leave, col_taps, leaving, residue, back):
    size = leave.count
    for member in members:
        for at, lanes in lane_chunks(tiles.width):
            here = slice(at, at + lanes)
            leaves = leaving[member, :, here].astype(F32)
            residue[member, :, here] = (leaves - measured(member, at, lanes)).astype(BF16)
        residue[member, :, tiles.width :] = residue[member, :, :LANES]

    def load(j):
        return jnp.concatenate(
            [
                jnp.concatenate([residue[member, :size, pair(j)], residue[member, size:, pair(j)]], axis=1)
                for member in members
            ],
            axis=0,
        )

    def store(j, y):
        y = y.astype(BF16)
        for k, member in enumerate(members):
            here = slice(k * size, (k + 1) * size)
            leave.write(back.at[member], tile(j), jnp.concatenate([y[here, :LANES], y[here, LANES:]], axis=0))

    column_step(tiles, lambda j: tiles.ahead(j, 5), col_taps, load, store, tiles.count)


def backward_rows(tiles, members, part, left, right, field, far_slab, col_taps, waves, carry, far_sum, into):
    size, mid = part.count, part.parts
    for at, lanes in lane_chunks(tiles.width):
        here = slice(at, at + lanes)
        there = slice(LANES + at, LANES + at + lanes)
        far = part.read(far_slab, here)
        sr, si = far[:size], far[size:]
        total = None
        for member in members:
            y = dot(left, right(member, here))
            br, bi = y[:size], y[size:]
            inner = part.read(field.at[member], here).astype(F32)
            ir, ii = inner[:size], inner[size:]
            carry[member, :size, there] = (sr * br + si * bi).astype(BF16)
            carry[member, size:, there] = (sr * bi - si * br).astype(BF16)
            term = jnp.concatenate([ir * br + ii * bi, ir * bi - ii * br], axis=0)
            total = term if total is None else total + term
        part.write(far_sum, there, total)
    for member in members:
        carry[member, :, :LANES] = carry[member, :, tiles.width :]

    def load(j):
        return jnp.concatenate(
            [
                jnp.concatenate([carry[member, :size, pair(j)], carry[member, size:, pair(j)]], axis=1)
                for member in members
            ],
            axis=0,
        )

    def store(j, y):
        for k, member in enumerate(members):
            re, im = y[k * size : (k + 1) * size, :LANES], y[k * size : (k + 1) * size, LANES:]
            vr, vi = waves[2 * member : 2 * member + 1, tile(j)], waves[2 * member + 1 : 2 * member + 2, tile(j)]
            both = jnp.concatenate([re * vr + im * vi, im * vr - re * vi], axis=0)
            part.write(into, tile(j), both.astype(BF16), member * 2 * mid)

    column_step(tiles, lambda j: tiles.back(j, 7), col_taps, load, store, tiles.count - 1)


def split_rows(tiles, part, split, far_raw, far_slab, half):
    for at, lanes in lane_chunks(tiles.width):
        window = far_raw[:, at : at + lanes + LANES]
        part.write(far_slab, slice(at, at + lanes), dot(split[...], window[:, half : half + lanes]))


def far_margin(tiles, half, part, far_sum, sums):
    for j in range(tiles.count - 1):
        y = part.read(far_sum, pair(j))[:, LANES - half : 2 * LANES - half]
        sums[:, tile(j)] = y.astype(BF16)


def outer_forward_kernel(
    half,
    slices, outer, early, across, corner,
    row_near, row_half, col_taps, split_far, waves,
    far_slab, field, after, leaving,
    near_raw, far_raw, entry, narrow,
):
    rows, cols = slices.shape[1], slices.shape[3]
    tiles = Tiles(cols)
    width = tiles.width
    mid = rows + 2 * half
    parity = lax.axis_index("rows") % 2

    begin, rest = 0, 0
    for slab, ref, margin in ((0, near_raw, 4 * half), (1, far_raw, 2 * half)):
        own = ref.shape[0] - margin
        first = parity * (rows - own // 2)
        at = pl.ds(pl.multiple_of((1 - parity) * margin, 16), own)
        ref[at, :cols] = slices[slab, pl.ds(first, own // 2)].reshape(own, cols)
        at = pl.ds(pl.multiple_of(margin + parity * (own - 2 * margin), 16), margin)
        ref[at, cols:width] = early[begin : begin + margin]
        at = pl.ds(pl.multiple_of((1 - parity) * 2 * margin, 16), own - margin)
        frm = pl.ds(pl.multiple_of(rest + parity * (2 * rows - own), 16), own - margin)
        ref[at, cols:width] = across[frm]
        at = pl.ds(pl.multiple_of(parity * own, 16), margin)
        ref[at, :cols] = outer[begin // 2 : (begin + margin) // 2].reshape(margin, cols)
        ref[at, cols:width] = corner[begin : begin + margin]
        begin, rest = begin + margin, rest + 2 * rows - margin
    far_raw[:, width:] = far_raw[:, :LANES]

    part = Rows(parity * (rows // 2), rows, mid)
    source = Rows(parity * (rows // 2), rows // 2, mid)
    split_rows(tiles, part, split_far, far_raw, far_slab, half)
    forward_rows(
        tiles, part, source, near_raw, parity * 4 * half, far_slab, row_near, row_half, col_taps, waves, entry, field, after,
        narrow, leaving,
    )


def outer_backward_kernel(
    half,
    far_slab, field, leaving, measured, measured_got,
    row_half_adj, row_edge, col_taps, split_meas, waves,
    back, far_sum, into, sums,
    residue, carry,
):
    cols = into.shape[1]
    tiles = Tiles(cols)
    mid = far_sum.shape[0] // 2
    rows = mid - 2 * half
    parity = lax.axis_index("rows") % 2
    leave = Rows(parity * (rows // 2), rows // 2, rows)
    edge = Rows(parity * rows, 2 * half, mid)
    pick = Rows(parity * 2 * half, 2 * half, rows)
    windows = (functools.partial(own_window, measured, parity), functools.partial(got_window, measured_got))

    def parts(member, at, size):
        return dot(split_meas[...], windows[member](at, size))

    residue_rows(tiles, (0, 1), parts, leave, col_taps, leaving, residue, back)
    backward_rows(
        tiles, (0, 1), edge, pick.read(row_half_adj, slice(None)), lambda one, here: leave.read(back.at[one], here),
        field, far_slab, col_taps, waves, carry, far_sum, into,
    )
    far_sum[:, :LANES] = far_sum[:, tiles.width :]
    left = row_edge[...].T
    for at, size in lane_chunks(cols):
        here = slice(at, at + size)
        right = jnp.concatenate([edge.read(into, here, member * 2 * mid) for member in range(2)], axis=0)
        sums[: 4 * half, here] = dot(left, right).astype(BF16)
    far_margin(tiles, half, Rows(parity * (rows + half), half, mid), far_sum, sums.at[4 * half :])


def inner_measured_kernel(measured, measured_got, split_meas, sent, parts):
    other = 1 - lax.axis_index("rows") % 2
    windows = (functools.partial(own_window, measured, other), functools.partial(got_window, measured_got))
    for member in range(2):
        for at, size in lane_chunks(parts.shape[2]):
            parts[member, :, at : at + size] = dot(split_meas[...], windows[member](at, size))


def inner_kernel(
    half,
    slices, inner, across, measured, far_slab_in, field_in, after_in, back_in, far_in, into_in,
    row_near, row_half, row_adj, row_near_adj, col_taps, split_meas, waves,
    far_slab, field, after, back, far_sum, into, sums, far_sums,
    near_raw, far_raw, entry, narrow, leaving, residue, carry,
):
    cols = into.shape[1]
    tiles = Tiles(cols)
    mid = far_sum.shape[0] // 2
    rows = mid - 2 * half
    other = 1 - lax.axis_index("rows") % 2
    part = Rows(other * rows, 2 * half, mid)
    source = Rows(other * (rows // 2), rows // 2, mid)
    leave = Rows(other * (rows // 2), rows // 2, rows)

    for slab, ref, margin in ((0, near_raw, 4 * half), (1, far_raw, 2 * half)):
        own = ref.shape[0] - margin
        begin = 0 if slab == 0 else 4 * half
        first = other * (rows - own // 2)
        at = pl.ds(pl.multiple_of((1 - other) * margin, 16), own)
        ref[at, :cols] = slices[slab, pl.ds(first, own // 2)].reshape(own, cols)
        ref[at, cols : tiles.width] = across[inner_rows(half, rows, other, slab)]
        ref[pl.ds(pl.multiple_of(other * own, 16), margin), : tiles.width] = inner[begin : begin + margin]
    far_raw[:, tiles.width :] = far_raw[:, :LANES]

    split_rows(tiles, part, split_meas, far_raw, far_slab, half)
    forward_rows(
        tiles, part, source, near_raw, other * 2 * rows, far_slab, row_near, row_half, col_taps, waves, entry, field, after,
        narrow, leaving,
    )
    residue_rows(
        tiles, (0, 1), lambda member, at, size: measured[member, :, at : at + size], leave, col_taps, leaving,
        residue, back,
    )
    rest = Rows(other * 2 * half, rows, mid)
    left = jnp.concatenate([row_adj[rest.at(0), :], row_adj[rest.at(1), :]], axis=0)
    backward_rows(
        tiles, (0, 1), rest, left, lambda one, here: back[one, :, here], field, far_slab, col_taps, waves, carry,
        far_sum, into,
    )
    far_sum[:, :LANES] = far_sum[:, tiles.width :]
    at = pl.ds(pl.multiple_of(other * 2 * (rows + 2 * half), 16), 4 * half)
    for first, size in lane_chunks(cols):
        here = slice(first, first + size)
        sums[:, here] = dot(row_near_adj[at, :], into[:, here]).astype(BF16)
    far_margin(tiles, half, Rows(other * (rows + half), half, mid), far_sum, far_sums)


def sums_kernel(half, into, far_sum, row_near_adj, near, far):
    cols = into.shape[1]
    mid = far_sum.shape[0] // 2
    rows = mid - 2 * half
    margin = 4 * half
    for at, size in lane_chunks(cols):
        here = slice(at, at + size)
        near[:, here] = dot(row_near_adj[margin : margin + 2 * rows], into[:, here])
    for j in range(cols // LANES):
        for comp in range(2):
            top = comp * mid + half
            far[comp, :, tile(j)] = far_sum[top : top + rows, pair(j)][:, LANES - half : 2 * LANES - half]


def inner_sums_kernel(half, near_sum, far_sum, inner, inner_far, near, far, near_rows, far_rows, sems):
    rows, cols = near.shape[0], near.shape[2]
    other = 1 - lax.axis_index("rows") % 2
    at = pl.ds(pl.multiple_of(other * (2 * rows - 4 * half), 16), 4 * half)
    near_rows[...] = (near_sum[at] + inner[...].astype(F32)).reshape(2 * half, 2, cols)
    near_copy = pltpu.make_async_copy(near_rows, near.at[pl.ds(other * (rows - 2 * half), 2 * half)], sems.at[0])
    near_copy.start()
    at = pl.ds(pl.multiple_of(other * (rows - half), 16), half)
    for comp in range(2):
        far_rows[pl.ds((1 - other) * half, rows - 2 * half), comp, :] = far_sum[comp, half : rows - half]
        added = far_sum[comp, at] + inner_far[comp * half : (comp + 1) * half].astype(F32)
        far_rows[pl.ds(other * (rows - 2 * half), half), comp, :] = added
    far_copy = pltpu.make_async_copy(far_rows, far.at[pl.ds(other * half, rows - half)], sems.at[1])
    far_copy.start()
    near_copy.wait()
    far_copy.wait()


def finish_kernel(half, near_in, far_in, near_sum, far_sum, outer, near, far, near_rows, far_rows, sems):
    rows, cols = near.shape[0], near.shape[2]
    parity = lax.axis_index("rows") % 2
    margin = 4 * half
    at = pl.ds(pl.multiple_of(parity * (2 * rows - margin), 16), margin)
    copies = []
    for piece in range(2):
        at = pl.ds(pl.multiple_of(parity * (2 * rows - margin) + piece * 2 * half, 16), 2 * half)
        added = near_sum[at] + outer[piece * 2 * half : (piece + 1) * 2 * half].astype(F32)
        here = pl.ds(piece * half, half)
        near_rows[here] = added.reshape(half, 2, cols)
        there = near.at[pl.ds(parity * (rows - 2 * half) + piece * half, half)]
        copies.append(pltpu.make_async_copy(near_rows.at[here], there, sems.at[piece]))
        copies[-1].start()
    at = pl.ds(pl.multiple_of(parity * (rows - half), 16), half)
    for comp in range(2):
        got = outer[margin + comp * half : margin + (comp + 1) * half].astype(F32)
        far_rows[:, comp, :] = far_sum[comp, at] + got
    far_copy = pltpu.make_async_copy(far_rows, far.at[pl.ds(parity * (rows - half), half)], sems.at[2])
    far_copy.start()
    for copy in copies:
        copy.wait()
    far_copy.wait()


def call(kernel, outs, operands, hbm=(), scalars=(), outside=(), outs_outside=(), scratch=(), aliases=None, flops=0):
    def place(i):
        if i in scalars:
            return pltpu.SMEM
        return pltpu.HBM if i in hbm else pl.ANY if i in outside else pltpu.VMEM

    return pl.pallas_call(
        kernel,
        out_shape=[jax.ShapeDtypeStruct(shape, dtype) for shape, dtype in outs],
        in_specs=[pl.BlockSpec(memory_space=place(i)) for i in range(len(operands))],
        out_specs=[
            pl.BlockSpec(memory_space=pl.ANY if i in outs_outside else pltpu.VMEM) for i in range(len(outs))
        ],
        scratch_shapes=[one if not isinstance(one, tuple) else pltpu.VMEM(*one) for one in scratch],
        input_output_aliases=aliases or {},
        compiler_params=pltpu.CompilerParams(vmem_limit_bytes=20 * 2**20),
        cost_estimate=pl.CostEstimate(flops=flops, bytes_accessed=0, transcendentals=0),
    )(*(pltpu.with_memory_space_constraint(x, pltpu.HBM) if i in hbm else x for i, x in enumerate(operands)))


def columns_local(measured, slices, kernel_taps, angle_freq, chosen):
    rows, cols = slices.shape[1], slices.shape[3]
    length = measured.shape[3]
    half = (kernel_taps.shape[1] - 1) // 2
    wide, mid, width = rows + 4 * half, rows + 2 * half, cols + LANES
    count = lax.axis_size("rows")
    outer_pairs = [(i, j) for i in range(count) if 0 <= (j := i - 1 + 2 * (i % 2)) < count]
    inner_pairs = [(i, i + 1 - 2 * (i % 2)) for i in range(count)]
    side_pairs = [(i, 1 - i) for i in range(lax.axis_size("ang"))]
    edge = 6 * half
    outer, early, across, table = call(
        functools.partial(edges_kernel, half),
        [
            ((3 * half, 2, cols), BF16), ((edge + 16, LANES), BF16), ((4 * rows - edge, LANES), BF16),
            (angle_freq.shape[::-1], F32),
        ],
        (slices, angle_freq.T), hbm=(0, 1), outs_outside=(0,),
        scratch=[((2, rows, 2, LANES), BF16), pltpu.SemaphoreType.DMA((4,))],
    )
    (early,) = call(
        frequencies_kernel, [((edge + 16, LANES), BF16)], (table, chosen, early, measured), scalars=(1,), aliases={2: 0},
    )
    outer_got = lax.ppermute(outer, "rows", outer_pairs)
    early_got = lax.ppermute(early, "ang", side_pairs)
    across_got = lax.ppermute(across, "ang", side_pairs)
    corner_got = lax.ppermute(early_got, "rows", outer_pairs)
    meas_outer, meas_inner = call(
        measured_kernel, [((rows, width), BF16)] * 2, (measured, across), outside=(1,),
    )
    outer_meas = lax.ppermute(meas_outer, "ang", side_pairs)
    inner_meas = lax.ppermute(meas_inner, "ang", side_pairs)
    phased = [
        ((4 * mid, 2 * wide), BF16), ((2 * wide, 4 * mid), BF16), ((8 * half, 4 * half), BF16), ((8, width), F32),
    ]
    row_real, row_imag, row_half, row_half_adj, row_adj, col_taps, split_far, split_meas, *partial = call(
        functools.partial(matrices_kernel, rows, length),
        [
            ((mid, 2 * wide), F32), ((mid, 2 * wide), F32), ((rows, 2 * rows), BF16), ((2 * rows, rows), BF16),
            ((2 * mid, 2 * rows), BF16), ((10, 4 * LANES, 2 * LANES), BF16), ((2 * rows, 2 * rows), BF16),
            ((rows, rows), BF16), *phased,
        ],
        (kernel_taps, early),
    )
    (inner,) = call(
        functools.partial(inner_edge_kernel, half), [((edge, width), BF16)], (slices, across_got, row_half), outside=(2,),
    )
    inner_got = lax.ppermute(inner, "rows", inner_pairs)
    row_near, row_near_adj, row_edge, waves = call(
        functools.partial(phases_kernel, half, length), phased, (row_real, row_imag, early_got, *partial),
        aliases={3: 0, 4: 1, 5: 2, 6: 3},
    )
    state = [
        ((2 * mid, width), F32), ((2, 2 * mid, width), BF16), ((2, 2 * mid, width), BF16),
        ((2, 2 * rows, width), BF16), ((2 * mid, width + LANES), F32), ((4 * mid, cols), BF16),
    ]
    leaving_shape = ((2, rows, width), BF16)
    far_slab, field, after, leaving = call(
        functools.partial(outer_forward_kernel, half),
        [*state[:3], leaving_shape],
        (slices, outer_got, early_got, across_got, corner_got, row_near, row_half, col_taps, split_far, waves),
        scratch=[
            ((2 * rows + 4 * half, width), BF16), ((2 * rows, width + LANES), BF16),
            ((2, 2 * rows, width + LANES), BF16), ((2, rows, width + LANES), BF16),
        ],
        flops=FORWARD_FLOPS,
    )
    back, far_sum, into, outer_sums = call(
        functools.partial(outer_backward_kernel, half),
        [*state[3:], ((edge, cols), BF16)],
        (
            far_slab, field, leaving, measured, outer_meas,
            row_half_adj, row_edge, col_taps, split_meas, waves,
        ),
        scratch=[((2, rows, width + LANES), BF16), ((2, 4 * half, width + LANES), BF16)],
        flops=BACKWARD_FLOPS,
    )
    outer_back = lax.ppermute(outer_sums, "rows", outer_pairs)
    (inner_parts,) = call(
        inner_measured_kernel, [((2, rows, width), F32)], (measured, inner_meas, split_meas, outer_sums), outside=(3,),
        flops=MEASURED_FLOPS,
    )
    far_slab, field, after, back, far_sum, into, inner_sums, inner_far = call(
        functools.partial(inner_kernel, half),
        [*state, ((4 * half, cols), BF16), ((2 * half, cols), BF16)],
        (
            slices, inner_got, across_got, inner_parts, far_slab, field, after, back, far_sum, into,
            row_near, row_half, row_adj, row_near_adj, col_taps, split_meas, waves,
        ),
        aliases={4: 0, 5: 1, 6: 2, 7: 3, 8: 4, 9: 5},
        scratch=[
            ((rows + 4 * half, width), BF16), ((4 * half, width + LANES), BF16),
            ((2, 4 * half, width + LANES), BF16), ((2, rows, width + LANES), BF16), leaving_shape,
            ((2, rows, width + LANES), BF16), ((2, 2 * rows, width + LANES), BF16),
        ],
        flops=INNER_FLOPS,
    )
    inner_back = lax.ppermute(inner_sums, "rows", inner_pairs)
    inner_far_back = lax.ppermute(inner_far, "rows", inner_pairs)
    near_sum, far_own = call(
        functools.partial(sums_kernel, half), [((2 * rows, cols), F32), ((2, rows, cols), F32)],
        (into, far_sum, row_near_adj),
    )
    near, far = call(
        functools.partial(inner_sums_kernel, half), [((rows, 2, cols), F32)] * 2,
        (near_sum, far_own, inner_back, inner_far_back), outs_outside=(0, 1),
        scratch=[((2 * half, 2, cols), F32), ((rows - half, 2, cols), F32), pltpu.SemaphoreType.DMA((2,))],
    )
    near, far = call(
        functools.partial(finish_kernel, half), [((rows, 2, cols), F32)] * 2,
        (near, far, near_sum, far_own, outer_back), outside=(0, 1), outs_outside=(0, 1), aliases={0: 0, 1: 1},
        scratch=[((2 * half, 2, cols), F32), ((half, 2, cols), F32), pltpu.SemaphoreType.DMA((3,))],
    )
    return near, far


def with_halo(block, sides, width):
    for axis, dim in sides:
        count = lax.axis_size(axis)
        forward = [(i, i + 1) for i in range(count - 1)]
        backward = [(target, source) for source, target in forward]
        low = lax.ppermute(
            lax.slice_in_dim(block, block.shape[dim] - width, None, axis=dim), axis, forward
        )
        high = lax.ppermute(lax.slice_in_dim(block, 0, width, axis=dim), axis, backward)
        block = jnp.concatenate([low, block, high], axis=dim)
    return block


def toeplitz(row_taps, out_width):
    tap_count = row_taps.shape[0]
    window = out_width + tap_count - 1
    padded = jnp.concatenate([row_taps, jnp.zeros((out_width,), row_taps.dtype)])
    tiled = jnp.tile(padded, out_width)[: out_width * window]
    return tiled.reshape(out_width, window).T


def kernel_pair(kernel_taps, out_width):
    return jnp.concatenate(
        [toeplitz(kernel_taps[0], out_width), toeplitz(kernel_taps[1], out_width)], axis=1
    )


def adjoint_taps(kernel_taps):
    return jnp.stack([kernel_taps[0][::-1], -kernel_taps[1][::-1]])


def correlate_columns(field, kernel):
    window, doubled = kernel.shape
    tile_len = doubled // 2
    half_taps = (window - tile_len) // 2
    leading, comps, length = field.shape
    blocks = length // tile_len
    padded = jnp.pad(field, ((0, 0), (0, 0), (half_taps, tile_len - half_taps)))
    main_part = padded[:, :, :length].reshape(leading, comps, blocks, tile_len)
    tail_part = padded[:, :, tile_len : tile_len + length].reshape(
        leading, comps, blocks, tile_len
    )[..., : 2 * half_taps]
    windows = jnp.concatenate([main_part, tail_part], axis=3)
    product = jnp.einsum("rpnw,wk->rpnk", windows, kernel, preferred_element_type=jnp.float32)
    real_part = product[:, 0, :, :tile_len] - product[:, 1, :, tile_len:]
    imag_part = product[:, 0, :, tile_len:] + product[:, 1, :, :tile_len]
    return (
        jnp.stack([real_part, imag_part], axis=1)
        .reshape(leading, comps, length)
        .astype(jnp.bfloat16)
    )


def band_rows(padded, band):
    out_rows = band.shape[1] // 2
    product = jnp.einsum("jpc,jk->kpc", padded, band, preferred_element_type=jnp.float32)
    real_part = product[:out_rows, 0] - product[out_rows:, 1]
    imag_part = product[out_rows:, 0] + product[:out_rows, 1]
    return jnp.stack([real_part, imag_part], axis=1).astype(jnp.bfloat16)


def complex_times(left, right):
    left = left.astype(jnp.float32)
    right = right.astype(jnp.float32)
    real_part = left[:, 0] * right[:, 0] - left[:, 1] * right[:, 1]
    imag_part = left[:, 0] * right[:, 1] + left[:, 1] * right[:, 0]
    return jnp.stack([real_part, imag_part], axis=1)


def conjugate_times(left, right):
    left = left.astype(jnp.float32)
    right = right.astype(jnp.float32)
    real_part = left[:, 0] * right[:, 0] + left[:, 1] * right[:, 1]
    imag_part = left[:, 0] * right[:, 1] - left[:, 1] * right[:, 0]
    return jnp.stack([real_part, imag_part], axis=1)


def incident(freq, row_pos, col_pos, length):
    scale = 2.0 * math.pi / length
    phase = scale * (freq[0] * row_pos[:, None] + freq[1] * col_pos[None, :])
    return jnp.stack([jnp.cos(phase), jnp.sin(phase)], axis=1)


def local(measured, slices, kernel_taps, angle_freq, chosen):
    rows_dev = measured.shape[1]
    length = measured.shape[3]
    half_taps = (kernel_taps.shape[1] - 1) // 2
    backward_taps = adjoint_taps(kernel_taps)
    forward_kernel = kernel_pair(kernel_taps, 128)
    adjoint_kernel = kernel_pair(backward_taps, 128)
    forward_band = kernel_pair(kernel_taps, rows_dev)
    adjoint_band = kernel_pair(backward_taps, rows_dev)
    gathered = lax.all_gather(slices, "ang", axis=3, tiled=True)
    near_slab = gathered[0]
    far_slab = gathered[1]
    start = lax.axis_index("rows") * rows_dev
    row_pos = (start + jnp.arange(rows_dev, dtype=jnp.int32)).astype(jnp.float32)
    col_pos = jnp.arange(length).astype(jnp.float32)
    onehot = (chosen[:, None] == jnp.arange(angle_freq.shape[0], dtype=jnp.int32)[None, :]).astype(
        jnp.float32
    )
    freqs = jnp.dot(onehot, angle_freq, precision=lax.Precision.HIGHEST)

    def along_rows(field, band):
        padded = with_halo(field, (("rows", 0),), half_taps)
        result = band_rows(padded, band)
        return result

    member = 0
    entering = incident(freqs[member], row_pos, col_pos, length)
    entry0 = complex_times(near_slab, entering).astype(jnp.bfloat16)
    inner = along_rows(correlate_columns(entry0, forward_kernel), forward_band)
    entry1 = complex_times(far_slab, inner).astype(jnp.bfloat16)
    exit_field = along_rows(correlate_columns(entry1, forward_kernel), forward_band)
    residue = (exit_field.astype(jnp.float32) - measured[member].astype(jnp.float32)).astype(
        jnp.bfloat16
    )
    back_far = correlate_columns(along_rows(residue, adjoint_band), adjoint_kernel)
    grad_far = conjugate_times(inner, back_far)
    carried_list = [conjugate_times(far_slab, back_far).astype(jnp.bfloat16)]
    member = 0
    entering = incident(freqs[member], row_pos, col_pos, length)
    back_near = correlate_columns(along_rows(carried_list[member], adjoint_band), adjoint_kernel)
    grad_near = conjugate_times(entering, back_near)
    near_total, far_total = (
        lax.psum_scatter(
            grad_near.astype(jnp.bfloat16), "ang", scatter_dimension=2, tiled=True
        ).astype(jnp.float32),
        lax.psum_scatter(
            grad_far.astype(jnp.bfloat16), "ang", scatter_dimension=2, tiled=True
        ).astype(jnp.float32),
    )
    return (near_total, far_total)


def pick(measured, slices, kernel_taps, angle_freq, chosen):
    rows, cols = slices.shape[1], slices.shape[3]
    taps = kernel_taps.shape[1]
    fits = (
        lax.axis_size("ang") == 2
        and lax.axis_size("rows") % 2 == 0
        and 2 * (taps - 1) == LANES
        and rows == 2 * (taps - 1)
        and cols % (2 * LANES) == 0
    )
    run = columns_local if fits else local
    return run(measured, slices, kernel_taps, angle_freq, chosen)


def solution(mesh):
    return jax.shard_map(
        pick,
        mesh=mesh,
        in_specs=(P("ang", "rows", None, None), P(None, "rows", None, "ang"), P(), P(), P("ang")),
        out_specs=(P("rows", None, "ang"), P("rows", None, "ang")),
        check_vma=False,
    )
```

```python
import functools
import math

import jax
import jax.numpy as jnp
from jax import lax
from jax.experimental import pallas as pl
from jax.experimental.pallas import tpu as pltpu
from jax.sharding import PartitionSpec as P

LANES = 128
BF16 = jnp.bfloat16
INNER_FLOPS = 0
FORWARD_FLOPS = 24 * 10**8
BACKWARD_FLOPS = 10**9
MEASURED_FLOPS = 4 * 10**9
F32 = jnp.float32


def dot(left, right):
    return jnp.dot(left, right, preferred_element_type=F32)


def iota(shape, dim):
    return lax.broadcasted_iota(jnp.int32, shape, dim)


def lane_chunks(width, step=2 * LANES):
    return [(at, min(step, width - at)) for at in range(0, width, step)]


def edges_kernel(half, slices, angle_freq, outer, early, across, table, strips, sems):
    rows, cols = slices.shape[1], slices.shape[3]
    parity = lax.axis_index("rows") % 2
    side = lax.axis_index("ang")
    lane = pl.multiple_of((1 - side) * (cols - LANES), LANES)
    copies = [(angle_freq, table), (slices.at[:, :, :, pl.ds(lane, LANES)], strips)]
    for slab, at, size in ((0, 0, 2 * half), (1, 2 * half, half)):
        copies.append((slices.at[slab, pl.ds(parity * (rows - size), size)], outer.at[pl.ds(at, size)]))
    copies = [pltpu.make_async_copy(frm, to, sems.at[i]) for i, (frm, to) in enumerate(copies)]
    for copy in copies:
        copy.start()
    for copy in copies[:2]:
        copy.wait()
    begin, rest = 0, 0
    for slab, size in ((0, 2 * half), (1, half)):
        there = strips[slab, pl.ds(parity * (rows - size), size)]
        early[begin : begin + 2 * size] = there.reshape(2 * size, LANES)
        there = strips[slab, pl.ds((1 - parity) * size, rows - size)]
        across[rest : rest + 2 * (rows - size)] = there.reshape(2 * (rows - size), LANES)
        begin, rest = begin + 2 * size, rest + 2 * (rows - size)
    early[begin:] = jnp.zeros((16, LANES), BF16)
    for copy in copies[2:]:
        copy.wait()


def frequencies_kernel(table, chosen, early_in, measured, early):
    row = iota((16, LANES), 0)
    block = jnp.zeros((16, LANES), F32)
    entry = jnp.where(iota(table.shape, 1) == chosen[0], table[...], 0.0)
    freqs = jnp.sum(entry, axis=1, keepdims=True)
    for part in range(2):
        rest = jnp.broadcast_to(freqs[part : part + 1], (16, LANES))
        for piece in range(3):
            rounded = rest.astype(BF16).astype(F32)
            block = jnp.where(row == 3 * part + piece, rounded, block)
            rest = rest - rounded
    early[early.shape[0] - 16 :] = block.astype(BF16)


def sent_frequencies(across):
    sent = across[across.shape[0] - 16 :].astype(F32)
    return [(sent[i : i + 1] + sent[i + 1 : i + 2] + sent[i + 2 : i + 3])[:, :1] for i in (0, 3)]


def inner_edge_kernel(half, slices, across, sent, edge):
    rows, cols = slices.shape[1], slices.shape[3]
    other = 1 - lax.axis_index("rows") % 2
    begin = 0
    for slab, size in ((0, 2 * half), (1, half)):
        there = slice(begin, begin + 2 * size)
        edge[there, :cols] = slices[slab, pl.ds(other * (rows - size), size)].reshape(2 * size, cols)
        begin += 2 * size
    edge[: 4 * half, cols:] = across[inner_rows(half, rows, other, 0)]
    edge[4 * half :, cols:] = across[inner_rows(half, rows, other, 1)]


def inner_rows(half, rows, other, slab):
    if slab == 0:
        return pl.ds(pl.multiple_of(other * (2 * rows - 8 * half), 16), 4 * half)
    return pl.ds(pl.multiple_of(2 * rows - 4 * half + other * (2 * rows - 4 * half), 16), 2 * half)


def measured_kernel(measured, sent, ready, outer, inner):
    size, cols = outer.shape[0] // 2, measured.shape[3] // 2
    parity = lax.axis_index("rows") % 2
    side = lax.axis_index("ang")
    for late, out in ((parity, outer), (1 - parity, inner)):
        rows = pl.ds(late * size, size)
        for at, first, second in ((0, cols, 0), (cols, cols - LANES, cols)):
            lanes = cols if at == 0 else LANES
            left = measured[0, rows, :, first : first + lanes].reshape(2 * size, lanes)
            right = measured[0, rows, :, second : second + lanes].reshape(2 * size, lanes)
            out[:, at : at + lanes] = jnp.where(side == 0, left, right)


def own_window(measured, late, at, size):
    half_rows, cols = measured.shape[1] // 2, measured.shape[3] // 2
    rows = pl.ds(late * half_rows, half_rows)
    first, second = (at, cols + at) if at < cols else (cols, cols - LANES)
    left = measured[0, rows, :, first : first + size].reshape(2 * half_rows, size)
    right = measured[0, rows, :, second : second + size].reshape(2 * half_rows, size)
    return jnp.where(lax.axis_index("ang") == 0, left, right)


def got_window(window, at, size):
    return window[:, at : at + size]


def skewed(base, count, stride):
    width = base.shape[1]
    return pltpu.roll(jnp.broadcast_to(base, (count, width)), 0, 1, stride=stride, stride_axis=0)


def matrices_kernel(
    rows, length, taps, across,
    row_real, row_imag, row_half, row_half_adj, row_adj, col_taps, split_far, split_meas,
    row_near, row_near_adj, row_edge, waves,
):
    count = taps.shape[1]
    half = (count - 1) // 2
    wide = rows + 4 * half
    mid = rows + 2 * half
    table = jnp.concatenate(
        [jnp.concatenate([taps[...], jnp.zeros((2, LANES - count), BF16)], axis=1),
         jnp.zeros((14, LANES), BF16)], axis=0,
    )

    def spread(width, place):
        tap = iota((LANES, width), 0)
        lane = iota((LANES, width), 1)
        hit = jnp.logical_and(lane == place(tap), tap < count)
        return dot(table, jnp.where(hit, 1.0, 0.0).astype(BF16))

    even = spread(2 * wide, lambda tap: 2 * tap)
    odd = spread(2 * wide, lambda tap: 2 * tap + 1)
    row_real[...] = skewed(even[0:1] - odd[1:2], mid, 2)
    row_imag[...] = skewed(even[1:2] + odd[0:1], mid, 2)

    add_phases(half, length, 0, across, row_real, row_imag, row_near, row_near_adj, row_edge, waves)

    low = spread(2 * mid, lambda tap: tap)
    high = spread(2 * mid, lambda tap: mid + tap)
    full = jnp.concatenate(
        [skewed(low[0:1] - high[1:2], rows, 1), skewed(low[1:2] + high[0:1], rows, 1)], axis=0
    )
    row_adj[...] = full.T.astype(BF16)
    low = spread(2 * rows, lambda tap: tap)
    high = spread(2 * rows, lambda tap: rows + tap)
    full = jnp.concatenate(
        [skewed(low[0:1] - high[1:2], rows // 2, 1), skewed(low[1:2] + high[0:1], rows // 2, 1)], axis=0
    )
    row_half[...] = full.astype(BF16)
    row_half_adj[...] = full.T.astype(BF16)

    window = 2 * LANES
    source = iota((window, LANES), 0)
    target = iota((window, LANES), 1)
    same_side = (source < LANES) == (target < LANES - half)
    left_only = source < window - half
    right_only = source >= LANES - half
    everything = source >= 0
    at = 0
    for adjoint in (False, True):
        for offset, masks in ((0, (everything, same_side)), (2 * half, (everything, left_only, right_only))):
            if adjoint:
                base = spread(window, lambda tap: (window - offset - (count - 1) + tap) % window)
            else:
                base = spread(window, lambda tap: (window - offset - tap) % window)
            re = skewed(base[0:1], window, 1)[:, :LANES]
            im = skewed(base[1:2], window, 1)[:, :LANES]
            im = -im if adjoint else im
            for mask in masks:
                mre = jnp.where(mask, re, 0.0).astype(BF16)
                mim = jnp.where(mask, im, 0.0).astype(BF16)
                col_taps[at, :window, :LANES] = mre
                col_taps[at, :window, LANES:] = mim
                col_taps[at, window:, :LANES] = -mim
                col_taps[at, window:, LANES:] = mre
                at += 1

    for out in (split_far, split_meas):
        size = out.shape[0]
        to, frm = iota((size, size), 0), iota((size, size), 1)
        out[...] = jnp.where(frm == 2 * (to % (size // 2)) + to // (size // 2), 1.0, 0.0).astype(BF16)


def add_phases(half, length, member, sent, row_real, row_imag, row_near, row_near_adj, row_edge, waves):
    mid, wide = row_real.shape[0], row_real.shape[1] // 2
    rows, cols = mid - 2 * half, waves.shape[1] - LANES
    side = lax.axis_index("ang")
    freq_row, freq_col = sent_frequencies(sent)
    scale = 2.0 * math.pi / length
    lane = iota((1, cols + LANES), 1)
    col = jnp.where(side == 0, lane, jnp.where(lane < cols, lane + cols, lane - LANES)).astype(F32)
    phase = scale * (freq_col * col)
    waves[2 * member : 2 * member + 1] = jnp.cos(phase)
    waves[2 * member + 1 : 2 * member + 2] = jnp.sin(phase)
    start = lax.axis_index("rows") * rows - 2 * half
    row = (start + iota((1, 2 * wide), 1) // 2).astype(F32)
    phase = scale * (freq_row * row)
    cos, sin = jnp.cos(phase), jnp.sin(phase)
    re = row_real[...] * cos - row_imag[...] * sin
    im = row_imag[...] * cos + row_real[...] * sin
    full = jnp.concatenate([re, im], axis=0)
    at = member * 2 * mid
    row_near[at : at + 2 * mid] = full.astype(BF16)
    row_near_adj[:, at : at + 2 * mid] = full.T.astype(BF16)
    for part in range(2):
        low, high = 4 * half, 2 * wide - 4 * half
        near = full[part * mid : part * mid + 2 * half, :low]
        far = full[part * mid + mid - 2 * half : (part + 1) * mid, high:]
        edge = jnp.where(lax.axis_index("rows") % 2 == 0, near, far)
        row_edge[(2 * member + part) * 2 * half : (2 * member + part + 1) * 2 * half] = edge.astype(BF16)


def phases_kernel(
    half, length, row_real, row_imag, across, near_in, near_adj_in, edge_in, waves_in,
    row_near, row_near_adj, row_edge, waves,
):
    add_phases(half, length, 1, across, row_real, row_imag, row_near, row_near_adj, row_edge, waves)


class Tiles:
    def __init__(self, cols):
        self.count = cols // LANES + 1
        self.width = self.count * LANES
        self.cut = self.count - 1 - lax.axis_index("ang")
        self.after = lax.rem(self.cut + 1, self.count)

    def ahead(self, j, base):
        return base + jnp.where(j == self.cut, 1, 0) if j >= self.count - 2 else base

    def back(self, j, base):
        if 0 < j < self.count - 2:
            return base
        return base + jnp.where(j == self.cut, 1, jnp.where(j == self.after, 2, 0))


def tile(j):
    return slice(j * LANES, (j + 1) * LANES)


def pair(j):
    return slice(j * LANES, (j + 2) * LANES)


class Rows:
    def __init__(self, first, count, parts):
        self.first, self.count, self.parts = first, count, parts

    def at(self, part, top=0):
        first = top + part * self.parts + self.first
        return pl.ds(first if isinstance(first, int) else pl.multiple_of(first, 16), self.count)

    def read(self, ref, lanes, top=0):
        return jnp.concatenate([ref[self.at(0, top), lanes], ref[self.at(1, top), lanes]], axis=0)

    def pairs(self, ref, j, top=0):
        return jnp.concatenate([ref[self.at(0, top), pair(j)], ref[self.at(1, top), pair(j)]], axis=1)

    def write(self, ref, lanes, both, top=0):
        ref[self.at(0, top), lanes] = both[: self.count]
        ref[self.at(1, top), lanes] = both[self.count :]


def column_step(tiles, index, col_taps, load, store, count, limit=256):
    groups, room = [], 0
    for j in range(count):
        which = index(j)
        plain = isinstance(which, int)
        if plain and groups and isinstance(groups[-1][0], int) and room > 0:
            groups[-1][1].append(j)
        else:
            groups.append((which, [j]))
            room = limit
        room -= load(j).shape[0] if plain else limit
    for which, members in groups:
        parts = [load(j) for j in members]
        size = parts[0].shape[0]
        y = dot(jnp.concatenate(parts, axis=0), col_taps[which])
        for at, j in enumerate(members):
            store(j, y[at * size : (at + 1) * size])


def forward_rows(
    tiles, part, leave, near_slab, near_first, far_slab, row_near, row_half, col_taps, waves, entry, field, after, narrow, leaving,
):
    mid, width = part.parts, tiles.width
    size = part.count
    block = near_slab.shape[0] // 2 - size
    for top in range(0, size, block):
        rows = Rows(part.first + top, block, mid)
        lefts = pl.ds(pl.multiple_of(near_first + 2 * top, LANES), 4 * block)
        left = jnp.concatenate(
            [row_near[rows.at(comp, member * 2 * mid), lefts] for member in range(2) for comp in range(2)], axis=0
        )
        for at, lanes in lane_chunks(width):
            here = slice(at, at + lanes)
            result = dot(left, near_slab[2 * top : 2 * top + 4 * block, here])
            for member in range(2):
                re = result[2 * member * block : (2 * member + 1) * block]
                im = result[(2 * member + 1) * block : (2 * member + 2) * block]
                vr, vi = waves[2 * member : 2 * member + 1, here], waves[2 * member + 1 : 2 * member + 2, here]
                entry[member, top : top + block, here] = (re * vr - im * vi).astype(BF16)
                entry[member, size + top : size + top + block, here] = (re * vi + im * vr).astype(BF16)
    entry[:, :, width:] = entry[:, :, :LANES]

    def load(j):
        return jnp.concatenate(
            [
                jnp.concatenate([entry[member, :size, pair(j)], entry[member, size:, pair(j)]], axis=1)
                for member in range(2)
            ],
            axis=0,
        )

    def store(j, y):
        far = part.read(far_slab, tile(j))
        sr, si = far[:size], far[size:]
        for member in range(2):
            re, im = y[member * size : (member + 1) * size, :LANES], y[member * size : (member + 1) * size, LANES:]
            part.write(field.at[member], tile(j), jnp.concatenate([re, im], axis=0).astype(BF16))
            both = jnp.concatenate([sr * re - si * im, sr * im + si * re], axis=0)
            part.write(after.at[member], tile(j), both.astype(BF16))

    column_step(tiles, lambda j: tiles.ahead(j, 0), col_taps, load, store, tiles.count)

    source = Rows(leave.first, 2 * leave.count, mid)
    for at, lanes in lane_chunks(width):
        here = slice(at, at + lanes)
        for member in range(2):
            y = dot(row_half[...], source.read(after.at[member], here)).astype(BF16)
            narrow[member, :, LANES + at : LANES + at + lanes] = y
    narrow[:, :, :LANES] = narrow[:, :, width:]
    size2 = leave.count

    def load2(j):
        return jnp.concatenate(
            [
                jnp.concatenate([narrow[member, :size2, pair(j)], narrow[member, size2:, pair(j)]], axis=1)
                for member in range(2)
            ],
            axis=0,
        )

    def store2(j, y):
        y = y.astype(BF16)
        for member in range(2):
            here = slice(member * size2, (member + 1) * size2)
            leaving[member, :size2, tile(j)] = y[here, :LANES]
            leaving[member, size2:, tile(j)] = y[here, LANES:]

    column_step(tiles, lambda j: tiles.back(j, 2), col_taps, load2, store2, tiles.count)


def residue_rows(tiles, members, measured, leave, col_taps, leaving, residue, back):
    size = leave.count
    for member in members:
        for at, lanes in lane_chunks(tiles.width):
            here = slice(at, at + lanes)
            leaves = leaving[member, :, here].astype(F32)
            residue[member, :, here] = (leaves - measured(member, at, lanes)).astype(BF16)
        residue[member, :, tiles.width :] = residue[member, :, :LANES]

    def load(j):
        return jnp.concatenate(
            [
                jnp.concatenate([residue[member, :size, pair(j)], residue[member, size:, pair(j)]], axis=1)
                for member in members
            ],
            axis=0,
        )

    def store(j, y):
        y = y.astype(BF16)
        for k, member in enumerate(members):
            here = slice(k * size, (k + 1) * size)
            leave.write(back.at[member], tile(j), jnp.concatenate([y[here, :LANES], y[here, LANES:]], axis=0))

    column_step(tiles, lambda j: tiles.ahead(j, 5), col_taps, load, store, tiles.count)


def backward_rows(tiles, members, part, left, right, field, far_slab, col_taps, waves, carry, far_sum, into):
    size, mid = part.count, part.parts
    for at, lanes in lane_chunks(tiles.width):
        here = slice(at, at + lanes)
        there = slice(LANES + at, LANES + at + lanes)
        far = part.read(far_slab, here)
        sr, si = far[:size], far[size:]
        total = None
        for member in members:
            y = dot(left, right(member, here))
            br, bi = y[:size], y[size:]
            inner = part.read(field.at[member], here).astype(F32)
            ir, ii = inner[:size], inner[size:]
            carry[member, :size, there] = (sr * br + si * bi).astype(BF16)
            carry[member, size:, there] = (sr * bi - si * br).astype(BF16)
            term = jnp.concatenate([ir * br + ii * bi, ir * bi - ii * br], axis=0)
            total = term if total is None else total + term
        part.write(far_sum, there, total)
    for member in members:
        carry[member, :, :LANES] = carry[member, :, tiles.width :]

    def load(j):
        return jnp.concatenate(
            [
                jnp.concatenate([carry[member, :size, pair(j)], carry[member, size:, pair(j)]], axis=1)
                for member in members
            ],
            axis=0,
        )

    def store(j, y):
        for k, member in enumerate(members):
            re, im = y[k * size : (k + 1) * size, :LANES], y[k * size : (k + 1) * size, LANES:]
            vr, vi = waves[2 * member : 2 * member + 1, tile(j)], waves[2 * member + 1 : 2 * member + 2, tile(j)]
            both = jnp.concatenate([re * vr + im * vi, im * vr - re * vi], axis=0)
            part.write(into, tile(j), both.astype(BF16), member * 2 * mid)

    column_step(tiles, lambda j: tiles.back(j, 7), col_taps, load, store, tiles.count - 1)


def split_rows(tiles, part, split, far_raw, far_slab, half):
    for at, lanes in lane_chunks(tiles.width):
        window = far_raw[:, at : at + lanes + LANES]
        part.write(far_slab, slice(at, at + lanes), dot(split[...], window[:, half : half + lanes]))


def far_margin(tiles, half, part, far_sum, sums):
    for j in range(tiles.count - 1):
        y = part.read(far_sum, pair(j))[:, LANES - half : 2 * LANES - half]
        sums[:, tile(j)] = y.astype(BF16)


def outer_forward_kernel(
    half,
    slices, outer, early, across, corner,
    row_near, row_half, col_taps, split_far, waves,
    far_slab, field, after, leaving,
    near_raw, far_raw, entry, narrow,
):
    rows, cols = slices.shape[1], slices.shape[3]
    tiles = Tiles(cols)
    width = tiles.width
    mid = rows + 2 * half
    parity = lax.axis_index("rows") % 2

    begin, rest = 0, 0
    for slab, ref, margin in ((0, near_raw, 4 * half), (1, far_raw, 2 * half)):
        own = ref.shape[0] - margin
        first = parity * (rows - own // 2)
        at = pl.ds(pl.multiple_of((1 - parity) * margin, 16), own)
        ref[at, :cols] = slices[slab, pl.ds(first, own // 2)].reshape(own, cols)
        at = pl.ds(pl.multiple_of(margin + parity * (own - 2 * margin), 16), margin)
        ref[at, cols:width] = early[begin : begin + margin]
        at = pl.ds(pl.multiple_of((1 - parity) * 2 * margin, 16), own - margin)
        frm = pl.ds(pl.multiple_of(rest + parity * (2 * rows - own), 16), own - margin)
        ref[at, cols:width] = across[frm]
        at = pl.ds(pl.multiple_of(parity * own, 16), margin)
        ref[at, :cols] = outer[begin // 2 : (begin + margin) // 2].reshape(margin, cols)
        ref[at, cols:width] = corner[begin : begin + margin]
        begin, rest = begin + margin, rest + 2 * rows - margin
    far_raw[:, width:] = far_raw[:, :LANES]

    part = Rows(parity * (rows // 2), rows, mid)
    source = Rows(parity * (rows // 2), rows // 2, mid)
    split_rows(tiles, part, split_far, far_raw, far_slab, half)
    forward_rows(
        tiles, part, source, near_raw, parity * 4 * half, far_slab, row_near, row_half, col_taps, waves, entry, field, after,
        narrow, leaving,
    )


def outer_backward_kernel(
    half,
    far_slab, field, leaving, measured, measured_got,
    row_half_adj, row_edge, col_taps, split_meas, waves,
    back, far_sum, into, sums,
    residue, carry,
):
    cols = into.shape[1]
    tiles = Tiles(cols)
    mid = far_sum.shape[0] // 2
    rows = mid - 2 * half
    parity = lax.axis_index("rows") % 2
    leave = Rows(parity * (rows // 2), rows // 2, rows)
    edge = Rows(parity * rows, 2 * half, mid)
    pick = Rows(parity * 2 * half, 2 * half, rows)
    windows = (functools.partial(own_window, measured, parity), functools.partial(got_window, measured_got))

    def parts(member, at, size):
        return dot(split_meas[...], windows[member](at, size))

    residue_rows(tiles, (0, 1), parts, leave, col_taps, leaving, residue, back)
    backward_rows(
        tiles, (0, 1), edge, pick.read(row_half_adj, slice(None)), lambda one, here: leave.read(back.at[one], here),
        field, far_slab, col_taps, waves, carry, far_sum, into,
    )
    far_sum[:, :LANES] = far_sum[:, tiles.width :]
    left = row_edge[...].T
    for at, size in lane_chunks(cols):
        here = slice(at, at + size)
        right = jnp.concatenate([edge.read(into, here, member * 2 * mid) for member in range(2)], axis=0)
        sums[: 4 * half, here] = dot(left, right).astype(BF16)
    far_margin(tiles, half, Rows(parity * (rows + half), half, mid), far_sum, sums.at[4 * half :])


def inner_measured_kernel(measured, measured_got, split_meas, sent, parts):
    other = 1 - lax.axis_index("rows") % 2
    windows = (functools.partial(own_window, measured, other), functools.partial(got_window, measured_got))
    for member in range(2):
        for at, size in lane_chunks(parts.shape[2]):
            parts[member, :, at : at + size] = dot(split_meas[...], windows[member](at, size))


def inner_kernel(
    half,
    slices, inner, across, measured, far_slab_in, field_in, after_in, back_in, far_in, into_in,
    row_near, row_half, row_adj, row_near_adj, col_taps, split_meas, waves,
    far_slab, field, after, back, far_sum, into, sums, far_sums,
    near_raw, far_raw, entry, narrow, leaving, residue, carry,
):
    cols = into.shape[1]
    tiles = Tiles(cols)
    mid = far_sum.shape[0] // 2
    rows = mid - 2 * half
    other = 1 - lax.axis_index("rows") % 2
    part = Rows(other * rows, 2 * half, mid)
    source = Rows(other * (rows // 2), rows // 2, mid)
    leave = Rows(other * (rows // 2), rows // 2, rows)

    for slab, ref, margin in ((0, near_raw, 4 * half), (1, far_raw, 2 * half)):
        own = ref.shape[0] - margin
        begin = 0 if slab == 0 else 4 * half
        first = other * (rows - own // 2)
        at = pl.ds(pl.multiple_of((1 - other) * margin, 16), own)
        ref[at, :cols] = slices[slab, pl.ds(first, own // 2)].reshape(own, cols)
        ref[at, cols : tiles.width] = across[inner_rows(half, rows, other, slab)]
        ref[pl.ds(pl.multiple_of(other * own, 16), margin), : tiles.width] = inner[begin : begin + margin]
    far_raw[:, tiles.width :] = far_raw[:, :LANES]

    split_rows(tiles, part, split_meas, far_raw, far_slab, half)
    forward_rows(
        tiles, part, source, near_raw, other * 2 * rows, far_slab, row_near, row_half, col_taps, waves, entry, field, after,
        narrow, leaving,
    )
    residue_rows(
        tiles, (0, 1), lambda member, at, size: measured[member, :, at : at + size], leave, col_taps, leaving,
        residue, back,
    )
    rest = Rows(other * 2 * half, rows, mid)
    left = jnp.concatenate([row_adj[rest.at(0), :], row_adj[rest.at(1), :]], axis=0)
    backward_rows(
        tiles, (0, 1), rest, left, lambda one, here: back[one, :, here], field, far_slab, col_taps, waves, carry,
        far_sum, into,
    )
    far_sum[:, :LANES] = far_sum[:, tiles.width :]
    at = pl.ds(pl.multiple_of(other * 2 * (rows + 2 * half), 16), 4 * half)
    for first, size in lane_chunks(cols):
        here = slice(first, first + size)
        sums[:, here] = dot(row_near_adj[at, :], into[:, here]).astype(BF16)
    far_margin(tiles, half, Rows(other * (rows + half), half, mid), far_sum, far_sums)


def sums_kernel(half, into, far_sum, row_near_adj, near, far):
    cols = into.shape[1]
    mid = far_sum.shape[0] // 2
    rows = mid - 2 * half
    margin = 4 * half
    for at, size in lane_chunks(cols):
        here = slice(at, at + size)
        near[:, here] = dot(row_near_adj[margin : margin + 2 * rows], into[:, here])
    for j in range(cols // LANES):
        for comp in range(2):
            top = comp * mid + half
            far[comp, :, tile(j)] = far_sum[top : top + rows, pair(j)][:, LANES - half : 2 * LANES - half]


def inner_sums_kernel(half, near_sum, far_sum, inner, inner_far, near, far, near_rows, far_rows, sems):
    rows, cols = near.shape[0], near.shape[2]
    other = 1 - lax.axis_index("rows") % 2
    at = pl.ds(pl.multiple_of(other * (2 * rows - 4 * half), 16), 4 * half)
    near_rows[...] = (near_sum[at] + inner[...].astype(F32)).reshape(2 * half, 2, cols)
    near_copy = pltpu.make_async_copy(near_rows, near.at[pl.ds(other * (rows - 2 * half), 2 * half)], sems.at[0])
    near_copy.start()
    at = pl.ds(pl.multiple_of(other * (rows - half), 16), half)
    for comp in range(2):
        far_rows[pl.ds((1 - other) * half, rows - 2 * half), comp, :] = far_sum[comp, half : rows - half]
        added = far_sum[comp, at] + inner_far[comp * half : (comp + 1) * half].astype(F32)
        far_rows[pl.ds(other * (rows - 2 * half), half), comp, :] = added
    far_copy = pltpu.make_async_copy(far_rows, far.at[pl.ds(other * half, rows - half)], sems.at[1])
    far_copy.start()
    near_copy.wait()
    far_copy.wait()


def finish_kernel(half, near_in, far_in, near_sum, far_sum, outer, near, far, near_rows, far_rows, sems):
    rows, cols = near.shape[0], near.shape[2]
    parity = lax.axis_index("rows") % 2
    margin = 4 * half
    at = pl.ds(pl.multiple_of(parity * (2 * rows - margin), 16), margin)
    copies = []
    for piece in range(2):
        at = pl.ds(pl.multiple_of(parity * (2 * rows - margin) + piece * 2 * half, 16), 2 * half)
        added = near_sum[at] + outer[piece * 2 * half : (piece + 1) * 2 * half].astype(F32)
        here = pl.ds(piece * half, half)
        near_rows[here] = added.reshape(half, 2, cols)
        there = near.at[pl.ds(parity * (rows - 2 * half) + piece * half, half)]
        copies.append(pltpu.make_async_copy(near_rows.at[here], there, sems.at[piece]))
        copies[-1].start()
    at = pl.ds(pl.multiple_of(parity * (rows - half), 16), half)
    for comp in range(2):
        got = outer[margin + comp * half : margin + (comp + 1) * half].astype(F32)
        far_rows[:, comp, :] = far_sum[comp, at] + got
    far_copy = pltpu.make_async_copy(far_rows, far.at[pl.ds(parity * (rows - half), half)], sems.at[2])
    far_copy.start()
    for copy in copies:
        copy.wait()
    far_copy.wait()


def call(kernel, outs, operands, hbm=(), scalars=(), outside=(), outs_outside=(), scratch=(), aliases=None, flops=0):
    def place(i):
        if i in scalars:
            return pltpu.SMEM
        return pltpu.HBM if i in hbm else pl.ANY if i in outside else pltpu.VMEM

    return pl.pallas_call(
        kernel,
        out_shape=[jax.ShapeDtypeStruct(shape, dtype) for shape, dtype in outs],
        in_specs=[pl.BlockSpec(memory_space=place(i)) for i in range(len(operands))],
        out_specs=[
            pl.BlockSpec(memory_space=pl.ANY if i in outs_outside else pltpu.VMEM) for i in range(len(outs))
        ],
        scratch_shapes=[one if not isinstance(one, tuple) else pltpu.VMEM(*one) for one in scratch],
        input_output_aliases=aliases or {},
        compiler_params=pltpu.CompilerParams(vmem_limit_bytes=20 * 2**20),
        cost_estimate=pl.CostEstimate(flops=flops, bytes_accessed=0, transcendentals=0),
    )(*(pltpu.with_memory_space_constraint(x, pltpu.HBM) if i in hbm else x for i, x in enumerate(operands)))


def columns_local(measured, slices, kernel_taps, angle_freq, chosen):
    rows, cols = slices.shape[1], slices.shape[3]
    length = measured.shape[3]
    half = (kernel_taps.shape[1] - 1) // 2
    wide, mid, width = rows + 4 * half, rows + 2 * half, cols + LANES
    count = lax.axis_size("rows")
    outer_pairs = [(i, j) for i in range(count) if 0 <= (j := i - 1 + 2 * (i % 2)) < count]
    inner_pairs = [(i, i + 1 - 2 * (i % 2)) for i in range(count)]
    side_pairs = [(i, 1 - i) for i in range(lax.axis_size("ang"))]
    edge = 6 * half
    outer, early, across, table = call(
        functools.partial(edges_kernel, half),
        [
            ((3 * half, 2, cols), BF16), ((edge + 16, LANES), BF16), ((4 * rows - edge, LANES), BF16),
            (angle_freq.shape[::-1], F32),
        ],
        (slices, angle_freq.T), hbm=(0, 1), outs_outside=(0,),
        scratch=[((2, rows, 2, LANES), BF16), pltpu.SemaphoreType.DMA((4,))],
    )
    (early,) = call(
        frequencies_kernel, [((edge + 16, LANES), BF16)], (table, chosen, early, measured), scalars=(1,), aliases={2: 0},
    )
    outer_got = lax.ppermute(outer, "rows", outer_pairs)
    early_got = lax.ppermute(early, "ang", side_pairs)
    across_got = lax.ppermute(across, "ang", side_pairs)
    corner_got = lax.ppermute(early_got, "rows", outer_pairs)
    phased = [
        ((4 * mid, 2 * wide), BF16), ((2 * wide, 4 * mid), BF16), ((8 * half, 4 * half), BF16), ((8, width), F32),
    ]
    row_real, row_imag, row_half, row_half_adj, row_adj, col_taps, split_far, split_meas, *partial = call(
        functools.partial(matrices_kernel, rows, length),
        [
            ((mid, 2 * wide), F32), ((mid, 2 * wide), F32), ((rows, 2 * rows), BF16), ((2 * rows, rows), BF16),
            ((2 * mid, 2 * rows), BF16), ((10, 4 * LANES, 2 * LANES), BF16), ((2 * rows, 2 * rows), BF16),
            ((rows, rows), BF16), *phased,
        ],
        (kernel_taps, early),
    )
    meas_outer, meas_inner = call(
        measured_kernel, [((rows, width), BF16)] * 2, (measured, across, row_half), outside=(1, 2),
    )
    outer_meas = lax.ppermute(meas_outer, "ang", side_pairs)
    inner_meas = lax.ppermute(meas_inner, "ang", side_pairs)
    (inner,) = call(
        functools.partial(inner_edge_kernel, half), [((edge, width), BF16)], (slices, across_got, row_half), outside=(2,),
    )
    inner_got = lax.ppermute(inner, "rows", inner_pairs)
    row_near, row_near_adj, row_edge, waves = call(
        functools.partial(phases_kernel, half, length), phased, (row_real, row_imag, early_got, *partial),
        aliases={3: 0, 4: 1, 5: 2, 6: 3},
    )
    state = [
        ((2 * mid, width), F32), ((2, 2 * mid, width), BF16), ((2, 2 * mid, width), BF16),
        ((2, 2 * rows, width), BF16), ((2 * mid, width + LANES), F32), ((4 * mid, cols), BF16),
    ]
    leaving_shape = ((2, rows, width), BF16)
    far_slab, field, after, leaving = call(
        functools.partial(outer_forward_kernel, half),
        [*state[:3], leaving_shape],
        (slices, outer_got, early_got, across_got, corner_got, row_near, row_half, col_taps, split_far, waves),
        scratch=[
            ((2 * rows + 4 * half, width), BF16), ((2 * rows, width + LANES), BF16),
            ((2, 2 * rows, width + LANES), BF16), ((2, rows, width + LANES), BF16),
        ],
        flops=FORWARD_FLOPS,
    )
    back, far_sum, into, outer_sums = call(
        functools.partial(outer_backward_kernel, half),
        [*state[3:], ((edge, cols), BF16)],
        (
            far_slab, field, leaving, measured, outer_meas,
            row_half_adj, row_edge, col_taps, split_meas, waves,
        ),
        scratch=[((2, rows, width + LANES), BF16), ((2, 4 * half, width + LANES), BF16)],
        flops=BACKWARD_FLOPS,
    )
    outer_back = lax.ppermute(outer_sums, "rows", outer_pairs)
    (inner_parts,) = call(
        inner_measured_kernel, [((2, rows, width), F32)], (measured, inner_meas, split_meas, outer_sums), outside=(3,),
        flops=MEASURED_FLOPS,
    )
    far_slab, field, after, back, far_sum, into, inner_sums, inner_far = call(
        functools.partial(inner_kernel, half),
        [*state, ((4 * half, cols), BF16), ((2 * half, cols), BF16)],
        (
            slices, inner_got, across_got, inner_parts, far_slab, field, after, back, far_sum, into,
            row_near, row_half, row_adj, row_near_adj, col_taps, split_meas, waves,
        ),
        aliases={4: 0, 5: 1, 6: 2, 7: 3, 8: 4, 9: 5},
        scratch=[
            ((rows + 4 * half, width), BF16), ((4 * half, width + LANES), BF16),
            ((2, 4 * half, width + LANES), BF16), ((2, rows, width + LANES), BF16), leaving_shape,
            ((2, rows, width + LANES), BF16), ((2, 2 * rows, width + LANES), BF16),
        ],
        flops=INNER_FLOPS,
    )
    inner_back = lax.ppermute(inner_sums, "rows", inner_pairs)
    inner_far_back = lax.ppermute(inner_far, "rows", inner_pairs)
    near_sum, far_own = call(
        functools.partial(sums_kernel, half), [((2 * rows, cols), F32), ((2, rows, cols), F32)],
        (into, far_sum, row_near_adj),
    )
    near, far = call(
        functools.partial(inner_sums_kernel, half), [((rows, 2, cols), F32)] * 2,
        (near_sum, far_own, inner_back, inner_far_back), outs_outside=(0, 1),
        scratch=[((2 * half, 2, cols), F32), ((rows - half, 2, cols), F32), pltpu.SemaphoreType.DMA((2,))],
    )
    near, far = call(
        functools.partial(finish_kernel, half), [((rows, 2, cols), F32)] * 2,
        (near, far, near_sum, far_own, outer_back), outside=(0, 1), outs_outside=(0, 1), aliases={0: 0, 1: 1},
        scratch=[((2 * half, 2, cols), F32), ((half, 2, cols), F32), pltpu.SemaphoreType.DMA((3,))],
    )
    return near, far


def with_halo(block, sides, width):
    for axis, dim in sides:
        count = lax.axis_size(axis)
        forward = [(i, i + 1) for i in range(count - 1)]
        backward = [(target, source) for source, target in forward]
        low = lax.ppermute(
            lax.slice_in_dim(block, block.shape[dim] - width, None, axis=dim), axis, forward
        )
        high = lax.ppermute(lax.slice_in_dim(block, 0, width, axis=dim), axis, backward)
        block = jnp.concatenate([low, block, high], axis=dim)
    return block


def toeplitz(row_taps, out_width):
    tap_count = row_taps.shape[0]
    window = out_width + tap_count - 1
    padded = jnp.concatenate([row_taps, jnp.zeros((out_width,), row_taps.dtype)])
    tiled = jnp.tile(padded, out_width)[: out_width * window]
    return tiled.reshape(out_width, window).T


def kernel_pair(kernel_taps, out_width):
    return jnp.concatenate(
        [toeplitz(kernel_taps[0], out_width), toeplitz(kernel_taps[1], out_width)], axis=1
    )


def adjoint_taps(kernel_taps):
    return jnp.stack([kernel_taps[0][::-1], -kernel_taps[1][::-1]])


def correlate_columns(field, kernel):
    window, doubled = kernel.shape
    tile_len = doubled // 2
    half_taps = (window - tile_len) // 2
    leading, comps, length = field.shape
    blocks = length // tile_len
    padded = jnp.pad(field, ((0, 0), (0, 0), (half_taps, tile_len - half_taps)))
    main_part = padded[:, :, :length].reshape(leading, comps, blocks, tile_len)
    tail_part = padded[:, :, tile_len : tile_len + length].reshape(
        leading, comps, blocks, tile_len
    )[..., : 2 * half_taps]
    windows = jnp.concatenate([main_part, tail_part], axis=3)
    product = jnp.einsum("rpnw,wk->rpnk", windows, kernel, preferred_element_type=jnp.float32)
    real_part = product[:, 0, :, :tile_len] - product[:, 1, :, tile_len:]
    imag_part = product[:, 0, :, tile_len:] + product[:, 1, :, :tile_len]
    return (
        jnp.stack([real_part, imag_part], axis=1)
        .reshape(leading, comps, length)
        .astype(jnp.bfloat16)
    )


def band_rows(padded, band):
    out_rows = band.shape[1] // 2
    product = jnp.einsum("jpc,jk->kpc", padded, band, preferred_element_type=jnp.float32)
    real_part = product[:out_rows, 0] - product[out_rows:, 1]
    imag_part = product[out_rows:, 0] + product[:out_rows, 1]
    return jnp.stack([real_part, imag_part], axis=1).astype(jnp.bfloat16)


def complex_times(left, right):
    left = left.astype(jnp.float32)
    right = right.astype(jnp.float32)
    real_part = left[:, 0] * right[:, 0] - left[:, 1] * right[:, 1]
    imag_part = left[:, 0] * right[:, 1] + left[:, 1] * right[:, 0]
    return jnp.stack([real_part, imag_part], axis=1)


def conjugate_times(left, right):
    left = left.astype(jnp.float32)
    right = right.astype(jnp.float32)
    real_part = left[:, 0] * right[:, 0] + left[:, 1] * right[:, 1]
    imag_part = left[:, 0] * right[:, 1] - left[:, 1] * right[:, 0]
    return jnp.stack([real_part, imag_part], axis=1)


def incident(freq, row_pos, col_pos, length):
    scale = 2.0 * math.pi / length
    phase = scale * (freq[0] * row_pos[:, None] + freq[1] * col_pos[None, :])
    return jnp.stack([jnp.cos(phase), jnp.sin(phase)], axis=1)


def local(measured, slices, kernel_taps, angle_freq, chosen):
    rows_dev = measured.shape[1]
    length = measured.shape[3]
    half_taps = (kernel_taps.shape[1] - 1) // 2
    backward_taps = adjoint_taps(kernel_taps)
    forward_kernel = kernel_pair(kernel_taps, 128)
    adjoint_kernel = kernel_pair(backward_taps, 128)
    forward_band = kernel_pair(kernel_taps, rows_dev)
    adjoint_band = kernel_pair(backward_taps, rows_dev)
    gathered = lax.all_gather(slices, "ang", axis=3, tiled=True)
    near_slab = gathered[0]
    far_slab = gathered[1]
    start = lax.axis_index("rows") * rows_dev
    row_pos = (start + jnp.arange(rows_dev, dtype=jnp.int32)).astype(jnp.float32)
    col_pos = jnp.arange(length).astype(jnp.float32)
    onehot = (chosen[:, None] == jnp.arange(angle_freq.shape[0], dtype=jnp.int32)[None, :]).astype(
        jnp.float32
    )
    freqs = jnp.dot(onehot, angle_freq, precision=lax.Precision.HIGHEST)

    def along_rows(field, band):
        padded = with_halo(field, (("rows", 0),), half_taps)
        result = band_rows(padded, band)
        return result

    member = 0
    entering = incident(freqs[member], row_pos, col_pos, length)
    entry0 = complex_times(near_slab, entering).astype(jnp.bfloat16)
    inner = along_rows(correlate_columns(entry0, forward_kernel), forward_band)
    entry1 = complex_times(far_slab, inner).astype(jnp.bfloat16)
    exit_field = along_rows(correlate_columns(entry1, forward_kernel), forward_band)
    residue = (exit_field.astype(jnp.float32) - measured[member].astype(jnp.float32)).astype(
        jnp.bfloat16
    )
    back_far = correlate_columns(along_rows(residue, adjoint_band), adjoint_kernel)
    grad_far = conjugate_times(inner, back_far)
    carried_list = [conjugate_times(far_slab, back_far).astype(jnp.bfloat16)]
    member = 0
    entering = incident(freqs[member], row_pos, col_pos, length)
    back_near = correlate_columns(along_rows(carried_list[member], adjoint_band), adjoint_kernel)
    grad_near = conjugate_times(entering, back_near)
    near_total, far_total = (
        lax.psum_scatter(
            grad_near.astype(jnp.bfloat16), "ang", scatter_dimension=2, tiled=True
        ).astype(jnp.float32),
        lax.psum_scatter(
            grad_far.astype(jnp.bfloat16), "ang", scatter_dimension=2, tiled=True
        ).astype(jnp.float32),
    )
    return (near_total, far_total)


def pick(measured, slices, kernel_taps, angle_freq, chosen):
    rows, cols = slices.shape[1], slices.shape[3]
    taps = kernel_taps.shape[1]
    fits = (
        lax.axis_size("ang") == 2
        and lax.axis_size("rows") % 2 == 0
        and 2 * (taps - 1) == LANES
        and rows == 2 * (taps - 1)
        and cols % (2 * LANES) == 0
    )
    run = columns_local if fits else local
    return run(measured, slices, kernel_taps, angle_freq, chosen)


def solution(mesh):
    return jax.shard_map(
        pick,
        mesh=mesh,
        in_specs=(P("ang", "rows", None, None), P(None, "rows", None, "ang"), P(), P(), P("ang")),
        out_specs=(P("rows", None, "ang"), P("rows", None, "ang")),
        check_vma=False,
    )
```

```python
import functools
import math

import jax
import jax.numpy as jnp
from jax import lax
from jax.experimental import pallas as pl
from jax.experimental.pallas import tpu as pltpu
from jax.sharding import PartitionSpec as P

LANES = 128
BF16 = jnp.bfloat16
INNER_FLOPS = 0
FORWARD_FLOPS = 24 * 10**8
BACKWARD_FLOPS = 10**9
MEASURED_FLOPS = 4 * 10**9
F32 = jnp.float32


def dot(left, right):
    return jnp.dot(left, right, preferred_element_type=F32)


def iota(shape, dim):
    return lax.broadcasted_iota(jnp.int32, shape, dim)


def lane_chunks(width, step=2 * LANES):
    return [(at, min(step, width - at)) for at in range(0, width, step)]


def edges_kernel(half, slices, angle_freq, outer, early, across, table, strips, sems):
    rows, cols = slices.shape[1], slices.shape[3]
    parity = lax.axis_index("rows") % 2
    side = lax.axis_index("ang")
    lane = pl.multiple_of((1 - side) * (cols - LANES), LANES)
    copies = [(angle_freq, table), (slices.at[:, :, :, pl.ds(lane, LANES)], strips)]
    for slab, at, size in ((0, 0, 2 * half), (1, 2 * half, half)):
        copies.append((slices.at[slab, pl.ds(parity * (rows - size), size)], outer.at[pl.ds(at, size)]))
    copies = [pltpu.make_async_copy(frm, to, sems.at[i]) for i, (frm, to) in enumerate(copies)]
    for copy in copies:
        copy.start()
    for copy in copies[:2]:
        copy.wait()
    begin, rest = 0, 0
    for slab, size in ((0, 2 * half), (1, half)):
        there = strips[slab, pl.ds(parity * (rows - size), size)]
        early[begin : begin + 2 * size] = there.reshape(2 * size, LANES)
        there = strips[slab, pl.ds((1 - parity) * size, rows - size)]
        across[rest : rest + 2 * (rows - size)] = there.reshape(2 * (rows - size), LANES)
        begin, rest = begin + 2 * size, rest + 2 * (rows - size)
    early[begin:] = jnp.zeros((16, LANES), BF16)
    for copy in copies[2:]:
        copy.wait()


def frequencies_kernel(table, chosen, early_in, measured, early):
    row = iota((16, LANES), 0)
    block = jnp.zeros((16, LANES), F32)
    entry = jnp.where(iota(table.shape, 1) == chosen[0], table[...], 0.0)
    freqs = jnp.sum(entry, axis=1, keepdims=True)
    for part in range(2):
        rest = jnp.broadcast_to(freqs[part : part + 1], (16, LANES))
        for piece in range(3):
            rounded = rest.astype(BF16).astype(F32)
            block = jnp.where(row == 3 * part + piece, rounded, block)
            rest = rest - rounded
    early[early.shape[0] - 16 :] = block.astype(BF16)


def sent_frequencies(across):
    sent = across[across.shape[0] - 16 :].astype(F32)
    return [(sent[i : i + 1] + sent[i + 1 : i + 2] + sent[i + 2 : i + 3])[:, :1] for i in (0, 3)]


def inner_edge_kernel(half, slices, across, sent, edge):
    rows, cols = slices.shape[1], slices.shape[3]
    other = 1 - lax.axis_index("rows") % 2
    begin = 0
    for slab, size in ((0, 2 * half), (1, half)):
        there = slice(begin, begin + 2 * size)
        edge[there, :cols] = slices[slab, pl.ds(other * (rows - size), size)].reshape(2 * size, cols)
        begin += 2 * size
    edge[: 4 * half, cols:] = across[inner_rows(half, rows, other, 0)]
    edge[4 * half :, cols:] = across[inner_rows(half, rows, other, 1)]


def inner_rows(half, rows, other, slab):
    if slab == 0:
        return pl.ds(pl.multiple_of(other * (2 * rows - 8 * half), 16), 4 * half)
    return pl.ds(pl.multiple_of(2 * rows - 4 * half + other * (2 * rows - 4 * half), 16), 2 * half)


def measured_kernel(measured, sent, ready, outer, inner):
    size, cols = outer.shape[0] // 2, measured.shape[3] // 2
    parity = lax.axis_index("rows") % 2
    side = lax.axis_index("ang")
    for late, out in ((parity, outer), (1 - parity, inner)):
        rows = pl.ds(late * size, size)
        for at, first, second in ((0, cols, 0), (cols, cols - LANES, cols)):
            lanes = cols if at == 0 else LANES
            left = measured[0, rows, :, first : first + lanes].reshape(2 * size, lanes)
            right = measured[0, rows, :, second : second + lanes].reshape(2 * size, lanes)
            out[:, at : at + lanes] = jnp.where(side == 0, left, right)


def own_window(measured, late, at, size):
    half_rows, cols = measured.shape[1] // 2, measured.shape[3] // 2
    rows = pl.ds(late * half_rows, half_rows)
    first, second = (at, cols + at) if at < cols else (cols, cols - LANES)
    left = measured[0, rows, :, first : first + size].reshape(2 * half_rows, size)
    right = measured[0, rows, :, second : second + size].reshape(2 * half_rows, size)
    return jnp.where(lax.axis_index("ang") == 0, left, right)


def got_window(window, at, size):
    return window[:, at : at + size]


def skewed(base, count, stride):
    width = base.shape[1]
    return pltpu.roll(jnp.broadcast_to(base, (count, width)), 0, 1, stride=stride, stride_axis=0)


def matrices_kernel(
    rows, length, taps, across,
    row_real, row_imag, row_half, row_half_adj, row_fwd, col_taps, split_far, split_meas,
    row_near, row_edge, waves,
):
    count = taps.shape[1]
    half = (count - 1) // 2
    wide = rows + 4 * half
    mid = rows + 2 * half
    table = jnp.concatenate(
        [jnp.concatenate([taps[...], jnp.zeros((2, LANES - count), BF16)], axis=1),
         jnp.zeros((14, LANES), BF16)], axis=0,
    )

    def spread(width, place):
        tap = iota((LANES, width), 0)
        lane = iota((LANES, width), 1)
        hit = jnp.logical_and(lane == place(tap), tap < count)
        return dot(table, jnp.where(hit, 1.0, 0.0).astype(BF16))

    even = spread(2 * wide, lambda tap: 2 * tap)
    odd = spread(2 * wide, lambda tap: 2 * tap + 1)
    row_real[...] = skewed(even[0:1] - odd[1:2], mid, 2)
    row_imag[...] = skewed(even[1:2] + odd[0:1], mid, 2)

    add_phases(half, length, 0, across, row_real, row_imag, row_near, row_edge, waves)

    low = spread(2 * mid, lambda tap: tap)
    high = spread(2 * mid, lambda tap: mid + tap)
    full = jnp.concatenate(
        [skewed(low[0:1] - high[1:2], rows, 1), skewed(low[1:2] + high[0:1], rows, 1)], axis=0
    )
    row_fwd[...] = full.astype(BF16)
    low = spread(2 * rows, lambda tap: tap)
    high = spread(2 * rows, lambda tap: rows + tap)
    full = jnp.concatenate(
        [skewed(low[0:1] - high[1:2], rows // 2, 1), skewed(low[1:2] + high[0:1], rows // 2, 1)], axis=0
    )
    row_half[...] = full.astype(BF16)
    row_half_adj[...] = full.T.astype(BF16)

    window = 2 * LANES
    source = iota((window, LANES), 0)
    target = iota((window, LANES), 1)
    same_side = (source < LANES) == (target < LANES - half)
    left_only = source < window - half
    right_only = source >= LANES - half
    everything = source >= 0
    at = 0
    for adjoint in (False, True):
        for offset, masks in ((0, (everything, same_side)), (2 * half, (everything, left_only, right_only))):
            if adjoint:
                base = spread(window, lambda tap: (window - offset - (count - 1) + tap) % window)
            else:
                base = spread(window, lambda tap: (window - offset - tap) % window)
            re = skewed(base[0:1], window, 1)[:, :LANES]
            im = skewed(base[1:2], window, 1)[:, :LANES]
            im = -im if adjoint else im
            for mask in masks:
                mre = jnp.where(mask, re, 0.0).astype(BF16)
                mim = jnp.where(mask, im, 0.0).astype(BF16)
                col_taps[at, :window, :LANES] = mre
                col_taps[at, :window, LANES:] = mim
                col_taps[at, window:, :LANES] = -mim
                col_taps[at, window:, LANES:] = mre
                at += 1

    for out in (split_far, split_meas):
        size = out.shape[0]
        to, frm = iota((size, size), 0), iota((size, size), 1)
        out[...] = jnp.where(frm == 2 * (to % (size // 2)) + to // (size // 2), 1.0, 0.0).astype(BF16)


def add_phases(half, length, member, sent, row_real, row_imag, row_near, row_edge, waves):
    mid, wide = row_real.shape[0], row_real.shape[1] // 2
    rows, cols = mid - 2 * half, waves.shape[1] - LANES
    side = lax.axis_index("ang")
    freq_row, freq_col = sent_frequencies(sent)
    scale = 2.0 * math.pi / length
    lane = iota((1, cols + LANES), 1)
    col = jnp.where(side == 0, lane, jnp.where(lane < cols, lane + cols, lane - LANES)).astype(F32)
    phase = scale * (freq_col * col)
    waves[2 * member : 2 * member + 1] = jnp.cos(phase)
    waves[2 * member + 1 : 2 * member + 2] = jnp.sin(phase)
    start = lax.axis_index("rows") * rows - 2 * half
    row = (start + iota((1, 2 * wide), 1) // 2).astype(F32)
    phase = scale * (freq_row * row)
    cos, sin = jnp.cos(phase), jnp.sin(phase)
    re = row_real[...] * cos - row_imag[...] * sin
    im = row_imag[...] * cos + row_real[...] * sin
    full = jnp.concatenate([re, im], axis=0)
    at = member * 2 * mid
    row_near[at : at + 2 * mid] = full.astype(BF16)
    for part in range(2):
        low, high = 4 * half, 2 * wide - 4 * half
        near = full[part * mid : part * mid + 2 * half, :low]
        far = full[part * mid + mid - 2 * half : (part + 1) * mid, high:]
        edge = jnp.where(lax.axis_index("rows") % 2 == 0, near, far)
        row_edge[(2 * member + part) * 2 * half : (2 * member + part + 1) * 2 * half] = edge.astype(BF16)


def phases_kernel(
    half, length, row_real, row_imag, across, near_in, edge_in, waves_in,
    row_near, row_edge, waves,
):
    add_phases(half, length, 1, across, row_real, row_imag, row_near, row_edge, waves)


class Tiles:
    def __init__(self, cols):
        self.count = cols // LANES + 1
        self.width = self.count * LANES
        self.cut = self.count - 1 - lax.axis_index("ang")
        self.after = lax.rem(self.cut + 1, self.count)

    def ahead(self, j, base):
        return base + jnp.where(j == self.cut, 1, 0) if j >= self.count - 2 else base

    def back(self, j, base):
        if 0 < j < self.count - 2:
            return base
        return base + jnp.where(j == self.cut, 1, jnp.where(j == self.after, 2, 0))


def tile(j):
    return slice(j * LANES, (j + 1) * LANES)


def pair(j):
    return slice(j * LANES, (j + 2) * LANES)


class Rows:
    def __init__(self, first, count, parts):
        self.first, self.count, self.parts = first, count, parts

    def at(self, part, top=0):
        first = top + part * self.parts + self.first
        return pl.ds(first if isinstance(first, int) else pl.multiple_of(first, 16), self.count)

    def read(self, ref, lanes, top=0):
        return jnp.concatenate([ref[self.at(0, top), lanes], ref[self.at(1, top), lanes]], axis=0)

    def pairs(self, ref, j, top=0):
        return jnp.concatenate([ref[self.at(0, top), pair(j)], ref[self.at(1, top), pair(j)]], axis=1)

    def write(self, ref, lanes, both, top=0):
        ref[self.at(0, top), lanes] = both[: self.count]
        ref[self.at(1, top), lanes] = both[self.count :]


def column_step(tiles, index, col_taps, load, store, count, limit=256):
    groups, room = [], 0
    for j in range(count):
        which = index(j)
        plain = isinstance(which, int)
        if plain and groups and isinstance(groups[-1][0], int) and room > 0:
            groups[-1][1].append(j)
        else:
            groups.append((which, [j]))
            room = limit
        room -= load(j).shape[0] if plain else limit
    for which, members in groups:
        parts = [load(j) for j in members]
        size = parts[0].shape[0]
        y = dot(jnp.concatenate(parts, axis=0), col_taps[which])
        for at, j in enumerate(members):
            store(j, y[at * size : (at + 1) * size])


def forward_rows(
    tiles, part, leave, near_slab, near_first, far_slab, row_near, row_half, col_taps, waves, entry, field, after, narrow, leaving,
):
    mid, width = part.parts, tiles.width
    size = part.count
    block = near_slab.shape[0] // 2 - size
    for top in range(0, size, block):
        rows = Rows(part.first + top, block, mid)
        lefts = pl.ds(pl.multiple_of(near_first + 2 * top, LANES), 4 * block)
        left = jnp.concatenate(
            [row_near[rows.at(comp, member * 2 * mid), lefts] for member in range(2) for comp in range(2)], axis=0
        )
        for at, lanes in lane_chunks(width):
            here = slice(at, at + lanes)
            result = dot(left, near_slab[2 * top : 2 * top + 4 * block, here])
            for member in range(2):
                re = result[2 * member * block : (2 * member + 1) * block]
                im = result[(2 * member + 1) * block : (2 * member + 2) * block]
                vr, vi = waves[2 * member : 2 * member + 1, here], waves[2 * member + 1 : 2 * member + 2, here]
                entry[member, top : top + block, here] = (re * vr - im * vi).astype(BF16)
                entry[member, size + top : size + top + block, here] = (re * vi + im * vr).astype(BF16)
    entry[:, :, width:] = entry[:, :, :LANES]

    def load(j):
        return jnp.concatenate(
            [
                jnp.concatenate([entry[member, :size, pair(j)], entry[member, size:, pair(j)]], axis=1)
                for member in range(2)
            ],
            axis=0,
        )

    def store(j, y):
        far = part.read(far_slab, tile(j))
        sr, si = far[:size], far[size:]
        for member in range(2):
            re, im = y[member * size : (member + 1) * size, :LANES], y[member * size : (member + 1) * size, LANES:]
            part.write(field.at[member], tile(j), jnp.concatenate([re, im], axis=0).astype(BF16))
            both = jnp.concatenate([sr * re - si * im, sr * im + si * re], axis=0)
            part.write(after.at[member], tile(j), both.astype(BF16))

    column_step(tiles, lambda j: tiles.ahead(j, 0), col_taps, load, store, tiles.count)

    source = Rows(leave.first, 2 * leave.count, mid)
    for at, lanes in lane_chunks(width):
        here = slice(at, at + lanes)
        for member in range(2):
            y = dot(row_half[...], source.read(after.at[member], here)).astype(BF16)
            narrow[member, :, LANES + at : LANES + at + lanes] = y
    narrow[:, :, :LANES] = narrow[:, :, width:]
    size2 = leave.count

    def load2(j):
        return jnp.concatenate(
            [
                jnp.concatenate([narrow[member, :size2, pair(j)], narrow[member, size2:, pair(j)]], axis=1)
                for member in range(2)
            ],
            axis=0,
        )

    def store2(j, y):
        y = y.astype(BF16)
        for member in range(2):
            here = slice(member * size2, (member + 1) * size2)
            leaving[member, :size2, tile(j)] = y[here, :LANES]
            leaving[member, size2:, tile(j)] = y[here, LANES:]

    column_step(tiles, lambda j: tiles.back(j, 2), col_taps, load2, store2, tiles.count)


def residue_rows(tiles, members, measured, leave, col_taps, leaving, residue, back):
    size = leave.count
    for member in members:
        for at, lanes in lane_chunks(tiles.width):
            here = slice(at, at + lanes)
            leaves = leaving[member, :, here].astype(F32)
            residue[member, :, here] = (leaves - measured(member, at, lanes)).astype(BF16)
        residue[member, :, tiles.width :] = residue[member, :, :LANES]

    def load(j):
        return jnp.concatenate(
            [
                jnp.concatenate([residue[member, :size, pair(j)], residue[member, size:, pair(j)]], axis=1)
                for member in members
            ],
            axis=0,
        )

    def store(j, y):
        y = y.astype(BF16)
        for k, member in enumerate(members):
            here = slice(k * size, (k + 1) * size)
            leave.write(back.at[member], tile(j), jnp.concatenate([y[here, :LANES], y[here, LANES:]], axis=0))

    column_step(tiles, lambda j: tiles.ahead(j, 5), col_taps, load, store, tiles.count)


def backward_rows(tiles, members, part, left, right, field, far_slab, col_taps, waves, carry, far_sum, into):
    size, mid = part.count, part.parts
    for at, lanes in lane_chunks(tiles.width):
        here = slice(at, at + lanes)
        there = slice(LANES + at, LANES + at + lanes)
        far = part.read(far_slab, here)
        sr, si = far[:size], far[size:]
        total = None
        for member in members:
            y = dot(left, right(member, here))
            br, bi = y[:size], y[size:]
            inner = part.read(field.at[member], here).astype(F32)
            ir, ii = inner[:size], inner[size:]
            carry[member, :size, there] = (sr * br + si * bi).astype(BF16)
            carry[member, size:, there] = (sr * bi - si * br).astype(BF16)
            term = jnp.concatenate([ir * br + ii * bi, ir * bi - ii * br], axis=0)
            total = term if total is None else total + term
        part.write(far_sum, there, total)
    for member in members:
        carry[member, :, :LANES] = carry[member, :, tiles.width :]

    def load(j):
        return jnp.concatenate(
            [
                jnp.concatenate([carry[member, :size, pair(j)], carry[member, size:, pair(j)]], axis=1)
                for member in members
            ],
            axis=0,
        )

    def store(j, y):
        for k, member in enumerate(members):
            re, im = y[k * size : (k + 1) * size, :LANES], y[k * size : (k + 1) * size, LANES:]
            vr, vi = waves[2 * member : 2 * member + 1, tile(j)], waves[2 * member + 1 : 2 * member + 2, tile(j)]
            both = jnp.concatenate([re * vr + im * vi, im * vr - re * vi], axis=0)
            part.write(into, tile(j), both.astype(BF16), member * 2 * mid)

    column_step(tiles, lambda j: tiles.back(j, 7), col_taps, load, store, tiles.count - 1)


def split_rows(tiles, part, split, far_raw, far_slab, half):
    for at, lanes in lane_chunks(tiles.width):
        window = far_raw[:, at : at + lanes + LANES]
        part.write(far_slab, slice(at, at + lanes), dot(split[...], window[:, half : half + lanes]))


def far_margin(tiles, half, part, far_sum, sums):
    for j in range(tiles.count - 1):
        y = part.read(far_sum, pair(j))[:, LANES - half : 2 * LANES - half]
        sums[:, tile(j)] = y.astype(BF16)


def outer_forward_kernel(
    half,
    slices, outer, early, across, corner,
    row_near, row_half, col_taps, split_far, waves,
    far_slab, field, after, leaving,
    near_raw, far_raw, entry, narrow,
):
    rows, cols = slices.shape[1], slices.shape[3]
    tiles = Tiles(cols)
    width = tiles.width
    mid = rows + 2 * half
    parity = lax.axis_index("rows") % 2

    begin, rest = 0, 0
    for slab, ref, margin in ((0, near_raw, 4 * half), (1, far_raw, 2 * half)):
        own = ref.shape[0] - margin
        first = parity * (rows - own // 2)
        at = pl.ds(pl.multiple_of((1 - parity) * margin, 16), own)
        ref[at, :cols] = slices[slab, pl.ds(first, own // 2)].reshape(own, cols)
        at = pl.ds(pl.multiple_of(margin + parity * (own - 2 * margin), 16), margin)
        ref[at, cols:width] = early[begin : begin + margin]
        at = pl.ds(pl.multiple_of((1 - parity) * 2 * margin, 16), own - margin)
        frm = pl.ds(pl.multiple_of(rest + parity * (2 * rows - own), 16), own - margin)
        ref[at, cols:width] = across[frm]
        at = pl.ds(pl.multiple_of(parity * own, 16), margin)
        ref[at, :cols] = outer[begin // 2 : (begin + margin) // 2].reshape(margin, cols)
        ref[at, cols:width] = corner[begin : begin + margin]
        begin, rest = begin + margin, rest + 2 * rows - margin
    far_raw[:, width:] = far_raw[:, :LANES]

    part = Rows(parity * (rows // 2), rows, mid)
    source = Rows(parity * (rows // 2), rows // 2, mid)
    split_rows(tiles, part, split_far, far_raw, far_slab, half)
    forward_rows(
        tiles, part, source, near_raw, parity * 4 * half, far_slab, row_near, row_half, col_taps, waves, entry, field, after,
        narrow, leaving,
    )


def outer_backward_kernel(
    half,
    far_slab, field, leaving, measured, measured_got,
    row_half_adj, row_edge, col_taps, split_meas, waves,
    back, far_sum, into, sums,
    residue, carry,
):
    cols = into.shape[1]
    tiles = Tiles(cols)
    mid = far_sum.shape[0] // 2
    rows = mid - 2 * half
    parity = lax.axis_index("rows") % 2
    leave = Rows(parity * (rows // 2), rows // 2, rows)
    edge = Rows(parity * rows, 2 * half, mid)
    pick = Rows(parity * 2 * half, 2 * half, rows)
    windows = (functools.partial(own_window, measured, parity), functools.partial(got_window, measured_got))

    def parts(member, at, size):
        return dot(split_meas[...], windows[member](at, size))

    residue_rows(tiles, (0, 1), parts, leave, col_taps, leaving, residue, back)
    backward_rows(
        tiles, (0, 1), edge, pick.read(row_half_adj, slice(None)), lambda one, here: leave.read(back.at[one], here),
        field, far_slab, col_taps, waves, carry, far_sum, into,
    )
    far_sum[:, :LANES] = far_sum[:, tiles.width :]
    left = row_edge[...].T
    for at, size in lane_chunks(cols):
        here = slice(at, at + size)
        right = jnp.concatenate([edge.read(into, here, member * 2 * mid) for member in range(2)], axis=0)
        sums[: 4 * half, here] = dot(left, right).astype(BF16)
    far_margin(tiles, half, Rows(parity * (rows + half), half, mid), far_sum, sums.at[4 * half :])


def inner_measured_kernel(measured, measured_got, split_meas, row_near, row_fwd, sent, parts, row_near_adj, row_adj):
    row_near_adj[...] = row_near[...].astype(F32).T.astype(BF16)
    row_adj[...] = row_fwd[...].astype(F32).T.astype(BF16)
    other = 1 - lax.axis_index("rows") % 2
    windows = (functools.partial(own_window, measured, other), functools.partial(got_window, measured_got))
    for member in range(2):
        for at, size in lane_chunks(parts.shape[2]):
            parts[member, :, at : at + size] = dot(split_meas[...], windows[member](at, size))


def inner_kernel(
    half,
    slices, inner, across, measured, far_slab_in, field_in, after_in, back_in, far_in, into_in,
    row_near, row_half, row_adj, row_near_adj, col_taps, split_meas, waves,
    far_slab, field, after, back, far_sum, into, sums, far_sums,
    near_raw, far_raw, entry, narrow, leaving, residue, carry,
):
    cols = into.shape[1]
    tiles = Tiles(cols)
    mid = far_sum.shape[0] // 2
    rows = mid - 2 * half
    other = 1 - lax.axis_index("rows") % 2
    part = Rows(other * rows, 2 * half, mid)
    source = Rows(other * (rows // 2), rows // 2, mid)
    leave = Rows(other * (rows // 2), rows // 2, rows)

    for slab, ref, margin in ((0, near_raw, 4 * half), (1, far_raw, 2 * half)):
        own = ref.shape[0] - margin
        begin = 0 if slab == 0 else 4 * half
        first = other * (rows - own // 2)
        at = pl.ds(pl.multiple_of((1 - other) * margin, 16), own)
        ref[at, :cols] = slices[slab, pl.ds(first, own // 2)].reshape(own, cols)
        ref[at, cols : tiles.width] = across[inner_rows(half, rows, other, slab)]
        ref[pl.ds(pl.multiple_of(other * own, 16), margin), : tiles.width] = inner[begin : begin + margin]
    far_raw[:, tiles.width :] = far_raw[:, :LANES]

    split_rows(tiles, part, split_meas, far_raw, far_slab, half)
    forward_rows(
        tiles, part, source, near_raw, other * 2 * rows, far_slab, row_near, row_half, col_taps, waves, entry, field, after,
        narrow, leaving,
    )
    residue_rows(
        tiles, (0, 1), lambda member, at, size: measured[member, :, at : at + size], leave, col_taps, leaving,
        residue, back,
    )
    rest = Rows(other * 2 * half, rows, mid)
    left = jnp.concatenate([row_adj[rest.at(0), :], row_adj[rest.at(1), :]], axis=0)
    backward_rows(
        tiles, (0, 1), rest, left, lambda one, here: back[one, :, here], field, far_slab, col_taps, waves, carry,
        far_sum, into,
    )
    far_sum[:, :LANES] = far_sum[:, tiles.width :]
    at = pl.ds(pl.multiple_of(other * 2 * (rows + 2 * half), 16), 4 * half)
    for first, size in lane_chunks(cols):
        here = slice(first, first + size)
        sums[:, here] = dot(row_near_adj[at, :], into[:, here]).astype(BF16)
    far_margin(tiles, half, Rows(other * (rows + half), half, mid), far_sum, far_sums)


def sums_kernel(half, into, far_sum, row_near_adj, near, far):
    cols = into.shape[1]
    mid = far_sum.shape[0] // 2
    rows = mid - 2 * half
    margin = 4 * half
    for at, size in lane_chunks(cols):
        here = slice(at, at + size)
        near[:, here] = dot(row_near_adj[margin : margin + 2 * rows], into[:, here])
    for j in range(cols // LANES):
        for comp in range(2):
            top = comp * mid + half
            far[comp, :, tile(j)] = far_sum[top : top + rows, pair(j)][:, LANES - half : 2 * LANES - half]


def inner_sums_kernel(half, near_sum, far_sum, inner, inner_far, near, far, near_rows, far_rows, sems):
    rows, cols = near.shape[0], near.shape[2]
    other = 1 - lax.axis_index("rows") % 2
    at = pl.ds(pl.multiple_of(other * (2 * rows - 4 * half), 16), 4 * half)
    near_rows[...] = (near_sum[at] + inner[...].astype(F32)).reshape(2 * half, 2, cols)
    near_copy = pltpu.make_async_copy(near_rows, near.at[pl.ds(other * (rows - 2 * half), 2 * half)], sems.at[0])
    near_copy.start()
    at = pl.ds(pl.multiple_of(other * (rows - half), 16), half)
    for comp in range(2):
        far_rows[pl.ds((1 - other) * half, rows - 2 * half), comp, :] = far_sum[comp, half : rows - half]
        added = far_sum[comp, at] + inner_far[comp * half : (comp + 1) * half].astype(F32)
        far_rows[pl.ds(other * (rows - 2 * half), half), comp, :] = added
    far_copy = pltpu.make_async_copy(far_rows, far.at[pl.ds(other * half, rows - half)], sems.at[1])
    far_copy.start()
    near_copy.wait()
    far_copy.wait()


def finish_kernel(half, near_in, far_in, near_sum, far_sum, outer, near, far, near_rows, far_rows, sems):
    rows, cols = near.shape[0], near.shape[2]
    parity = lax.axis_index("rows") % 2
    margin = 4 * half
    at = pl.ds(pl.multiple_of(parity * (2 * rows - margin), 16), margin)
    copies = []
    for piece in range(2):
        at = pl.ds(pl.multiple_of(parity * (2 * rows - margin) + piece * 2 * half, 16), 2 * half)
        added = near_sum[at] + outer[piece * 2 * half : (piece + 1) * 2 * half].astype(F32)
        here = pl.ds(piece * half, half)
        near_rows[here] = added.reshape(half, 2, cols)
        there = near.at[pl.ds(parity * (rows - 2 * half) + piece * half, half)]
        copies.append(pltpu.make_async_copy(near_rows.at[here], there, sems.at[piece]))
        copies[-1].start()
    at = pl.ds(pl.multiple_of(parity * (rows - half), 16), half)
    for comp in range(2):
        got = outer[margin + comp * half : margin + (comp + 1) * half].astype(F32)
        far_rows[:, comp, :] = far_sum[comp, at] + got
    far_copy = pltpu.make_async_copy(far_rows, far.at[pl.ds(parity * (rows - half), half)], sems.at[2])
    far_copy.start()
    for copy in copies:
        copy.wait()
    far_copy.wait()


def call(kernel, outs, operands, hbm=(), scalars=(), outside=(), outs_outside=(), scratch=(), aliases=None, flops=0):
    def place(i):
        if i in scalars:
            return pltpu.SMEM
        return pltpu.HBM if i in hbm else pl.ANY if i in outside else pltpu.VMEM

    return pl.pallas_call(
        kernel,
        out_shape=[jax.ShapeDtypeStruct(shape, dtype) for shape, dtype in outs],
        in_specs=[pl.BlockSpec(memory_space=place(i)) for i in range(len(operands))],
        out_specs=[
            pl.BlockSpec(memory_space=pl.ANY if i in outs_outside else pltpu.VMEM) for i in range(len(outs))
        ],
        scratch_shapes=[one if not isinstance(one, tuple) else pltpu.VMEM(*one) for one in scratch],
        input_output_aliases=aliases or {},
        compiler_params=pltpu.CompilerParams(vmem_limit_bytes=20 * 2**20),
        cost_estimate=pl.CostEstimate(flops=flops, bytes_accessed=0, transcendentals=0),
    )(*(pltpu.with_memory_space_constraint(x, pltpu.HBM) if i in hbm else x for i, x in enumerate(operands)))


def columns_local(measured, slices, kernel_taps, angle_freq, chosen):
    rows, cols = slices.shape[1], slices.shape[3]
    length = measured.shape[3]
    half = (kernel_taps.shape[1] - 1) // 2
    wide, mid, width = rows + 4 * half, rows + 2 * half, cols + LANES
    count = lax.axis_size("rows")
    outer_pairs = [(i, j) for i in range(count) if 0 <= (j := i - 1 + 2 * (i % 2)) < count]
    inner_pairs = [(i, i + 1 - 2 * (i % 2)) for i in range(count)]
    side_pairs = [(i, 1 - i) for i in range(lax.axis_size("ang"))]
    edge = 6 * half
    outer, early, across, table = call(
        functools.partial(edges_kernel, half),
        [
            ((3 * half, 2, cols), BF16), ((edge + 16, LANES), BF16), ((4 * rows - edge, LANES), BF16),
            (angle_freq.shape[::-1], F32),
        ],
        (slices, angle_freq.T), hbm=(0, 1), outs_outside=(0,),
        scratch=[((2, rows, 2, LANES), BF16), pltpu.SemaphoreType.DMA((4,))],
    )
    (early,) = call(
        frequencies_kernel, [((edge + 16, LANES), BF16)], (table, chosen, early, measured), scalars=(1,), aliases={2: 0},
    )
    outer_got = lax.ppermute(outer, "rows", outer_pairs)
    early_got = lax.ppermute(early, "ang", side_pairs)
    across_got = lax.ppermute(across, "ang", side_pairs)
    corner_got = lax.ppermute(early_got, "rows", outer_pairs)
    phased = [
        ((4 * mid, 2 * wide), BF16), ((8 * half, 4 * half), BF16), ((8, width), F32),
    ]
    row_real, row_imag, row_half, row_half_adj, row_fwd, col_taps, split_far, split_meas, *partial = call(
        functools.partial(matrices_kernel, rows, length),
        [
            ((mid, 2 * wide), F32), ((mid, 2 * wide), F32), ((rows, 2 * rows), BF16), ((2 * rows, rows), BF16),
            ((2 * rows, 2 * mid), BF16), ((10, 4 * LANES, 2 * LANES), BF16), ((2 * rows, 2 * rows), BF16),
            ((rows, rows), BF16), *phased,
        ],
        (kernel_taps, early),
    )
    meas_outer, meas_inner = call(
        measured_kernel, [((rows, width), BF16)] * 2, (measured, across, row_half), outside=(1, 2),
    )
    outer_meas = lax.ppermute(meas_outer, "ang", side_pairs)
    inner_meas = lax.ppermute(meas_inner, "ang", side_pairs)
    (inner,) = call(
        functools.partial(inner_edge_kernel, half), [((edge, width), BF16)], (slices, across_got, row_half), outside=(2,),
    )
    inner_got = lax.ppermute(inner, "rows", inner_pairs)
    row_near, row_edge, waves = call(
        functools.partial(phases_kernel, half, length), phased, (row_real, row_imag, early_got, *partial),
        aliases={3: 0, 4: 1, 5: 2},
    )
    state = [
        ((2 * mid, width), F32), ((2, 2 * mid, width), BF16), ((2, 2 * mid, width), BF16),
        ((2, 2 * rows, width), BF16), ((2 * mid, width + LANES), F32), ((4 * mid, cols), BF16),
    ]
    leaving_shape = ((2, rows, width), BF16)
    far_slab, field, after, leaving = call(
        functools.partial(outer_forward_kernel, half),
        [*state[:3], leaving_shape],
        (slices, outer_got, early_got, across_got, corner_got, row_near, row_half, col_taps, split_far, waves),
        scratch=[
            ((2 * rows + 4 * half, width), BF16), ((2 * rows, width + LANES), BF16),
            ((2, 2 * rows, width + LANES), BF16), ((2, rows, width + LANES), BF16),
        ],
        flops=FORWARD_FLOPS,
    )
    back, far_sum, into, outer_sums = call(
        functools.partial(outer_backward_kernel, half),
        [*state[3:], ((edge, cols), BF16)],
        (
            far_slab, field, leaving, measured, outer_meas,
            row_half_adj, row_edge, col_taps, split_meas, waves,
        ),
        scratch=[((2, rows, width + LANES), BF16), ((2, 4 * half, width + LANES), BF16)],
        flops=BACKWARD_FLOPS,
    )
    outer_back = lax.ppermute(outer_sums, "rows", outer_pairs)
    inner_parts, row_near_adj, row_adj = call(
        inner_measured_kernel,
        [((2, rows, width), F32), ((2 * wide, 4 * mid), BF16), ((2 * mid, 2 * rows), BF16)],
        (measured, inner_meas, split_meas, row_near, row_fwd, outer_sums), outside=(5,),
        flops=MEASURED_FLOPS,
    )
    far_slab, field, after, back, far_sum, into, inner_sums, inner_far = call(
        functools.partial(inner_kernel, half),
        [*state, ((4 * half, cols), BF16), ((2 * half, cols), BF16)],
        (
            slices, inner_got, across_got, inner_parts, far_slab, field, after, back, far_sum, into,
            row_near, row_half, row_adj, row_near_adj, col_taps, split_meas, waves,
        ),
        aliases={4: 0, 5: 1, 6: 2, 7: 3, 8: 4, 9: 5},
        scratch=[
            ((rows + 4 * half, width), BF16), ((4 * half, width + LANES), BF16),
            ((2, 4 * half, width + LANES), BF16), ((2, rows, width + LANES), BF16), leaving_shape,
            ((2, rows, width + LANES), BF16), ((2, 2 * rows, width + LANES), BF16),
        ],
        flops=INNER_FLOPS,
    )
    inner_back = lax.ppermute(inner_sums, "rows", inner_pairs)
    inner_far_back = lax.ppermute(inner_far, "rows", inner_pairs)
    near_sum, far_own = call(
        functools.partial(sums_kernel, half), [((2 * rows, cols), F32), ((2, rows, cols), F32)],
        (into, far_sum, row_near_adj),
    )
    near, far = call(
        functools.partial(inner_sums_kernel, half), [((rows, 2, cols), F32)] * 2,
        (near_sum, far_own, inner_back, inner_far_back), outs_outside=(0, 1),
        scratch=[((2 * half, 2, cols), F32), ((rows - half, 2, cols), F32), pltpu.SemaphoreType.DMA((2,))],
    )
    near, far = call(
        functools.partial(finish_kernel, half), [((rows, 2, cols), F32)] * 2,
        (near, far, near_sum, far_own, outer_back), outside=(0, 1), outs_outside=(0, 1), aliases={0: 0, 1: 1},
        scratch=[((2 * half, 2, cols), F32), ((half, 2, cols), F32), pltpu.SemaphoreType.DMA((3,))],
    )
    return near, far


def with_halo(block, sides, width):
    for axis, dim in sides:
        count = lax.axis_size(axis)
        forward = [(i, i + 1) for i in range(count - 1)]
        backward = [(target, source) for source, target in forward]
        low = lax.ppermute(
            lax.slice_in_dim(block, block.shape[dim] - width, None, axis=dim), axis, forward
        )
        high = lax.ppermute(lax.slice_in_dim(block, 0, width, axis=dim), axis, backward)
        block = jnp.concatenate([low, block, high], axis=dim)
    return block


def toeplitz(row_taps, out_width):
    tap_count = row_taps.shape[0]
    window = out_width + tap_count - 1
    padded = jnp.concatenate([row_taps, jnp.zeros((out_width,), row_taps.dtype)])
    tiled = jnp.tile(padded, out_width)[: out_width * window]
    return tiled.reshape(out_width, window).T


def kernel_pair(kernel_taps, out_width):
    return jnp.concatenate(
        [toeplitz(kernel_taps[0], out_width), toeplitz(kernel_taps[1], out_width)], axis=1
    )


def adjoint_taps(kernel_taps):
    return jnp.stack([kernel_taps[0][::-1], -kernel_taps[1][::-1]])


def correlate_columns(field, kernel):
    window, doubled = kernel.shape
    tile_len = doubled // 2
    half_taps = (window - tile_len) // 2
    leading, comps, length = field.shape
    blocks = length // tile_len
    padded = jnp.pad(field, ((0, 0), (0, 0), (half_taps, tile_len - half_taps)))
    main_part = padded[:, :, :length].reshape(leading, comps, blocks, tile_len)
    tail_part = padded[:, :, tile_len : tile_len + length].reshape(
        leading, comps, blocks, tile_len
    )[..., : 2 * half_taps]
    windows = jnp.concatenate([main_part, tail_part], axis=3)
    product = jnp.einsum("rpnw,wk->rpnk", windows, kernel, preferred_element_type=jnp.float32)
    real_part = product[:, 0, :, :tile_len] - product[:, 1, :, tile_len:]
    imag_part = product[:, 0, :, tile_len:] + product[:, 1, :, :tile_len]
    return (
        jnp.stack([real_part, imag_part], axis=1)
        .reshape(leading, comps, length)
        .astype(jnp.bfloat16)
    )


def band_rows(padded, band):
    out_rows = band.shape[1] // 2
    product = jnp.einsum("jpc,jk->kpc", padded, band, preferred_element_type=jnp.float32)
    real_part = product[:out_rows, 0] - product[out_rows:, 1]
    imag_part = product[out_rows:, 0] + product[:out_rows, 1]
    return jnp.stack([real_part, imag_part], axis=1).astype(jnp.bfloat16)


def complex_times(left, right):
    left = left.astype(jnp.float32)
    right = right.astype(jnp.float32)
    real_part = left[:, 0] * right[:, 0] - left[:, 1] * right[:, 1]
    imag_part = left[:, 0] * right[:, 1] + left[:, 1] * right[:, 0]
    return jnp.stack([real_part, imag_part], axis=1)


def conjugate_times(left, right):
    left = left.astype(jnp.float32)
    right = right.astype(jnp.float32)
    real_part = left[:, 0] * right[:, 0] + left[:, 1] * right[:, 1]
    imag_part = left[:, 0] * right[:, 1] - left[:, 1] * right[:, 0]
    return jnp.stack([real_part, imag_part], axis=1)


def incident(freq, row_pos, col_pos, length):
    scale = 2.0 * math.pi / length
    phase = scale * (freq[0] * row_pos[:, None] + freq[1] * col_pos[None, :])
    return jnp.stack([jnp.cos(phase), jnp.sin(phase)], axis=1)


def local(measured, slices, kernel_taps, angle_freq, chosen):
    rows_dev = measured.shape[1]
    length = measured.shape[3]
    half_taps = (kernel_taps.shape[1] - 1) // 2
    backward_taps = adjoint_taps(kernel_taps)
    forward_kernel = kernel_pair(kernel_taps, 128)
    adjoint_kernel = kernel_pair(backward_taps, 128)
    forward_band = kernel_pair(kernel_taps, rows_dev)
    adjoint_band = kernel_pair(backward_taps, rows_dev)
    gathered = lax.all_gather(slices, "ang", axis=3, tiled=True)
    near_slab = gathered[0]
    far_slab = gathered[1]
    start = lax.axis_index("rows") * rows_dev
    row_pos = (start + jnp.arange(rows_dev, dtype=jnp.int32)).astype(jnp.float32)
    col_pos = jnp.arange(length).astype(jnp.float32)
    onehot = (chosen[:, None] == jnp.arange(angle_freq.shape[0], dtype=jnp.int32)[None, :]).astype(
        jnp.float32
    )
    freqs = jnp.dot(onehot, angle_freq, precision=lax.Precision.HIGHEST)

    def along_rows(field, band):
        padded = with_halo(field, (("rows", 0),), half_taps)
        result = band_rows(padded, band)
        return result

    member = 0
    entering = incident(freqs[member], row_pos, col_pos, length)
    entry0 = complex_times(near_slab, entering).astype(jnp.bfloat16)
    inner = along_rows(correlate_columns(entry0, forward_kernel), forward_band)
    entry1 = complex_times(far_slab, inner).astype(jnp.bfloat16)
    exit_field = along_rows(correlate_columns(entry1, forward_kernel), forward_band)
    residue = (exit_field.astype(jnp.float32) - measured[member].astype(jnp.float32)).astype(
        jnp.bfloat16
    )
    back_far = correlate_columns(along_rows(residue, adjoint_band), adjoint_kernel)
    grad_far = conjugate_times(inner, back_far)
    carried_list = [conjugate_times(far_slab, back_far).astype(jnp.bfloat16)]
    member = 0
    entering = incident(freqs[member], row_pos, col_pos, length)
    back_near = correlate_columns(along_rows(carried_list[member], adjoint_band), adjoint_kernel)
    grad_near = conjugate_times(entering, back_near)
    near_total, far_total = (
        lax.psum_scatter(
            grad_near.astype(jnp.bfloat16), "ang", scatter_dimension=2, tiled=True
        ).astype(jnp.float32),
        lax.psum_scatter(
            grad_far.astype(jnp.bfloat16), "ang", scatter_dimension=2, tiled=True
        ).astype(jnp.float32),
    )
    return (near_total, far_total)


def pick(measured, slices, kernel_taps, angle_freq, chosen):
    rows, cols = slices.shape[1], slices.shape[3]
    taps = kernel_taps.shape[1]
    fits = (
        lax.axis_size("ang") == 2
        and lax.axis_size("rows") % 2 == 0
        and 2 * (taps - 1) == LANES
        and rows == 2 * (taps - 1)
        and cols % (2 * LANES) == 0
    )
    run = columns_local if fits else local
    return run(measured, slices, kernel_taps, angle_freq, chosen)


def solution(mesh):
    return jax.shard_map(
        pick,
        mesh=mesh,
        in_specs=(P("ang", "rows", None, None), P(None, "rows", None, "ang"), P(), P(), P("ang")),
        out_specs=(P("rows", None, "ang"), P("rows", None, "ang")),
        check_vma=False,
    )
```
